256 devices in a mesh: band: 4 (over y), dx: 8 (over z), dy: 8 (over x, core).
Axes of the slice: x: 4, y: 4, z: 8, core: 2. Of those that a mesh axis runs over, the one named last changes fastest.
Arguments:
- wave_bands: float32 [4, 64, 128, 128], P('band', 'dx', 'dy'), may hold values from -6 to 6
- potential: float32 [64, 128, 128], P('dx', 'dy', 'band'), may hold values from -1.5 to 0.5
- atom_offsets: int32 [8, 8, 4, 3], P('dx', 'dy'), may hold values from 0 to 95, as said below
- proj_counts: int32 [8, 8, 4], P('dx', 'dy'), may hold values from 0 to 9, as said below
- dh_matrix: float32 [8, 8, 4, 9, 9], P('dx', 'dy'), as said below
- ds_matrix: float32 [8, 8, 4, 9, 9], P('dx', 'dy'), as said below
Outputs:
- new_bands: float32 [4, 64, 128, 128], P('band', 'dx', 'dy')
- new_residual: float32 [4, 64, 128, 128], P('band', 'dx', 'dy')
- band_energy: float32 [4], P('band')
The draws below stay inside these ranges and needn't reach their ends.
Inputs may be any that keep to these rules, and one draw needn't show every extreme that they name: `atom_offsets`: columns are x in 0..7, y in 0..15, z in 32..3*128/4-1. `proj_counts`: each count is 0 (empty slot), 1, 4 or 9. `dh_matrix`: each matrix is symmetric. `ds_matrix`: each matrix is symmetric, and each diagonal entry exceeds the sum of the magnitudes of the other entries in its row.
All inputs are finite; a program needn't handle non-finite values.
Results may differ from the reference program's by a relative error of at most 0.00017.
Values sent between devices are 32-bit elements; how exact they have to be, the bound alone decides.
A program may use at most 64 MiB of HBM per device.

```python
import jax
import jax.numpy as jnp
from jax import lax

CX = 8
CY = 16
NZ = 128
ATOM_DEV = 4
NPROJ = 9
COARSE_SWEEPS = 2
BANDS = 4
TILES_X = 8
TILES_Y = 8
NX = 64
NY = 128


def draw_atom_offsets(key, part):
    key_x, key_y, key_z = jax.random.split(key, 3)
    array_shape = (TILES_X, TILES_Y, ATOM_DEV)
    offset_x = jax.random.randint(key_x, array_shape, 0, CX)
    offset_y = jax.random.randint(key_y, array_shape, 0, CY)
    offset_z = jax.random.randint(key_z, array_shape, NZ // 4, 3 * NZ // 4)
    offset_x = offset_x.at[0, 0, 0].set(CX - 1).at[0, 0, 1].set(0)
    offset_y = offset_y.at[0, 0, 0].set(CY - 1)
    offset_z = offset_z.at[0, 0, 0].set(3 * NZ // 4 - 1)
    return jnp.stack([offset_x, offset_y, offset_z], axis=-1).astype(jnp.int32)


def draw_proj_counts(key, part):
    drawn_kind = jax.random.randint(key, (TILES_X, TILES_Y, ATOM_DEV), 0, 4)
    counts = jnp.where(drawn_kind == 0, 0, jnp.where(drawn_kind == 1, 1, jnp.where(drawn_kind == 2, 4, NPROJ)))
    return counts.at[0, 0, 0].set(NPROJ).at[0, 0, 1].set(0).astype(jnp.int32)


def draw_dh_matrix(key, part):
    key_off, key_diag = jax.random.split(jax.random.fold_in(key, 11))
    array_shape = (TILES_X, TILES_Y, ATOM_DEV, NPROJ, NPROJ)
    gaussian = jax.random.normal(key_off, array_shape, jnp.float32) * 0.4
    symmetric = 0.5 * (gaussian + jnp.swapaxes(gaussian, -1, -2))
    identity = jnp.eye(NPROJ, dtype=jnp.float32)
    diagonal = jax.random.uniform(key_diag, array_shape[:-1], jnp.float32, -2.0, 2.0)
    return symmetric * (1.0 - identity) + diagonal[..., None] * identity


def draw_ds_matrix(key, part):
    key_off, key_diag = jax.random.split(jax.random.fold_in(key, 23))
    array_shape = (TILES_X, TILES_Y, ATOM_DEV, NPROJ, NPROJ)
    uniform_off = jax.random.uniform(key_off, array_shape, jnp.float32, -0.1, 0.1)
    symmetric = 0.5 * (uniform_off + jnp.swapaxes(uniform_off, -1, -2))
    identity = jnp.eye(NPROJ, dtype=jnp.float32)
    diagonal = 1.0 + jax.random.uniform(key_diag, array_shape[:-1], jnp.float32, 0.0, 1.0)
    return symmetric * (1.0 - identity) + diagonal[..., None] * identity


def shard_levels(rng, dims, cuts, smallest, top_value):
    def one(position, shards_of):
        heights = jax.random.uniform(jax.random.fold_in(jax.random.fold_in(rng, 6), position), (shards_of,), jnp.float32, smallest / len(cuts), top_value / len(cuts))
        return jnp.repeat(jnp.exp(heights), dims[position] // shards_of).reshape((-1,) + (1,) * (len(dims) - position - 1))

    gain = one(*cuts[0])
    for cut in cuts[1:]:
        gain = gain * one(*cut)
    return gain


def noise(own_key, dims, scale, limit, shards=(), held_as=jnp.bfloat16):
    values = jax.random.normal(own_key, dims, jnp.float32) * scale
    if len(shards) > 0:
        values = shard_levels(own_key, dims, shards, -0.22, 0.18) * values
    return jnp.clip(values, min=-limit, max=limit).astype(held_as)


def setup_inputs(seed: int = 0) -> dict:
    key_list = jax.random.split(jax.random.key(seed), 7)
    wave_bands = noise(key_list[0], (BANDS, NX, NY, NZ), 1.0, 6.0, ((0, 4), (1, 8), (2, 8)), jnp.float32)
    potential = jnp.clip(-1.5 + 2.0 * jax.random.uniform(key_list[1], (NX, NY, NZ), jnp.float32) ** shard_levels(key_list[1], (NX, NY, NZ), ((0, 8), (1, 8), (2, 4)), -0.2, 0.2), -1.5, 0.5)
    atom_offsets = draw_atom_offsets(jax.random.fold_in(key_list[6], 71), 0)
    proj_counts = draw_proj_counts(jax.random.fold_in(key_list[6], 71), 0)
    dh_matrix = draw_dh_matrix(jax.random.fold_in(key_list[6], 71), 0)
    ds_matrix = draw_ds_matrix(jax.random.fold_in(key_list[6], 71), 0)
    return dict(wave_bands=wave_bands, potential=potential, atom_offsets=atom_offsets, proj_counts=proj_counts, dh_matrix=dh_matrix, ds_matrix=ds_matrix)


STENCIL = (-49.0 / 18.0, 1.5, -0.15, 1.0 / 90.0)
RELAXATION = 2.0 / 3.0
MASS_SHIFT = 0.25
AMPLITUDE = 0.15
PRECISE = lax.Precision.HIGHEST


def projector_table():
    box_steps = jnp.arange(12, dtype=jnp.float32) - 6.0
    filler = jnp.ones((12, 12, 12), jnp.float32)
    along_x = box_steps[:, None, None] * filler
    along_y = box_steps[None, :, None] * filler
    along_z = box_steps[None, None, :] * filler
    radius_sq = along_x * along_x + along_y * along_y + along_z * along_z
    radial_s = jnp.exp(-radius_sq / 8.0)
    radial_p = jnp.exp(-radius_sq / 9.68) / 2.2
    radial_d = jnp.exp(-radius_sq / 11.52) / 5.76
    angular = [radial_s, radial_p * along_x, radial_p * along_y, radial_p * along_z,
               radial_d * along_x * along_y, radial_d * along_y * along_z, radial_d * along_z * along_x,
               0.5 * radial_d * (along_x * along_x - along_y * along_y),
               radial_d * (3.0 * along_z * along_z - radius_sq) * 0.28867513]
    return AMPLITUDE * jnp.stack(angular).reshape(9, 1728)


def shift_z(field, reach):
    depth = field.shape[-1]
    zeros_rim = jnp.zeros(field.shape[:-1] + (abs(reach),), field.dtype)
    if reach > 0:
        return jnp.concatenate([zeros_rim, field[..., :depth - reach]], axis=-1)
    return jnp.concatenate([field[..., -reach:], zeros_rim], axis=-1)


def kinetic(field):
    laplacian = 3.0 * STENCIL[0] * field
    for reach in (1, 2, 3):
        weight = STENCIL[reach]
        laplacian = laplacian + weight * (jnp.roll(field, reach, 1) + jnp.roll(field, -reach, 1)
                                          + jnp.roll(field, reach, 2) + jnp.roll(field, -reach, 2)
                                          + shift_z(field, reach) + shift_z(field, -reach))
    return -0.5 * laplacian


def projector_terms(field, atom_offsets, proj_counts, dh_matrix, ds_matrix, projector_rows):
    nbands = field.shape[0]
    box_steps = jnp.arange(12, dtype=jnp.int32)
    first_tile = jnp.arange(TILES_X, dtype=jnp.int32)[:, None, None]
    second_tile = jnp.arange(TILES_Y, dtype=jnp.int32)[None, :, None]
    centre_x = (first_tile * CX + atom_offsets[..., 0]).reshape(-1)
    centre_y = (second_tile * CY + atom_offsets[..., 1]).reshape(-1)
    centre_z = atom_offsets[..., 2].reshape(-1)
    cells_x = (centre_x[:, None] - 6 + box_steps[None, :]) % NX
    cells_y = (centre_y[:, None] - 6 + box_steps[None, :]) % NY
    cells_z = centre_z[:, None] - 6 + box_steps[None, :]
    index_x = cells_x[:, :, None, None]
    index_y = cells_y[:, None, :, None]
    index_z = cells_z[:, None, None, :]
    box_values = field[:, index_x, index_y, index_z].reshape(nbands, -1, 1728)
    active = (jnp.arange(NPROJ, dtype=jnp.int32)[None, :] < proj_counts.reshape(-1)[:, None]).astype(jnp.float32)
    intersection = jnp.einsum("ik,bak->aib", projector_rows, box_values, precision=PRECISE) * active[:, :, None]
    dh_flat = dh_matrix.reshape(-1, NPROJ, NPROJ)
    ds_flat = ds_matrix.reshape(-1, NPROJ, NPROJ)
    coefficients = jnp.stack([jnp.einsum("aij,ajb->aib", dh_flat, intersection, precision=PRECISE),
                              jnp.einsum("aij,ajb->aib", ds_flat, intersection, precision=PRECISE)])
    coefficients = coefficients * active[None, :, :, None]
    spread = jnp.einsum("ik,haib->hbak", projector_rows, coefficients, precision=PRECISE)
    spread = spread.reshape(2, nbands, -1, 12, 12, 12)
    correction = jnp.zeros((2,) + field.shape, jnp.float32).at[:, :, index_x, index_y, index_z].add(spread)
    return correction[0], correction[1]


def hamiltonian(field, potential, atom_offsets, proj_counts, dh_matrix, ds_matrix, projector_rows):
    corr_h, corr_s = projector_terms(field, atom_offsets, proj_counts, dh_matrix, ds_matrix, projector_rows)
    return kinetic(field) + potential[None] * field + corr_h, field + corr_s


def level_apply(field, level):
    neighbours = (jnp.roll(field, 1, 1) + jnp.roll(field, -1, 1) + jnp.roll(field, 1, 2) + jnp.roll(field, -1, 2)
                  + shift_z(field, 1) + shift_z(field, -1))
    return -0.5 * (neighbours - 6.0 * field) / 4.0 ** level + MASS_SHIFT * field


def diagonal_of(level):
    return 3.0 / 4.0 ** level + MASS_SHIFT


def relax(field, source, level):
    return field + RELAXATION * (source - level_apply(field, level)) / diagonal_of(level)


def restrict(field):
    nbands, size_x, size_y, size_z = field.shape
    return field.reshape(nbands, size_x // 2, 2, size_y // 2, 2, size_z // 2, 2).mean(axis=(2, 4, 6))


def prolong(field):
    return jnp.repeat(jnp.repeat(jnp.repeat(field, 2, axis=1), 2, axis=2), 2, axis=3)


def precondition(source_zero):
    guess_zero = RELAXATION * source_zero / diagonal_of(0)
    source_one = restrict(source_zero - level_apply(guess_zero, 0))
    guess_one = RELAXATION * source_one / diagonal_of(1)
    source_two = restrict(source_one - level_apply(guess_one, 1))
    guess_two = RELAXATION * source_two / diagonal_of(2)
    for sweep_index in range(COARSE_SWEEPS):
        guess_two = relax(guess_two, source_two, 2)
    guess_one = relax(guess_one + prolong(guess_two), source_one, 1)
    return relax(guess_zero + prolong(guess_one), source_zero, 0)


def reference(wave_bands, potential, atom_offsets, proj_counts, dh_matrix, ds_matrix):
    projector_rows = projector_table()
    h_band, s_band = hamiltonian(wave_bands, potential, atom_offsets, proj_counts, dh_matrix, ds_matrix, projector_rows)
    band_energy = jnp.sum(wave_bands * h_band, axis=(1, 2, 3)) / jnp.sum(wave_bands * s_band, axis=(1, 2, 3))
    energy_grid = band_energy[:, None, None, None]
    residual = h_band - energy_grid * s_band
    direction = precondition(residual)
    h_dir, s_dir = hamiltonian(direction, potential, atom_offsets, proj_counts, dh_matrix, ds_matrix, projector_rows)
    change = h_dir - energy_grid * s_dir
    step_length = -jnp.sum(residual * change, axis=(1, 2, 3)) / jnp.sum(change * change, axis=(1, 2, 3))
    step_grid = step_length[:, None, None, None]
    return wave_bands + step_grid * direction, residual + step_grid * change, band_energy
```

```python
import functools

import jax
import jax.numpy as jnp
import numpy as np
from jax import lax
from jax.experimental import pallas as pl
from jax.experimental.pallas import tpu as pltpu
from jax.sharding import PartitionSpec as P

MESH = pl.DeviceIdType.MESH
HIGHEST = lax.Precision.HIGHEST
F32 = jnp.float32

STENCIL = (-49.0 / 18.0, 1.5, -0.15, 1.0 / 90.0)
RELAXATION = 2.0 / 3.0
MASS_SHIFT = 0.25
AMPLITUDE = 0.15
D_NORM = 0.28867513
CX, CY, NZ = 8, 16, 128
ATOMS = 4

DIAG = [3.0 / 4.0**level + MASS_SHIFT for level in range(3)]
GAIN = [RELAXATION / d for d in DIAG]
SIDE = [0.5 * GAIN[level] / 4.0**level for level in range(3)]


def pad8(n):
    return (n + 7) // 8 * 8


def cells(x0, x1, y0, y1):
    return [(i, j) for i in range(x0, x1) for j in range(y0, y1)]


def cross(out, inp):
    where = {c: n for n, c in enumerate(inp)}
    m = np.zeros((len(out), len(inp)))
    for row, (i, j) in enumerate(out):
        for c in ((i - 1, j), (i + 1, j), (i, j - 1), (i, j + 1)):
            if c in where:
                m[row, where[c]] = 1.0
    return m


def pick(out, inp):
    where = {c: n for n, c in enumerate(inp)}
    m = np.zeros((len(out), len(inp)))
    for row, c in enumerate(out):
        if c in where:
            m[row, where[c]] = 1.0
    return m


def average(out, inp):
    where = {c: n for n, c in enumerate(inp)}
    m = np.zeros((len(out), len(inp)))
    for row, (i, j) in enumerate(out):
        for c in cells(2 * i, 2 * i + 2, 2 * j, 2 * j + 2):
            if c in where:
                m[row, where[c]] = 0.25
    return m


def spread_to(out, inp):
    where = {c: n for n, c in enumerate(inp)}
    m = np.zeros((len(out), len(inp)))
    for row, (i, j) in enumerate(out):
        m[row, where[(i // 2, j // 2)]] = 1.0
    return m


def along_z(n):
    return np.eye(n, k=1) + np.eye(n, k=-1)


def halve_z(n):
    return np.repeat(np.eye(n // 2), 2, axis=0) * 0.5


def double_z(n):
    return np.repeat(np.eye(n), 2, axis=1)


def both(m):
    z = np.zeros_like(m)
    return np.block([[m, z], [z, m]])


def grown(m, rows, cols):
    out = np.zeros((rows, cols))
    out[: m.shape[0], : m.shape[1]] = m
    return out


FINE = cells(0, CX, 0, CY)
ONE = cells(-1, 5, -1, 9)
ONE_WIDE = cells(-2, 6, -2, 10)
TWO = cells(-1, 3, -1, 5)
TWO_WIDE = cells(-3, 5, -3, 7)

NEAR = [(a, b) for a in (-1, 0, 1) for b in (-1, 0, 1) if (a, b) != (0, 0)]
FAR = [(a, b) for a in (-2, -1, 0, 1, 2) for b in (-1, 0, 1) if (a, b) != (0, 0)]
RING = [(a, b) for a in range(-2, 3) for b in range(-2, 3) if (a, b) != (0, 0)]


def blocks(own, wide, step, targets):
    wide = set(wide)
    table, at = {}, 0
    for t in targets:
        block = [c for c in own if (c[0] - step[0] * t[0], c[1] - step[1] * t[1]) in wide]
        table[t] = (at, block)
        at += pad8(len(block))
    return table, at


BLOCKS_ONE, ROWS_ONE = blocks(ONE, ONE_WIDE, (4, 8), NEAR)
BLOCKS_TWO, ROWS_TWO = blocks(TWO, TWO_WIDE, (2, 4), FAR)
OWN_ONE = pad8(len(ONE))
OWN_TWO = pad8(len(TWO))
STACK_ONE = ROWS_ONE + OWN_ONE
STACK_TWO = ROWS_TWO + OWN_TWO


def senders(table, rows, own):
    m = np.zeros((rows + pad8(len(own)), len(own)))
    for at, block in table.values():
        m[at : at + len(block)] = pick(block, own)
    m[rows : rows + len(own)] = np.eye(len(own))
    return m


def receivers(table, rows, own, wide, step):
    m = np.zeros((len(wide), rows + pad8(len(own))))
    for t, (at, block) in table.items():
        here = [(i - step[0] * t[0], j - step[1] * t[1]) for i, j in block]
        m[:, at : at + len(block)] = pick(wide, here)
    m[:, rows : rows + len(own)] = pick(wide, own)
    return m


def constants():
    c = {}
    stack = {}
    kin_own = np.zeros((128, 128))
    kin_side = np.zeros((128, 144))
    kin_z = np.zeros((NZ, NZ))
    halo = (
        cells(-3, 0, 0, CY)
        + cells(8, 11, 0, CY)
        + [(x, y) for y in range(-3, 0) for x in range(CX)]
        + [(x, y) for y in range(16, 19) for x in range(CX)]
    )
    where_own = {cell: n for n, cell in enumerate(FINE)}
    where_halo = {cell: n for n, cell in enumerate(halo)}
    for row, (x, y) in enumerate(FINE):
        kin_own[row, row] = -1.5 * STENCIL[0]
        for reach in (1, 2, 3):
            for cell in ((x - reach, y), (x + reach, y), (x, y - reach), (x, y + reach)):
                if cell in where_own:
                    kin_own[row, where_own[cell]] += -0.5 * STENCIL[reach]
                else:
                    kin_side[row, where_halo[cell]] += -0.5 * STENCIL[reach]
    for reach in (1, 2, 3):
        kin_z += -0.5 * STENCIL[reach] * (np.eye(NZ, k=reach) + np.eye(NZ, k=-reach))
    c["kin_own"], c["kin_side"], c["kin_z"] = kin_own, kin_side, kin_z

    ring0 = cells(-2, 10, -2, 18)
    avg = average(ONE, ring0)
    one_plane = avg @ (pick(ring0, FINE) / 3.0 + SIDE[0] * cross(ring0, FINE))
    one_along = avg @ pick(ring0, FINE) * SIDE[0]
    send = senders(BLOCKS_ONE, ROWS_ONE, ONE)
    c["down_one"] = np.concatenate([send @ one_plane, send @ one_along], axis=1)
    half = halve_z(NZ)
    c["down_one_z"] = np.concatenate([both(half), both(along_z(NZ) @ half)], axis=1)

    ring1 = cells(-2, 6, -2, 10)
    avg = average(TWO, ring1)
    two_plane = avg @ (pick(ring1, ONE) / 3.0 + SIDE[1] * cross(ring1, ONE))
    two_along = avg @ pick(ring1, ONE) * SIDE[1]
    send = senders(BLOCKS_TWO, ROWS_TWO, TWO)
    c["down_two"] = np.concatenate(
        [grown(send @ two_plane, STACK_TWO, OWN_ONE), grown(send @ two_along, STACK_TWO, OWN_ONE)], axis=1
    )
    half = halve_z(64)
    c["down_two_z"] = np.concatenate(
        [grown(both(half), 128, 128), grown(both(along_z(64) @ half), 128, 128)], axis=1
    )

    take = receivers(BLOCKS_TWO, ROWS_TWO, TWO, TWO_WIDE, (2, 4))
    mid = cells(-2, 4, -2, 6)
    n1 = cross(TWO, TWO_WIDE)
    n2 = cross(TWO, mid) @ cross(mid, TWO_WIDE)
    here = pick(TWO, TWO_WIDE)
    g, k = GAIN[2], SIDE[2]
    terms = [
        g * (13.0 / 9.0 * here + 5.0 / 3.0 * k * n1 + k * k * n2),
        g * (5.0 / 3.0 * k * here + 2.0 * k * k * n1),
        g * k * k * here,
    ]
    c["sweep_two"] = np.concatenate([t @ take for t in terms], axis=1)
    nz = along_z(32)
    c["sweep_two_z"] = np.concatenate(
        [grown(both(m), 128, 128) for m in (np.eye(32), nz, nz @ nz)], axis=1
    )

    take = receivers(BLOCKS_ONE, ROWS_ONE, ONE, ONE_WIDE, (4, 8))
    g, k = GAIN[1], SIDE[1]
    here, n1 = pick(ONE, ONE_WIDE), cross(ONE, ONE_WIDE)
    up = spread_to(ONE_WIDE, TWO)
    c["up_one"] = grown(
        np.concatenate(
            [
                g * (4.0 / 3.0 * here + k * n1) @ take,
                g * k * here @ take,
                (here / 3.0 + k * n1) @ up,
                k * here @ up,
            ],
            axis=1,
        ),
        OWN_ONE,
        2 * STACK_ONE + 2 * len(TWO),
    )
    nz = along_z(64)
    c["one_z"] = both(nz)
    double = double_z(32)
    c["up_one_z"] = np.concatenate(
        [grown(both(double), 128, 128), grown(both(double @ nz), 128, 128)], axis=1
    )

    g, k = GAIN[0], SIDE[0]
    ring0 = cells(-1, 9, -1, 17)
    here, n1 = pick(FINE, ring0), cross(FINE, ring0)
    up = spread_to(ring0, ONE)
    faces = (
        cells(-1, 0, 0, CY) + cells(8, 9, 0, CY) + [(x, -1) for x in range(CX)] + [(x, 16) for x in range(CX)]
    )
    c["up_zero"] = np.concatenate(
        [
            g * (4.0 / 3.0 * np.eye(128) + k * cross(FINE, FINE)),
            grown((here / 3.0 + k * n1) @ up, 128, OWN_ONE),
            grown(k * here @ up, 128, OWN_ONE),
            g * k * cross(FINE, faces),
        ],
        axis=1,
    )
    nz = along_z(NZ)
    double = double_z(64)
    c["zero_z"] = g * k * nz
    c["up_zero_z"] = np.concatenate([grown(double, 128, 128), grown(double @ nz, 128, 128)], axis=1)
    return {name: m.astype(np.float32) for name, m in c.items()}


NAMES = (
    "kin_own",
    "kin_side",
    "kin_z",
    "down_one",
    "down_one_z",
    "down_two",
    "down_two_z",
    "sweep_two",
    "sweep_two_z",
    "up_one",
    "one_z",
    "up_one_z",
    "up_zero",
    "zero_z",
    "up_zero_z",
)


def mm(a, b):
    return lax.dot_general(a, b, (((1,), (0,)), ((), ())), precision=HIGHEST, preferred_element_type=F32)


def mm_t(a, b):
    return lax.dot_general(a, b, (((1,), (1,)), ((), ())), precision=HIGHEST, preferred_element_type=F32)


def projector_of(p, right):
    left_of = jnp.where(p < 3, p, jnp.where(p == 3, 4, jnp.where(p == 4, 7, 99)))
    right_of = jnp.where(p == 0, 3, jnp.where(p < 3, p + 4, jnp.where(p < 5, 8, 99)))
    return jnp.where(right, right_of, left_of)


def kernel(shape, *refs):
    nb, nx, ny = shape
    w_ref, pot_ref, offs_ref, cnt_ref, dh_ref, ds_ref = refs[:6]
    const = dict(zip(NAMES, refs[6 : 6 + len(NAMES)]))
    outs = refs[6 + len(NAMES) : 9 + len(NAMES)]
    bands_ref, resid_ref, energy_ref = outs
    (
        stage, halo, halo2, dirs, info, infos, infot, pots, qbuf, qrecv, qbuf2, qrecv2,
        fields, bface, bhalo, one_s, one_r, two_s, two_r, esend, ebuf, lsend, lbuf, zfun, wfun,
        ssem, rsem,
    ) = refs[9 + len(NAMES) :]
    ib, ix, iy = lax.axis_index("band"), lax.axis_index("dx"), lax.axis_index("dy")

    def device(a, b, band=0):
        return (lax.rem(ib + band + nb, nb), lax.rem(ix + a + nx, nx), lax.rem(iy + b + ny, ny))

    def send(src, dst, k, where):
        pltpu.make_async_remote_copy(
            src_ref=src, dst_ref=dst, send_sem=ssem.at[k], recv_sem=rsem.at[k], device_id=where, device_id_type=MESH
        ).start()

    def arrive(ref, k):
        pltpu.make_async_copy(ref, ref, rsem.at[k]).wait()

    def left(ref, k):
        pltpu.make_async_copy(ref, ref, ssem.at[k]).wait()

    me = ix * ny + iy
    slot = lax.rem(ix, 4) * 4 + lax.rem(iy, 4)

    infos[...] = jnp.zeros_like(infos)
    barrier = pltpu.get_barrier_semaphore()

    def greet(i, carry):
        a, b = i // ny, lax.rem(i, ny)
        pl.semaphore_signal(barrier, inc=1, device_id=device(a, b), device_id_type=MESH)
        return carry

    lax.fori_loop(1, nx * ny, greet, 0)
    for i in range(1, nb):
        pl.semaphore_signal(barrier, inc=1, device_id=device(0, 0, i), device_id_type=MESH)

    for j in range(3):
        stage[8 * j : 8 * j + 8, :] = w_ref[pl.ds(j, 8, stride=16), :]
        stage[24 + 8 * j : 32 + 8 * j, :] = w_ref[pl.ds(13 + j, 8, stride=16), :]
    row = lax.broadcasted_iota(jnp.int32, (128, 128), 0)
    lane = lax.broadcasted_iota(jnp.int32, (1, 128), 1)
    place = (lax.broadcasted_iota(jnp.int32, (32, 128), 0) + 32 * ib == lax.broadcasted_iota(jnp.int32, (32, 128), 1)).astype(F32)
    pots[ib] = mm(pot_ref[...], place)
    crossed, p_from, p_to = lane // 40, (lane // 8) % 5, lane % 8
    which = lax.broadcasted_iota(jnp.int32, (9, 128), 0)
    lane4 = lax.broadcasted_iota(jnp.int32, (ATOMS, 128), 1)
    atom4 = lax.broadcasted_iota(jnp.int32, (ATOMS, 128), 0)
    for right in (0, 1):
        j_of = projector_of(p_from, (crossed != right))
        i_of = projector_of(p_to, lane * 0 + right == 1)
        chosen = ((which == i_of) & (lane < 80)).astype(F32)
        place_of = jnp.zeros((ATOMS, 128), F32)
        for k in range(ATOMS):
            for m, v in enumerate((offs_ref[0, 0, k, 0], offs_ref[0, 0, k, 1], offs_ref[0, 0, k, 2], cnt_ref[0, 0, k])):
                place_of = jnp.where((atom4 == k) & (lane4 == 80 + m), v.astype(F32), place_of)
        for n, ref in enumerate((dh_ref, ds_ref)):
            full = jnp.zeros((ATOMS, 9, 128), F32)
            for j in range(9):
                full = full + ref[:, :, j : j + 1] * (j_of == j).astype(F32)[None]
            rows = jnp.sum(full * chosen[None], axis=1)
            info[4 * right : 4 * right + 4, 128 * n : 128 * n + 128] = rows + place_of if n == 0 else rows
    infos[slot] = info[...]

    pl.semaphore_wait(barrier, nx * ny - 1 + nb - 1)

    for a, b in NEAR:
        send(info, infos.at[slot], 0, device(a, b))
    send(w_ref.at[pl.ds(0, 48)], halo.at[pl.ds(48, 48)], 1, device(-1, 0))
    send(w_ref.at[pl.ds(80, 48)], halo.at[pl.ds(0, 48)], 1, device(1, 0))
    send(stage.at[pl.ds(0, 24)], halo.at[pl.ds(120, 24)], 1, device(0, -1))
    send(stage.at[pl.ds(24, 24)], halo.at[pl.ds(96, 24)], 1, device(0, 1))
    for i in range(1, nb):
        send(pots.at[ib], pots.at[ib], 2, device(0, 0, i))
    w = w_ref[...]
    kin = mm(const["kin_own"][...], w) + mm(w, const["kin_z"][...])

    arrive(infos.at[pl.ds(0, 8)], 0)
    for n in range(2):
        infot[n] = jnp.swapaxes(infos[:, :, 128 * n : 128 * n + 128].reshape(128, 128), 0, 1)
    slot_x, slot_y = lane // 32, (lane // 8) % 4
    right_lane = (lane // 4) % 2 == 1
    rel_x = lax.rem(slot_x - ix + 1 + 16, 4) - 1
    rel_y = lax.rem(slot_y - iy + 1 + 16, 4) - 1
    own_lane = ((rel_x == 0) & (rel_y == 0)).astype(F32)
    centre_x = infot[0, 80:81, :] + (rel_x * CX).astype(F32)
    centre_y = infot[0, 81:82, :] + (rel_y * CY).astype(F32)
    centre_z = infot[0, 82:83, :]
    count = infot[0, 83:84, :]
    row8 = lax.broadcasted_iota(jnp.int32, (8, 128), 0)
    active = (projector_of(row8, jnp.broadcast_to(right_lane, (8, 128))).astype(F32) < count).astype(F32)

    def bells(n, centre):
        r = lax.broadcasted_iota(jnp.int32, (n, 128), 0).astype(F32) - centre
        inside = ((r > -6.5) & (r < 5.5)).astype(F32)
        q = r * r
        return r, q, [inside * jnp.exp(q * (-1.0 / s)) for s in (8.0, 9.68, 11.52)]

    rz, qz, (zs, zp, zd) = bells(NZ, centre_z)
    zp, zd = zp * (1.0 / 2.2), zd * (1.0 / 5.76)
    zfun[0] = jnp.where(right_lane, rz * zp, zs)
    zfun[1] = jnp.where(right_lane, rz * zd, zp)
    zfun[2] = jnp.where(right_lane, qz * zd, zd)
    zfun[3] = zd
    rx, qx, (xs, xp, xd) = bells(CX, centre_x)
    ry, qy, (ys, yp, yd) = bells(CY, centre_y)
    pairs = (
        (jnp.where(right_lane, xp, xs), jnp.where(right_lane, yp, ys)),
        (jnp.where(right_lane, xd, rx * xp), jnp.where(right_lane, ry * yd, yp)),
        (jnp.where(right_lane, rx * xd, xp), jnp.where(right_lane, yd, ry * yp)),
        (jnp.where(right_lane, xd, rx * xd), jnp.where(right_lane, (2.0 * D_NORM) * yd, ry * yd)),
    )
    for p, (fx, fy) in enumerate(pairs):
        wfun[p] = ((AMPLITUDE * fx)[:, None, :] * fy[None, :, :]).reshape(128, 128)
    on_x = jnp.where(right_lane, -D_NORM, 0.5) * AMPLITUDE
    on_y = jnp.where(right_lane, -D_NORM, -0.5) * AMPLITUDE
    wfun[4] = (
        (on_x * qx * xd)[:, None, :] * yd[None, :, :] + xd[:, None, :] * (on_y * qy * yd)[None, :, :]
    ).reshape(128, 128)
    tile_of = (0, 1, 1, 2, 3)

    def overlaps(field):
        part = [mm(field, zfun[t]) for t in range(4)]
        rows = [jnp.sum(part[tile_of[p]] * wfun[p], axis=0, keepdims=True) for p in range(5)]
        return jnp.concatenate(rows + [jnp.zeros((3, 128), F32)], axis=0)

    keep_x = {-2: (rel_x == -1).astype(F32), 2: (rel_x == 1).astype(F32)}
    keep_y = {-2: (rel_y == -1).astype(F32), 2: (rel_y == 1).astype(F32)}

    def gather_overlaps(own, ref):
        total = None
        for a in range(-2, 3):
            line = None
            for b in range(-2, 3):
                v = own if (a, b) == (0, 0) else ref[RING.index((a, b))]
                v = v * keep_y[b] if b in keep_y else v
                line = v if line is None else line + v
            line = line * keep_x[a] if a in keep_x else line
            total = line if total is None else total + line
        return total * active

    def coefficients(q, n):
        swapped = jnp.where(right_lane, pltpu.roll(q, 4, 1), pltpu.roll(q, 124, 1))
        total = None
        for c, v in enumerate((q, swapped)):
            for p in range(5):
                at = (c * 5 + p) * 8
                term = infot[n, at : at + 8, :] * v[p : p + 1, :]
                total = term if total is None else total + term
        return total * active

    def correction(coefs):
        total = None
        for t in range(4):
            weight = None
            for p in range(5):
                if tile_of[p] == t:
                    term = wfun[p] * coefs[p : p + 1, :]
                    weight = term if weight is None else weight + term
            term = mm_t(weight, zfun[t])
            total = term if total is None else total + term
        return total

    def ring_send(src, dst, k):
        for a, b in RING:
            send(src, dst.at[RING.index((-a, -b))], k, device(a, b))

    q_own = overlaps(w)
    qbuf[...] = q_own
    ring_send(qbuf, qrecv, 3)

    arrive(halo, 1)
    kin = kin + mm(const["kin_side"][...], halo[...])
    if nb > 1:
        arrive(pots.at[pl.ds(0, nb - 1)], 2)
    potential = pots[0]
    for i in range(1, nb):
        potential = potential + pots[i]
    h_local = kin + potential * w
    num_local = jnp.sum(w * h_local, axis=0, keepdims=True)
    den_local = jnp.sum(w * w, axis=0, keepdims=True)

    arrive(qrecv, 3)
    q = gather_overlaps(q_own, qrecv)
    coef_h, coef_s = coefficients(q, 0), coefficients(q, 1)

    def total_of(v):
        return jnp.sum(v, axis=1, keepdims=True)

    num = total_of(num_local + jnp.sum(q * coef_h, axis=0, keepdims=True) * own_lane)
    den = total_of(den_local + jnp.sum(q * coef_s, axis=0, keepdims=True) * own_lane)

    def share(first, second, mine, table, k):
        mine[...] = jnp.where(lane < 64, first, second)
        table[me] = mine[...]

        def one(i, carry):
            send(mine, table.at[me], k, device(i // ny, lax.rem(i, ny)))
            return carry

        lax.fori_loop(1, nx * ny, one, 0)

    def shared(table, k):
        arrive(table.at[pl.ds(0, nx * ny - 1)], k)
        total = jnp.sum(table[...], axis=0)
        return total[:, 0:1], total[:, 64:65]

    share(num, den, esend, ebuf, 4)
    h_w = h_local + correction(coef_h)
    s_w = w + correction(coef_s)
    fields[0] = h_w
    fields[1] = s_w

    for f in range(2):
        bface[f, 0:8, :] = fields[f, pl.ds(0, 8, stride=16), :]
        bface[f, 8:16, :] = fields[f, pl.ds(15, 8, stride=16), :]
    send(fields.at[:, pl.ds(0, 16)], bhalo.at[:, pl.ds(16, 16)], 5, device(-1, 0))
    send(fields.at[:, pl.ds(112, 16)], bhalo.at[:, pl.ds(0, 16)], 5, device(1, 0))
    send(bface.at[:, pl.ds(0, 8)], bhalo.at[:, pl.ds(40, 8)], 5, device(0, -1))
    send(bface.at[:, pl.ds(8, 8)], bhalo.at[:, pl.ds(32, 8)], 5, device(0, 1))
    flat = mm(jnp.concatenate([h_w, s_w], axis=1), const["down_one_z"][...])
    one = mm(const["down_one"][...], jnp.concatenate([flat[:, :128], flat[:, 128:]], axis=0))
    one_s[...] = one[:ROWS_ONE]
    one_r[ROWS_ONE:STACK_ONE, :] = one[ROWS_ONE:]
    for t in NEAR:
        at, block = BLOCKS_ONE[t]
        n = pad8(len(block))
        send(one_s.at[pl.ds(at, n)], one_r.at[pl.ds(at, n)], 6, device(*t))
    flat = mm(one[ROWS_ONE:], const["down_two_z"][...])
    two = mm(const["down_two"][...], jnp.concatenate([flat[:, :128], flat[:, 128:]], axis=0))
    two_s[...] = two[:ROWS_TWO]
    two_r[ROWS_TWO:STACK_TWO, :] = two[ROWS_TWO:]
    for t in FAR:
        at, block = BLOCKS_TWO[t]
        n = pad8(len(block))
        send(two_s.at[pl.ds(at, n)], two_r.at[pl.ds(at, n)], 7, device(*t))

    arrive(one_s, 6)
    level1 = one_r[...]
    level1_z = mm(level1, const["one_z"][...])
    arrive(two_s, 7)
    flat = mm(two_r[...], const["sweep_two_z"][...])
    x2 = mm(
        const["sweep_two"][...],
        jnp.concatenate([flat[:, :128], flat[:, 128:256], flat[:, 256:]], axis=0),
    )
    flat = mm(x2, const["up_one_z"][...])
    x1 = mm(const["up_one"][...], jnp.concatenate([level1, level1_z, flat[:, :128], flat[:, 128:]], axis=0))
    num, den = shared(ebuf, 4)
    energy = num / den
    residual = h_w - energy * s_w
    x1 = x1 - energy * pltpu.roll(x1, 64, 1)
    flat = mm(x1, const["up_zero_z"][...])
    arrive(bhalo, 5)
    faces = bhalo[0] - energy * bhalo[1]
    direction = mm(
        const["up_zero"][...],
        jnp.concatenate([residual, flat[:, :128], flat[:, 128:], faces], axis=0),
    ) + mm(residual, const["zero_z"][...])

    dirs[...] = direction
    for j in range(3):
        stage[48 + 8 * j : 56 + 8 * j, :] = dirs[pl.ds(j, 8, stride=16), :]
        stage[72 + 8 * j : 80 + 8 * j, :] = dirs[pl.ds(13 + j, 8, stride=16), :]
    send(dirs.at[pl.ds(0, 48)], halo2.at[pl.ds(48, 48)], 8, device(-1, 0))
    send(dirs.at[pl.ds(80, 48)], halo2.at[pl.ds(0, 48)], 8, device(1, 0))
    send(stage.at[pl.ds(48, 24)], halo2.at[pl.ds(120, 24)], 8, device(0, -1))
    send(stage.at[pl.ds(72, 24)], halo2.at[pl.ds(96, 24)], 8, device(0, 1))
    q_own = overlaps(direction)
    qbuf2[...] = q_own
    ring_send(qbuf2, qrecv2, 9)
    change = mm(const["kin_own"][...], direction) + mm(direction, const["kin_z"][...])
    change = change + (potential - energy) * direction
    arrive(halo2, 8)
    change = change + mm(const["kin_side"][...], halo2[...])
    arrive(qrecv2, 9)
    q = gather_overlaps(q_own, qrecv2)
    change = change + correction(coefficients(q, 0) - energy * coefficients(q, 1))
    along = total_of(jnp.sum(residual * change, axis=0, keepdims=True))
    square = total_of(jnp.sum(change * change, axis=0, keepdims=True))
    share(along, square, lsend, lbuf, 10)

    left(infos.at[pl.ds(0, 8)], 0)
    left(halo, 1)
    if nb > 1:
        left(pots.at[pl.ds(0, nb - 1)], 2)
    left(qrecv, 3)
    left(ebuf.at[pl.ds(0, nx * ny - 1)], 4)
    left(bhalo, 5)
    left(one_s, 6)
    left(two_s, 7)
    left(halo2, 8)
    left(qrecv2, 9)
    left(lbuf.at[pl.ds(0, nx * ny - 1)], 10)

    along, square = shared(lbuf, 10)
    step = -along / square
    bands_ref[...] = w + step * direction
    resid_ref[...] = residual + step * change
    energy_ref[0] = energy[0, 0]


def solution(mesh):
    shape = tuple(mesh.shape[name] for name in ("band", "dx", "dy"))
    nb, nx, ny = shape
    held = constants()

    def on_device(wave_bands, potential, atom_offsets, proj_counts, dh_matrix, ds_matrix):
        vmem = pl.BlockSpec(memory_space=pltpu.VMEM)
        smem = pl.BlockSpec(memory_space=pltpu.SMEM)
        v = lambda *dims: pltpu.VMEM(dims, F32)
        bands, resid, energy = pl.pallas_call(
            functools.partial(kernel, shape),
            out_shape=(
                jax.ShapeDtypeStruct((128, 128), F32),
                jax.ShapeDtypeStruct((128, 128), F32),
                jax.ShapeDtypeStruct((1,), F32),
            ),
            in_specs=[vmem, vmem, smem, smem, vmem, vmem] + [vmem] * len(NAMES),
            out_specs=(vmem, vmem, smem),
            scratch_shapes=[
                v(96, 128),
                v(144, 128),
                v(144, 128),
                v(128, 128),
                v(8, 256),
                v(16, 8, 256),
                v(2, 128, 128),
                v(nb, 128, 128),
                v(8, 128),
                v(24, 8, 128),
                v(8, 128),
                v(24, 8, 128),
                v(2, 128, 128),
                v(2, 16, 128),
                v(2, 48, 128),
                v(ROWS_ONE, 128),
                v(STACK_ONE, 128),
                v(ROWS_TWO, 128),
                v(STACK_TWO, 128),
                v(1, 128),
                v(nx * ny, 1, 128),
                v(1, 128),
                v(nx * ny, 1, 128),
                v(4, 128, 128),
                v(5, 128, 128),
                pltpu.SemaphoreType.DMA((11,)),
                pltpu.SemaphoreType.DMA((11,)),
            ],
            compiler_params=pltpu.CompilerParams(
                collective_id=0, has_side_effects=True, vmem_limit_bytes=40 << 20
            ),
        )(
            wave_bands.reshape(128, 128),
            potential.reshape(128, 32),
            atom_offsets,
            proj_counts,
            dh_matrix.reshape(ATOMS, 9, 9),
            ds_matrix.reshape(ATOMS, 9, 9),
            *[held[name] for name in NAMES],
        )
        return bands.reshape(1, CX, CY, NZ), resid.reshape(1, CX, CY, NZ), energy

    return jax.shard_map(
        on_device,
        mesh=mesh,
        in_specs=(
            P("band", "dx", "dy", None),
            P("dx", "dy", "band"),
            P("dx", "dy", None, None),
            P("dx", "dy", None),
            P("dx", "dy", None, None, None),
            P("dx", "dy", None, None, None),
        ),
        out_specs=(P("band", "dx", "dy", None), P("band", "dx", "dy", None), P("band")),
        check_vma=False,
    )
```

```python
import functools

import jax
import jax.numpy as jnp
import numpy as np
from jax import lax
from jax.experimental import pallas as pl
from jax.experimental.pallas import tpu as pltpu
from jax.sharding import PartitionSpec as P

MESH = pl.DeviceIdType.MESH
F32 = jnp.float32
BF16 = jnp.bfloat16

STENCIL = (-49.0 / 18.0, 1.5, -0.15, 1.0 / 90.0)
RELAXATION = 2.0 / 3.0
MASS_SHIFT = 0.25
AMPLITUDE = 0.15
D_NORM = 0.28867513
CX, CY, NZ = 8, 16, 128
ATOMS = 4

DIAG = [3.0 / 4.0**level + MASS_SHIFT for level in range(3)]
GAIN = [RELAXATION / d for d in DIAG]
SIDE = [0.5 * GAIN[level] / 4.0**level for level in range(3)]


def pad8(n):
    return (n + 7) // 8 * 8


def cells(x0, x1, y0, y1):
    return [(i, j) for i in range(x0, x1) for j in range(y0, y1)]


def cross(out, inp):
    where = {c: n for n, c in enumerate(inp)}
    m = np.zeros((len(out), len(inp)))
    for row, (i, j) in enumerate(out):
        for c in ((i - 1, j), (i + 1, j), (i, j - 1), (i, j + 1)):
            if c in where:
                m[row, where[c]] = 1.0
    return m


def pick(out, inp):
    where = {c: n for n, c in enumerate(inp)}
    m = np.zeros((len(out), len(inp)))
    for row, c in enumerate(out):
        if c in where:
            m[row, where[c]] = 1.0
    return m


def average(out, inp):
    where = {c: n for n, c in enumerate(inp)}
    m = np.zeros((len(out), len(inp)))
    for row, (i, j) in enumerate(out):
        for c in cells(2 * i, 2 * i + 2, 2 * j, 2 * j + 2):
            if c in where:
                m[row, where[c]] = 0.25
    return m


def spread_to(out, inp):
    where = {c: n for n, c in enumerate(inp)}
    m = np.zeros((len(out), len(inp)))
    for row, (i, j) in enumerate(out):
        m[row, where[(i // 2, j // 2)]] = 1.0
    return m


def along_z(n):
    return np.eye(n, k=1) + np.eye(n, k=-1)


def halve_z(n):
    return np.repeat(np.eye(n // 2), 2, axis=0) * 0.5


def double_z(n):
    return np.repeat(np.eye(n), 2, axis=1)


def both(m):
    z = np.zeros_like(m)
    return np.block([[m, z], [z, m]])


def grown(m, rows, cols):
    out = np.zeros((rows, cols))
    out[: m.shape[0], : m.shape[1]] = m
    return out


FINE = cells(0, CX, 0, CY)
ONE = cells(-1, 5, -1, 9)
ONE_WIDE = cells(-2, 6, -2, 10)
TWO = cells(-1, 3, -1, 5)
TWO_WIDE = cells(-3, 5, -3, 7)

NEAR = [(a, b) for a in (-1, 0, 1) for b in (-1, 0, 1) if (a, b) != (0, 0)]
FAR = [(a, b) for a in (-2, -1, 0, 1, 2) for b in (-1, 0, 1) if (a, b) != (0, 0)]
GREET = [(a, b) for a in (-1, 0, 1) for b in (-2, -1, 0, 1, 2) if (a, b) != (0, 0)]


def blocks(own, wide, step, targets):
    wide = set(wide)
    table, at = {}, 0
    for t in targets:
        block = [c for c in own if (c[0] - step[0] * t[0], c[1] - step[1] * t[1]) in wide]
        table[t] = (at, block)
        at += pad8(len(block))
    return table, at


BLOCKS_ONE, ROWS_ONE = blocks(ONE, ONE_WIDE, (4, 8), NEAR)
BLOCKS_TWO, ROWS_TWO = blocks(TWO, TWO_WIDE, (2, 4), FAR)
OWN_ONE = pad8(len(ONE))
OWN_TWO = 32
STACK_ONE = ROWS_ONE + OWN_ONE
STACK_TWO = ROWS_TWO + OWN_TWO


def senders(table, rows, own):
    m = np.zeros((rows + (OWN_ONE if own is ONE else OWN_TWO), len(own)))
    for at, block in table.values():
        m[at : at + len(block)] = pick(block, own)
    m[rows : rows + len(own)] = np.eye(len(own))
    return m


def receivers(table, rows, own, wide, step):
    m = np.zeros((len(wide), rows + (OWN_ONE if own is ONE else OWN_TWO)))
    for t, (at, block) in table.items():
        here = [(i - step[0] * t[0], j - step[1] * t[1]) for i, j in block]
        m[:, at : at + len(block)] = pick(wide, here)
    m[:, rows : rows + len(own)] = pick(wide, own)
    return m


def constants():
    c = {}
    stack = {}
    kin_own = np.zeros((128, 128))
    kin_side = np.zeros((128, 144))
    kin_z = np.zeros((NZ, NZ))
    halo = (
        cells(-3, 0, 0, CY)
        + cells(8, 11, 0, CY)
        + [(x, y) for y in range(-3, 0) for x in range(CX)]
        + [(x, y) for y in range(16, 19) for x in range(CX)]
    )
    where_own = {cell: n for n, cell in enumerate(FINE)}
    where_halo = {cell: n for n, cell in enumerate(halo)}
    for row, (x, y) in enumerate(FINE):
        kin_own[row, row] = -1.5 * STENCIL[0]
        for reach in (1, 2, 3):
            for cell in ((x - reach, y), (x + reach, y), (x, y - reach), (x, y + reach)):
                if cell in where_own:
                    kin_own[row, where_own[cell]] += -0.5 * STENCIL[reach]
                else:
                    kin_side[row, where_halo[cell]] += -0.5 * STENCIL[reach]
    for reach in (1, 2, 3):
        kin_z += -0.5 * STENCIL[reach] * (np.eye(NZ, k=reach) + np.eye(NZ, k=-reach))
    c["kin_own"], c["kin_side"], c["kin_z"] = kin_own, kin_side, kin_z

    ring0 = cells(-2, 10, -2, 18)
    avg = average(ONE, ring0)
    one_plane = avg @ (pick(ring0, FINE) / 3.0 + SIDE[0] * cross(ring0, FINE))
    one_along = avg @ pick(ring0, FINE) * SIDE[0]
    send = senders(BLOCKS_ONE, ROWS_ONE, ONE)
    c["down_one"] = np.concatenate([send @ one_plane, send @ one_along], axis=1)

    ring1 = cells(-2, 6, -2, 10)
    avg = average(TWO, ring1)
    two_plane = avg @ (pick(ring1, ONE) / 3.0 + SIDE[1] * cross(ring1, ONE))
    two_along = avg @ pick(ring1, ONE) * SIDE[1]
    send = senders(BLOCKS_TWO, ROWS_TWO, TWO)
    c["down_two"] = np.concatenate(
        [send @ two @ one for two in (two_plane, two_along) for one in (one_plane, one_along)], axis=1
    )
    h0, n0, h1, n1 = halve_z(NZ), along_z(NZ), halve_z(64), along_z(64)
    c["down_z"] = np.concatenate(
        [both(m) for m in (h0, n0 @ h0, h0 @ h1, n0 @ h0 @ h1, h0 @ n1 @ h1, n0 @ h0 @ n1 @ h1)], axis=1
    )

    take = receivers(BLOCKS_TWO, ROWS_TWO, TWO, TWO_WIDE, (2, 4))
    mid = cells(-2, 4, -2, 6)
    n1 = cross(TWO, TWO_WIDE)
    n2 = cross(TWO, mid) @ cross(mid, TWO_WIDE)
    here = pick(TWO, TWO_WIDE)
    g, k = GAIN[2], SIDE[2]
    terms = [
        g * (13.0 / 9.0 * here + 5.0 / 3.0 * k * n1 + k * k * n2),
        g * (5.0 / 3.0 * k * here + 2.0 * k * k * n1),
        g * k * k * here,
    ]
    c["sweep_two"] = np.concatenate([t @ take for t in terms], axis=1)
    nz = along_z(32)
    c["sweep_two_z"] = np.concatenate(
        [grown(both(m), 128, 128) for m in (np.eye(32), nz, nz @ nz)], axis=1
    )

    take = receivers(BLOCKS_ONE, ROWS_ONE, ONE, ONE_WIDE, (4, 8))
    g, k = GAIN[1], SIDE[1]
    here, n1 = pick(ONE, ONE_WIDE), cross(ONE, ONE_WIDE)
    up = spread_to(ONE_WIDE, TWO)
    c["up_one"] = grown(
        np.concatenate(
            [
                g * (4.0 / 3.0 * here + k * n1) @ take,
                g * k * here @ take,
                grown((here / 3.0 + k * n1) @ up, len(ONE), OWN_TWO),
                grown(k * here @ up, len(ONE), OWN_TWO),
            ],
            axis=1,
        ),
        OWN_ONE,
        2 * STACK_ONE + 2 * OWN_TWO,
    )
    nz = along_z(64)
    c["one_z"] = both(nz)
    double = double_z(32)
    c["up_one_z"] = np.concatenate(
        [grown(both(double), 128, 128), grown(both(double @ nz), 128, 128)], axis=1
    )

    g, k = GAIN[0], SIDE[0]
    ring0 = cells(-1, 9, -1, 17)
    here, n1 = pick(FINE, ring0), cross(FINE, ring0)
    up = spread_to(ring0, ONE)
    faces = (
        cells(-1, 0, 0, CY) + cells(8, 9, 0, CY) + [(x, -1) for x in range(CX)] + [(x, 16) for x in range(CX)]
    )
    c["up_zero"] = np.concatenate(
        [
            g * (4.0 / 3.0 * np.eye(128) + k * cross(FINE, FINE)),
            grown((here / 3.0 + k * n1) @ up, 128, OWN_ONE),
            grown(k * here @ up, 128, OWN_ONE),
            g * k * cross(FINE, faces),
        ],
        axis=1,
    )
    nz = along_z(NZ)
    double = double_z(64)
    c["zero_z"] = nz
    c["up_zero_z"] = np.concatenate([grown(double, 128, 128), grown(double @ nz, 128, 128)], axis=1)
    return c


def packed():
    table, parts, at = {}, [], 0
    for name, m in constants().items():
        rows, cols = m.shape
        rows = (rows + 15) // 16 * 16
        m = grown(m, rows, (cols + 127) // 128 * 128).astype(np.float32)
        high = m.astype(jnp.bfloat16)
        low = (m - high.astype(np.float32)).astype(jnp.bfloat16)
        exact = not low.astype(np.float32).any()
        places = []
        for part in (high,) if exact else (high, low):
            tiles = [part[:, t : t + 128] for t in range(0, m.shape[1], 128)]
            places.append([at + n * rows for n in range(len(tiles))])
            at += rows * len(tiles)
            parts += tiles
        table[name] = (rows, cols, places)
    return table, np.concatenate(parts, axis=0)


def dot(a, b):
    return lax.dot_general(a, b, (((1,), (0,)), ((), ())), preferred_element_type=F32)


def split(x):
    high = x.astype(BF16)
    return high, (x - high.astype(F32)).astype(BF16)


def dot3(a, b):
    return dot(a[0], b[0]) + dot(a[1], b[0]) + dot(a[0], b[1])


def projector_of(p, right):
    left_of = jnp.where(p < 3, p, jnp.where(p == 3, 4, jnp.where(p == 4, 7, 99)))
    right_of = jnp.where(p == 0, 3, jnp.where(p < 3, p + 4, jnp.where(p < 5, 8, 99)))
    return jnp.where(right, right_of, left_of)


def kernel(shape, table, *refs):
    nb, nx, ny = shape
    (
        w_in, pot_in, offs_in, cnt_in, dh_in, ds_in, const_in,
        bands_ref, resid_ref, energy_ref,
        w_ref, pot_ref, offs_ref, cnt_ref, d_ref, const,
        stage, halo, halo2, dirs, info, infos, infot, pots, qbuf, qrecv, qbuf2, qrecv2,
        fields, bface, bhalo, one_s, one_r, two_s, two_r, esend, ebuf, lsend, lbuf, zfun, zturn, wfun,
        lsem, ssem, rsem,
    ) = refs
    loads = [
        pltpu.make_async_copy(src, dst, lsem.at[n])
        for n, (src, dst) in enumerate(
            (
                (offs_in, offs_ref), (cnt_in, cnt_ref), (dh_in, d_ref.at[0]), (ds_in, d_ref.at[1]),
                (w_in, w_ref), (pot_in, pot_ref), (const_in, const),
            )
        )
    ]
    for load in loads:
        load.start()

    def held(name):
        rows, cols, places = table[name]
        return [jnp.concatenate([const[at : at + rows, :] for at in tiles], axis=1)[:, :cols] for tiles in places]

    def from_left(name, x):
        c, (high, low) = held(name), split(x)
        total = dot(c[0], high) + dot(c[0], low)
        return total + dot(c[1], high) if len(c) > 1 else total

    def from_right(x, name):
        c, (high, low) = held(name), split(x)
        total = dot(high, c[0]) + dot(low, c[0])
        return total + dot(high, c[1]) if len(c) > 1 else total

    ib, ix, iy = lax.axis_index("band"), lax.axis_index("dx"), lax.axis_index("dy")

    def device(a, b, band=0):
        return (lax.rem(ib + band + nb, nb), lax.rem(ix + a + nx, nx), lax.rem(iy + b + ny, ny))

    def send(src, dst, k, where):
        pltpu.make_async_remote_copy(
            src_ref=src, dst_ref=dst, send_sem=ssem.at[k], recv_sem=rsem.at[k], device_id=where, device_id_type=MESH
        ).start()

    def arrive(ref, k):
        pltpu.make_async_copy(ref, ref, rsem.at[k]).wait()

    def left(ref, k):
        pltpu.make_async_copy(ref, ref, ssem.at[k]).wait()

    me = ix * ny + iy
    slot = lax.rem(ix, 4) * 4 + lax.rem(iy, 4)

    infos[...] = jnp.zeros_like(infos)
    barrier = pltpu.get_barrier_semaphore()

    for a, b in GREET:
        pl.semaphore_signal(barrier, inc=1, device_id=device(a, b), device_id_type=MESH)
    for i in range(1, nb):
        pl.semaphore_signal(barrier, inc=1, device_id=device(0, 0, i), device_id_type=MESH)

    for load in loads[:6]:
        load.wait()
    for j in range(3):
        stage[8 * j : 8 * j + 8, :] = w_ref[pl.ds(j, 8, stride=16), :]
        stage[24 + 8 * j : 32 + 8 * j, :] = w_ref[pl.ds(13 + j, 8, stride=16), :]
    row = lax.broadcasted_iota(jnp.int32, (128, 128), 0)
    lane = lax.broadcasted_iota(jnp.int32, (1, 128), 1)
    place = (lax.broadcasted_iota(jnp.int32, (32, 128), 0) + 32 * ib == lax.broadcasted_iota(jnp.int32, (32, 128), 1)).astype(F32)
    place = place.astype(BF16)
    high, low = split(pot_ref[...])
    rest = pot_ref[...] - high.astype(F32) - low.astype(F32)
    pots[ib] = dot(high, place) + dot(low, place) + dot(rest.astype(BF16), place)
    crossed, p_from, p_to = lane // 40, (lane // 8) % 5, lane % 8
    lane4 = lax.broadcasted_iota(jnp.int32, (ATOMS, 128), 1)
    atom4 = lax.broadcasted_iota(jnp.int32, (ATOMS, 128), 0)
    for right in (0, 1):
        j_of = projector_of(p_from, (crossed != right))
        i_of = projector_of(p_to, lane * 0 + right == 1)
        chosen = [((i_of == i) & (lane < 80)).astype(F32) for i in range(9)]
        from_j = [(j_of == j).astype(F32) for j in range(9)]
        place_of = jnp.zeros((ATOMS, 128), F32)
        for k in range(ATOMS):
            for m, v in enumerate((offs_ref[0, 0, 0, k], offs_ref[0, 1, 0, k], offs_ref[0, 2, 0, k], cnt_ref[0, 0, k])):
                place_of = jnp.where((atom4 == k) & (lane4 == 80 + m), v.astype(F32), place_of)
        for n in range(2):
            rows = place_of if n == 0 else jnp.zeros((ATOMS, 128), F32)
            for i in range(9):
                of_i = d_ref[n, i]
                full = of_i[:, 0:1] * from_j[0]
                for j in range(1, 9):
                    full = full + of_i[:, j : j + 1] * from_j[j]
                rows = rows + full * chosen[i]
            info[4 * right : 4 * right + 4, 128 * n : 128 * n + 128] = rows
    infos[slot] = info[...]

    pl.semaphore_wait(barrier, len(GREET) + nb - 1)

    for a, b in NEAR:
        send(info, infos.at[slot], 0, device(a, b))
    send(w_ref.at[pl.ds(0, 48)], halo.at[pl.ds(48, 48)], 1, device(-1, 0))
    send(w_ref.at[pl.ds(80, 48)], halo.at[pl.ds(0, 48)], 1, device(1, 0))
    send(stage.at[pl.ds(0, 24)], halo.at[pl.ds(120, 24)], 1, device(0, -1))
    send(stage.at[pl.ds(24, 24)], halo.at[pl.ds(96, 24)], 1, device(0, 1))
    for i in range(1, nb):
        send(pots.at[ib], pots.at[ib], 2, device(0, 0, i))
    w = w_ref[...]
    loads[6].wait()
    kin = from_left("kin_own", w) + from_right(w, "kin_z")

    arrive(infos.at[pl.ds(0, 8)], 0)
    for n in range(2):
        infot[n] = jnp.swapaxes(infos[:, :, 128 * n : 128 * n + 128].reshape(128, 128), 0, 1)
    slot_x, slot_y = lane // 32, (lane // 8) % 4
    right_lane = (lane // 4) % 2 == 1
    rel_x = lax.rem(slot_x - ix + 1 + 16, 4) - 1
    rel_y = lax.rem(slot_y - iy + 1 + 16, 4) - 1
    own_lane = ((rel_x == 0) & (rel_y == 0)).astype(F32)
    centre_x = infot[0, 80:81, :] + (rel_x * CX).astype(F32)
    centre_y = infot[0, 81:82, :] + (rel_y * CY).astype(F32)
    centre_z = infot[0, 82:83, :]
    count = infot[0, 83:84, :]
    row8 = lax.broadcasted_iota(jnp.int32, (8, 128), 0)
    active = (projector_of(row8, jnp.broadcast_to(right_lane, (8, 128))).astype(F32) < count).astype(F32)

    def bells(n, centre):
        r = lax.broadcasted_iota(jnp.int32, (n, 128), 0).astype(F32) - centre
        inside = ((r > -6.5) & (r < 5.5)).astype(F32)
        q = r * r
        return r, q, [inside * jnp.exp(q * (-1.0 / s)) for s in (8.0, 9.68, 11.52)]

    rz, qz, (zs, zp, zd) = bells(NZ, centre_z)
    zp, zd = zp * (1.0 / 2.2), zd * (1.0 / 5.76)
    zs = (
        jnp.where(right_lane, rz * zp, zs), jnp.where(right_lane, rz * zd, zp), jnp.where(right_lane, qz * zd, zd), zd,
    )
    for n, v in enumerate(split(jnp.concatenate(zs, axis=1))):
        zfun[n] = v
    rx, qx, (xs, xp, xd) = bells(CX, centre_x)
    ry, qy, (ys, yp, yd) = bells(CY, centre_y)
    pairs = (
        (jnp.where(right_lane, xp, xs), jnp.where(right_lane, yp, ys)),
        (jnp.where(right_lane, xd, rx * xp), jnp.where(right_lane, ry * yd, yp)),
        (jnp.where(right_lane, rx * xd, xp), jnp.where(right_lane, yd, ry * yp)),
        (jnp.where(right_lane, xd, rx * xd), jnp.where(right_lane, (2.0 * D_NORM) * yd, ry * yd)),
    )
    for p, (fx, fy) in enumerate(pairs):
        wfun[p] = ((AMPLITUDE * fx)[:, None, :] * fy[None, :, :]).reshape(128, 128)
    on_x = jnp.where(right_lane, -D_NORM, 0.5) * AMPLITUDE
    on_y = jnp.where(right_lane, -D_NORM, -0.5) * AMPLITUDE
    wfun[4] = (
        (on_x * qx * xd)[:, None, :] * yd[None, :, :] + xd[:, None, :] * (on_y * qy * yd)[None, :, :]
    ).reshape(128, 128)
    tile_of = (0, 1, 1, 2, 3)

    def overlaps(field):
        part = dot3(split(field), (zfun[0], zfun[1]))
        rows = [
            jnp.sum(part[:, 128 * tile_of[p] : 128 * tile_of[p] + 128] * wfun[p], axis=0, keepdims=True) for p in range(5)
        ]
        return jnp.concatenate(rows + [jnp.zeros((3, 128), F32)], axis=0)

    keep_x = {-2: (rel_x == -1).astype(F32), 2: (rel_x == 1).astype(F32)}

    def gather_overlaps(own, ref):
        total = None
        for a in range(-2, 3):
            line = None
            for b in (-1, 0, 1):
                v = own if (a, b) == (0, 0) else ref[FAR.index((a, b))]
                line = v if line is None else line + v
            line = line * keep_x[a] if a in keep_x else line
            total = line if total is None else total + line
        return total * active

    def coefficients(q, n):
        swapped = jnp.where(right_lane, pltpu.roll(q, 4, 1), pltpu.roll(q, 124, 1))
        total = None
        for c, v in enumerate((q, swapped)):
            for p in range(5):
                at = (c * 5 + p) * 8
                term = infot[n, at : at + 8, :] * v[p : p + 1, :]
                total = term if total is None else total + term
        return total * active

    def weights(coefs):
        tiles = [None] * 4
        for p in range(5):
            term = wfun[p] * coefs[p : p + 1, :]
            t = tile_of[p]
            tiles[t] = term if tiles[t] is None else tiles[t] + term
        return jnp.concatenate(tiles, axis=1)

    def correction(weight):
        return dot3(split(weight), (zturn[0], zturn[1]))

    def ring_send(src, dst, k):
        for a, b in FAR:
            send(src, dst.at[FAR.index((-a, -b))], k, device(a, b))

    q_own = overlaps(w)
    qbuf[...] = q_own
    ring_send(qbuf, qrecv, 3)
    for n, v in enumerate(split(jnp.concatenate([jnp.swapaxes(z, 0, 1) for z in zs], axis=0))):
        zturn[n] = v

    arrive(halo, 1)
    kin = kin + from_left("kin_side", halo[...])
    if nb > 1:
        arrive(pots.at[pl.ds(0, nb - 1)], 2)
    potential = pots[0]
    for i in range(1, nb):
        potential = potential + pots[i]
    h_local = kin + potential * w
    num_local = jnp.sum(w * h_local, axis=0, keepdims=True)
    den_local = jnp.sum(w * w, axis=0, keepdims=True)

    arrive(qrecv, 3)
    q = gather_overlaps(q_own, qrecv)
    coef_h, coef_s = coefficients(q, 0), coefficients(q, 1)

    def total_of(v):
        return jnp.sum(v, axis=1, keepdims=True)

    num = total_of(num_local + jnp.sum(q * coef_h, axis=0, keepdims=True) * own_lane)
    den = total_of(den_local + jnp.sum(q * coef_s, axis=0, keepdims=True) * own_lane)

    def share(first, second, mine, table, k):
        mine[...] = jnp.where(lane < 64, first, second)
        table[me] = mine[...]

        def one(i, carry):
            send(mine, table.at[me], k, device(i // ny, lax.rem(i, ny)))
            return carry

        lax.fori_loop(1, nx * ny, one, 0)

    def shared(table, k):
        arrive(table.at[pl.ds(0, nx * ny - 1)], k)
        total = jnp.sum(table[...], axis=0)
        return total[:, 0:1], total[:, 64:65]

    both_terms = correction(jnp.concatenate([weights(coef_h), weights(coef_s)], axis=0))
    h_w = h_local + both_terms[:128]
    s_w = w + both_terms[128:]
    fields[0] = h_w
    fields[1] = s_w

    for f in range(2):
        bface[f, 0:8, :] = fields[f, pl.ds(0, 8, stride=16), :]
        bface[f, 8:16, :] = fields[f, pl.ds(15, 8, stride=16), :]
    send(fields.at[:, pl.ds(0, 16)], bhalo.at[:, pl.ds(16, 16)], 5, device(-1, 0))
    send(fields.at[:, pl.ds(112, 16)], bhalo.at[:, pl.ds(0, 16)], 5, device(1, 0))
    send(bface.at[:, pl.ds(0, 8)], bhalo.at[:, pl.ds(40, 8)], 5, device(0, -1))
    send(bface.at[:, pl.ds(8, 8)], bhalo.at[:, pl.ds(32, 8)], 5, device(0, 1))
    flat = from_right(jnp.concatenate([h_w, s_w], axis=1), "down_z")
    one = from_left("down_one", jnp.concatenate([flat[:, :128], flat[:, 128:256]], axis=0))
    one_s[...] = one[:ROWS_ONE]
    one_r[ROWS_ONE:STACK_ONE, :] = one[ROWS_ONE:]
    for t in NEAR:
        at, block = BLOCKS_ONE[t]
        n = pad8(len(block))
        send(one_s.at[pl.ds(at, n)], one_r.at[pl.ds(at, n)], 6, device(*t))
    lower, upper = flat[:, 256:384], flat[:, 384:]
    two = from_left(
        "down_two",
        jnp.concatenate([lower, pltpu.roll(lower, 64, 1), upper, pltpu.roll(upper, 64, 1)], axis=0),
    )
    two_s[...] = two[:ROWS_TWO]
    two_r[ROWS_TWO:STACK_TWO, :] = two[ROWS_TWO:]
    for t in FAR:
        at, block = BLOCKS_TWO[t]
        n = pad8(len(block))
        send(two_s.at[pl.ds(at, n)], two_r.at[pl.ds(at, n)], 7, device(*t))

    share(num, den, esend, ebuf, 4)

    arrive(one_s, 6)
    level1 = one_r[...]
    level1_z = from_right(level1, "one_z")
    arrive(two_s, 7)
    flat = from_right(two_r[...], "sweep_two_z")
    x2 = from_left("sweep_two", jnp.concatenate([flat[:, :128], flat[:, 128:256], flat[:, 256:]], axis=0))
    flat = from_right(x2, "up_one_z")
    x1 = from_left("up_one", jnp.concatenate([level1, level1_z, flat[:, :128], flat[:, 128:]], axis=0))
    num, den = shared(ebuf, 4)
    energy = num / den
    residual = h_w - energy * s_w
    x1 = x1 - energy * pltpu.roll(x1, 64, 1)
    flat = from_right(x1, "up_zero_z")
    arrive(bhalo, 5)
    faces = bhalo[0] - energy * bhalo[1]
    direction = from_left(
        "up_zero", jnp.concatenate([residual, flat[:, :128], flat[:, 128:], faces], axis=0)
    ) + (GAIN[0] * SIDE[0]) * from_right(residual, "zero_z")

    dirs[...] = direction
    for j in range(3):
        stage[48 + 8 * j : 56 + 8 * j, :] = dirs[pl.ds(j, 8, stride=16), :]
        stage[72 + 8 * j : 80 + 8 * j, :] = dirs[pl.ds(13 + j, 8, stride=16), :]
    send(dirs.at[pl.ds(0, 48)], halo2.at[pl.ds(48, 48)], 8, device(-1, 0))
    send(dirs.at[pl.ds(80, 48)], halo2.at[pl.ds(0, 48)], 8, device(1, 0))
    send(stage.at[pl.ds(48, 24)], halo2.at[pl.ds(120, 24)], 8, device(0, -1))
    send(stage.at[pl.ds(72, 24)], halo2.at[pl.ds(96, 24)], 8, device(0, 1))
    q_own = overlaps(direction)
    qbuf2[...] = q_own
    ring_send(qbuf2, qrecv2, 9)
    change = from_left("kin_own", direction) + from_right(direction, "kin_z")
    change = change + (potential - energy) * direction
    arrive(halo2, 8)
    change = change + from_left("kin_side", halo2[...])
    arrive(qrecv2, 9)
    q = gather_overlaps(q_own, qrecv2)
    change = change + correction(weights(coefficients(q, 0) - energy * coefficients(q, 1)))
    along = total_of(jnp.sum(residual * change, axis=0, keepdims=True))
    square = total_of(jnp.sum(change * change, axis=0, keepdims=True))
    share(along, square, lsend, lbuf, 10)

    left(infos.at[pl.ds(0, 8)], 0)
    left(halo, 1)
    if nb > 1:
        left(pots.at[pl.ds(0, nb - 1)], 2)
    left(qrecv, 3)
    left(ebuf.at[pl.ds(0, nx * ny - 1)], 4)
    left(bhalo, 5)
    left(one_s, 6)
    left(two_s, 7)
    left(halo2, 8)
    left(qrecv2, 9)
    left(lbuf.at[pl.ds(0, nx * ny - 1)], 10)

    along, square = shared(lbuf, 10)
    step = -along / square
    bands_ref[...] = w + step * direction
    resid_ref[...] = residual + step * change
    energy_ref[0] = energy[0, 0]


def solution(mesh):
    shape = tuple(mesh.shape[name] for name in ("band", "dx", "dy"))
    nb, nx, ny = shape
    table, packed_constants = packed()

    def on_device(wave_bands, potential, atom_offsets, proj_counts, dh_matrix, ds_matrix):
        vmem = pl.BlockSpec(memory_space=pltpu.VMEM)
        smem = pl.BlockSpec(memory_space=pltpu.SMEM)
        v = lambda *dims: pltpu.VMEM(dims, F32)
        bands, resid, energy = pl.pallas_call(
            functools.partial(kernel, shape, table),
            out_shape=(
                jax.ShapeDtypeStruct((128, 128), F32),
                jax.ShapeDtypeStruct((128, 128), F32),
                jax.ShapeDtypeStruct((1,), F32),
            ),
            in_specs=[pl.BlockSpec(memory_space=pltpu.HBM)] * 7,
            out_specs=(vmem, vmem, smem),
            scratch_shapes=[
                v(128, 128),
                v(128, 32),
                pltpu.SMEM((1, 3, 1, ATOMS), jnp.int32),
                pltpu.SMEM((1, 1, ATOMS), jnp.int32),
                v(2, 9, ATOMS, 9),
                pltpu.VMEM(packed_constants.shape, BF16),
                v(96, 128),
                v(144, 128),
                v(144, 128),
                v(128, 128),
                v(8, 256),
                v(16, 8, 256),
                v(2, 128, 128),
                v(nb, 128, 128),
                v(8, 128),
                v(14, 8, 128),
                v(8, 128),
                v(14, 8, 128),
                v(2, 128, 128),
                v(2, 16, 128),
                v(2, 48, 128),
                v(ROWS_ONE, 128),
                v(STACK_ONE, 128),
                v(ROWS_TWO, 128),
                v(STACK_TWO, 128),
                v(1, 128),
                v(nx * ny, 1, 128),
                v(1, 128),
                v(nx * ny, 1, 128),
                pltpu.VMEM((2, 128, 512), BF16),
                pltpu.VMEM((2, 512, 128), BF16),
                v(5, 128, 128),
                pltpu.SemaphoreType.DMA((7,)),
                pltpu.SemaphoreType.DMA((11,)),
                pltpu.SemaphoreType.DMA((11,)),
            ],
            compiler_params=pltpu.CompilerParams(
                collective_id=0, has_side_effects=True, vmem_limit_bytes=60 << 20
            ),
        )(
            wave_bands.reshape(128, 128),
            potential.reshape(128, 32),
            jnp.transpose(atom_offsets, (0, 3, 1, 2)),
            proj_counts,
            jnp.transpose(dh_matrix, (0, 1, 3, 2, 4)).reshape(9, ATOMS, 9),
            jnp.transpose(ds_matrix, (0, 1, 3, 2, 4)).reshape(9, ATOMS, 9),
            jnp.asarray(packed_constants),
        )
        return bands.reshape(1, CX, CY, NZ), resid.reshape(1, CX, CY, NZ), energy

    return jax.shard_map(
        on_device,
        mesh=mesh,
        in_specs=(
            P("band", "dx", "dy", None),
            P("dx", "dy", "band"),
            P("dx", "dy", None, None),
            P("dx", "dy", None),
            P("dx", "dy", None, None, None),
            P("dx", "dy", None, None, None),
        ),
        out_specs=(P("band", "dx", "dy", None), P("band", "dx", "dy", None), P("band")),
        check_vma=False,
    )
```

```python
import functools

import jax
import jax.numpy as jnp
import numpy as np
from jax import lax
from jax.experimental import pallas as pl
from jax.experimental.pallas import tpu as pltpu
from jax.sharding import PartitionSpec as P

MESH = pl.DeviceIdType.MESH
F32 = jnp.float32
BF16 = jnp.bfloat16

STENCIL = (-49.0 / 18.0, 1.5, -0.15, 1.0 / 90.0)
RELAXATION = 2.0 / 3.0
MASS_SHIFT = 0.25
AMPLITUDE = 0.15
D_NORM = 0.28867513
CX, CY, NZ = 8, 16, 128
ATOMS = 4

DIAG = [3.0 / 4.0**level + MASS_SHIFT for level in range(3)]
GAIN = [RELAXATION / d for d in DIAG]
SIDE = [0.5 * GAIN[level] / 4.0**level for level in range(3)]


def pad8(n):
    return (n + 7) // 8 * 8


def cells(x0, x1, y0, y1):
    return [(i, j) for i in range(x0, x1) for j in range(y0, y1)]


def cross(out, inp):
    where = {c: n for n, c in enumerate(inp)}
    m = np.zeros((len(out), len(inp)))
    for row, (i, j) in enumerate(out):
        for c in ((i - 1, j), (i + 1, j), (i, j - 1), (i, j + 1)):
            if c in where:
                m[row, where[c]] = 1.0
    return m


def pick(out, inp):
    where = {c: n for n, c in enumerate(inp)}
    m = np.zeros((len(out), len(inp)))
    for row, c in enumerate(out):
        if c in where:
            m[row, where[c]] = 1.0
    return m


def average(out, inp):
    where = {c: n for n, c in enumerate(inp)}
    m = np.zeros((len(out), len(inp)))
    for row, (i, j) in enumerate(out):
        for c in cells(2 * i, 2 * i + 2, 2 * j, 2 * j + 2):
            if c in where:
                m[row, where[c]] = 0.25
    return m


def spread_to(out, inp):
    where = {c: n for n, c in enumerate(inp)}
    m = np.zeros((len(out), len(inp)))
    for row, (i, j) in enumerate(out):
        m[row, where[(i // 2, j // 2)]] = 1.0
    return m


def along_z(n):
    return np.eye(n, k=1) + np.eye(n, k=-1)


def halve_z(n):
    return np.repeat(np.eye(n // 2), 2, axis=0) * 0.5


def double_z(n):
    return np.repeat(np.eye(n), 2, axis=1)


def both(m):
    z = np.zeros_like(m)
    return np.block([[m, z], [z, m]])


def grown(m, rows, cols):
    out = np.zeros((rows, cols))
    out[: m.shape[0], : m.shape[1]] = m
    return out


FINE = cells(0, CX, 0, CY)
ONE = cells(-1, 5, -1, 9)
ONE_WIDE = cells(-2, 6, -2, 10)
TWO = cells(-1, 3, -1, 5)
TWO_WIDE = cells(-3, 5, -3, 7)

NEAR = [(a, b) for a in (-1, 0, 1) for b in (-1, 0, 1) if (a, b) != (0, 0)]
FAR = [(a, b) for a in (-2, -1, 0, 1, 2) for b in (-1, 0, 1) if (a, b) != (0, 0)]
GREET = NEAR + [(-1, -2), (1, -2)]
WINDOWS = [(a, b) for a in (0, 3, 6) for b in range(8) if (a, b) != (0, 0)]
SIDES = [(-1, 0), (1, 0)]


def blocks(own, wide, step, targets):
    wide = set(wide)
    table, at = {}, 0
    for t in targets:
        block = [c for c in own if (c[0] - step[0] * t[0], c[1] - step[1] * t[1]) in wide]
        table[t] = (at, block)
        at += pad8(len(block))
    return table, at


BLOCKS_ONE, ROWS_ONE = blocks(ONE, ONE_WIDE, (4, 8), NEAR)
BLOCKS_TWO, ROWS_TWO = blocks(TWO, TWO_WIDE, (2, 4), FAR)
OWN_ONE = pad8(len(ONE))
OWN_TWO = 32
STACK_ONE = ROWS_ONE + OWN_ONE
STACK_TWO = ROWS_TWO + OWN_TWO


def senders(table, rows, own):
    m = np.zeros((rows + (OWN_ONE if own is ONE else OWN_TWO), len(own)))
    for at, block in table.values():
        m[at : at + len(block)] = pick(block, own)
    m[rows : rows + len(own)] = np.eye(len(own))
    return m


def receivers(table, rows, own, wide, step):
    m = np.zeros((len(wide), rows + (OWN_ONE if own is ONE else OWN_TWO)))
    for t, (at, block) in table.items():
        here = [(i - step[0] * t[0], j - step[1] * t[1]) for i, j in block]
        m[:, at : at + len(block)] = pick(wide, here)
    m[:, rows : rows + len(own)] = pick(wide, own)
    return m


def constants():
    c = {}
    stack = {}
    kin_own = np.zeros((128, 128))
    kin_side = np.zeros((128, 144))
    kin_z = np.zeros((NZ, NZ))
    halo = (
        cells(-3, 0, 0, CY)
        + cells(8, 11, 0, CY)
        + [(x, y) for y in range(-3, 0) for x in range(CX)]
        + [(x, y) for y in range(16, 19) for x in range(CX)]
    )
    where_own = {cell: n for n, cell in enumerate(FINE)}
    where_halo = {cell: n for n, cell in enumerate(halo)}
    for row, (x, y) in enumerate(FINE):
        kin_own[row, row] = -1.5 * STENCIL[0]
        for reach in (1, 2, 3):
            for cell in ((x - reach, y), (x + reach, y), (x, y - reach), (x, y + reach)):
                if cell in where_own:
                    kin_own[row, where_own[cell]] += -0.5 * STENCIL[reach]
                else:
                    kin_side[row, where_halo[cell]] += -0.5 * STENCIL[reach]
    for reach in (1, 2, 3):
        kin_z += -0.5 * STENCIL[reach] * (np.eye(NZ, k=reach) + np.eye(NZ, k=-reach))
    c["kin_own"], c["kin_side"], c["kin_z"] = kin_own, kin_side, kin_z

    ring0 = cells(-2, 10, -2, 18)
    avg = average(ONE, ring0)
    one_plane = avg @ (pick(ring0, FINE) / 3.0 + SIDE[0] * cross(ring0, FINE))
    one_along = avg @ pick(ring0, FINE) * SIDE[0]
    send = senders(BLOCKS_ONE, ROWS_ONE, ONE)
    c["down_one"] = np.concatenate([send @ one_plane, send @ one_along], axis=1)

    ring1 = cells(-2, 6, -2, 10)
    avg = average(TWO, ring1)
    two_plane = avg @ (pick(ring1, ONE) / 3.0 + SIDE[1] * cross(ring1, ONE))
    two_along = avg @ pick(ring1, ONE) * SIDE[1]
    send = senders(BLOCKS_TWO, ROWS_TWO, TWO)
    c["down_two"] = np.concatenate(
        [send @ two @ one for two in (two_plane, two_along) for one in (one_plane, one_along)], axis=1
    )
    h0, n0, h1, n1 = halve_z(NZ), along_z(NZ), halve_z(64), along_z(64)
    c["down_z"] = np.concatenate(
        [both(m) for m in (h0, n0 @ h0, h0 @ h1, n0 @ h0 @ h1, h0 @ n1 @ h1, n0 @ h0 @ n1 @ h1)], axis=1
    )

    take = receivers(BLOCKS_TWO, ROWS_TWO, TWO, TWO_WIDE, (2, 4))
    mid = cells(-2, 4, -2, 6)
    n1 = cross(TWO, TWO_WIDE)
    n2 = cross(TWO, mid) @ cross(mid, TWO_WIDE)
    here = pick(TWO, TWO_WIDE)
    g, k = GAIN[2], SIDE[2]
    terms = [
        g * (13.0 / 9.0 * here + 5.0 / 3.0 * k * n1 + k * k * n2),
        g * (5.0 / 3.0 * k * here + 2.0 * k * k * n1),
        g * k * k * here,
    ]
    c["sweep_two"] = np.concatenate([t @ take for t in terms], axis=1)
    nz = along_z(32)
    c["sweep_two_z"] = np.concatenate(
        [grown(both(m), 128, 128) for m in (np.eye(32), nz, nz @ nz)], axis=1
    )

    take = receivers(BLOCKS_ONE, ROWS_ONE, ONE, ONE_WIDE, (4, 8))
    g, k = GAIN[1], SIDE[1]
    here, n1 = pick(ONE, ONE_WIDE), cross(ONE, ONE_WIDE)
    up = spread_to(ONE_WIDE, TWO)
    c["up_one"] = grown(
        np.concatenate(
            [
                g * (4.0 / 3.0 * here + k * n1) @ take,
                g * k * here @ take,
                grown((here / 3.0 + k * n1) @ up, len(ONE), OWN_TWO),
                grown(k * here @ up, len(ONE), OWN_TWO),
            ],
            axis=1,
        ),
        OWN_ONE,
        2 * STACK_ONE + 2 * OWN_TWO,
    )
    nz = along_z(64)
    c["one_z"] = both(nz)
    double = double_z(32)
    c["up_one_z"] = np.concatenate(
        [grown(both(double), 128, 128), grown(both(double @ nz), 128, 128)], axis=1
    )

    g, k = GAIN[0], SIDE[0]
    ring0 = cells(-1, 9, -1, 17)
    here, n1 = pick(FINE, ring0), cross(FINE, ring0)
    up = spread_to(ring0, ONE)
    faces = (
        cells(-1, 0, 0, CY) + cells(8, 9, 0, CY) + [(x, -1) for x in range(CX)] + [(x, 16) for x in range(CX)]
    )
    c["up_zero"] = np.concatenate(
        [
            g * (4.0 / 3.0 * np.eye(128) + k * cross(FINE, FINE)),
            grown((here / 3.0 + k * n1) @ up, 128, OWN_ONE),
            grown(k * here @ up, 128, OWN_ONE),
            g * k * cross(FINE, faces),
        ],
        axis=1,
    )
    nz = along_z(NZ)
    double = double_z(64)
    c["zero_z"] = nz
    c["up_zero_z"] = np.concatenate([grown(double, 128, 128), grown(double @ nz, 128, 128)], axis=1)
    return c


def packed():
    table, parts, at = {}, [], 0
    for name, m in constants().items():
        rows, cols = m.shape
        rows = (rows + 15) // 16 * 16
        m = grown(m, rows, (cols + 127) // 128 * 128).astype(np.float32)
        high = m.astype(jnp.bfloat16)
        low = (m - high.astype(np.float32)).astype(jnp.bfloat16)
        exact = not low.astype(np.float32).any()
        places = []
        for part in (high,) if exact else (high, low):
            tiles = [part[:, t : t + 128] for t in range(0, m.shape[1], 128)]
            places.append([at + n * rows for n in range(len(tiles))])
            at += rows * len(tiles)
            parts += tiles
        table[name] = (rows, cols, places)
    return table, np.concatenate(parts, axis=0)


def dot(a, b):
    return lax.dot_general(a, b, (((1,), (0,)), ((), ())), preferred_element_type=F32)


def split(x):
    high = x.astype(BF16)
    return high, (x - high.astype(F32)).astype(BF16)


def dot3(a, b):
    return dot(a[0], b[0]) + dot(a[1], b[0]) + dot(a[0], b[1])


def projector_of(p, right):
    left_of = jnp.where(p < 3, p, jnp.where(p == 3, 4, jnp.where(p == 4, 7, 99)))
    right_of = jnp.where(p == 0, 3, jnp.where(p < 3, p + 4, jnp.where(p < 5, 8, 99)))
    return jnp.where(right, right_of, left_of)


def kernel(shape, table, *refs):
    nb, nx, ny = shape
    (
        w_in, pot_in, offs_in, cnt_in, dh_in, ds_in, const_in,
        dirs_out, resid_out, change_out, sums_ref,
        w_ref, pot_ref, offs_ref, cnt_ref, d_ref, const,
        stage, halo, halo2, dirs, resid, changes, geo, geos, info, infos, infot, pots, qbuf, qrecv, qbuf2, qrecv2,
        fields, bface, bhalo, one_s, one_r, two_s, two_r, esend, ebuf, nbuf, nrecv, lsend, lbuf, zfun, zturn, wfun,
        lsem, ssem, rsem, osem,
    ) = refs
    loads = [
        pltpu.make_async_copy(src, dst, lsem.at[n])
        for n, (src, dst) in enumerate(
            (
                (offs_in, offs_ref), (cnt_in, cnt_ref), (dh_in, d_ref.at[0]), (ds_in, d_ref.at[1]),
                (w_in, w_ref), (pot_in, pot_ref), (const_in, const),
            )
        )
    ]
    for load in loads:
        load.start()

    def held(name):
        rows, cols, places = table[name]
        return [jnp.concatenate([const[at : at + rows, :] for at in tiles], axis=1)[:, :cols] for tiles in places]

    def from_left(name, x):
        c, (high, low) = held(name), split(x)
        total = dot(c[0], high) + dot(c[0], low)
        return total + dot(c[1], high) if len(c) > 1 else total

    def from_right(x, name):
        c, (high, low) = held(name), split(x)
        total = dot(high, c[0]) + dot(low, c[0])
        return total + dot(high, c[1]) if len(c) > 1 else total

    ib, ix, iy = lax.axis_index("band"), lax.axis_index("dx"), lax.axis_index("dy")

    def device(a, b, band=0):
        return (lax.rem(ib + band + nb, nb), lax.rem(ix + a + nx, nx), lax.rem(iy + b + ny, ny))

    def send(src, dst, k, where):
        pltpu.make_async_remote_copy(
            src_ref=src, dst_ref=dst, send_sem=ssem.at[k], recv_sem=rsem.at[k], device_id=where, device_id_type=MESH
        ).start()

    def arrive(ref, k):
        pltpu.make_async_copy(ref, ref, rsem.at[k]).wait()

    def left(ref, k):
        pltpu.make_async_copy(ref, ref, ssem.at[k]).wait()

    me = ix * ny + iy
    slot = lax.rem(ix, 4) * 4 + lax.rem(iy, 4)

    def kept(n):
        src, dst = ((dirs, dirs_out), (resid, resid_out), (changes, change_out))[n]
        return pltpu.make_async_copy(src, dst, osem.at[n])

    def keep(n):
        kept(n).start()

    infos[...] = jnp.zeros_like(infos)
    geos[...] = jnp.zeros_like(geos)
    barrier = pltpu.get_barrier_semaphore()

    for a, b in GREET:
        pl.semaphore_signal(barrier, inc=1, device_id=device(a, b), device_id_type=MESH)
    for i in range(1, nb):
        pl.semaphore_signal(barrier, inc=1, device_id=device(0, 0, i), device_id_type=MESH)

    lane = lax.broadcasted_iota(jnp.int32, (1, 128), 1)
    lane8 = lax.broadcasted_iota(jnp.int32, (8, 128), 1)
    row8 = lax.broadcasted_iota(jnp.int32, (8, 128), 0)
    loads[0].wait()
    loads[1].wait()
    centres = jnp.zeros((8, 128), F32)
    for k in range(ATOMS):
        for m, v in enumerate((offs_ref[0, 0, 0, k], offs_ref[0, 1, 0, k], offs_ref[0, 2, 0, k], cnt_ref[0, 0, k])):
            centres = jnp.where((lax.rem(row8, 4) == k) & (lane8 == m), v.astype(F32), centres)
    geo[...] = centres
    geos[slot] = centres
    loads[4].wait()
    for j in range(3):
        stage[8 * j : 8 * j + 8, :] = w_ref[pl.ds(j, 8, stride=16), :]
        stage[24 + 8 * j : 32 + 8 * j, :] = w_ref[pl.ds(13 + j, 8, stride=16), :]

    pl.semaphore_wait(barrier, len(GREET) + nb - 1)

    for a, b in NEAR:
        send(geo, geos.at[slot], 11, device(a, b))
    send(w_ref.at[pl.ds(0, 48)], halo.at[pl.ds(48, 48)], 1, device(-1, 0))
    send(w_ref.at[pl.ds(80, 48)], halo.at[pl.ds(0, 48)], 1, device(1, 0))
    send(stage.at[pl.ds(0, 24)], halo.at[pl.ds(120, 24)], 1, device(0, -1))
    send(stage.at[pl.ds(24, 24)], halo.at[pl.ds(96, 24)], 1, device(0, 1))
    for load in (loads[2], loads[3], loads[5]):
        load.wait()
    crossed, p_from, p_to = lane // 40, (lane // 8) % 5, lane % 8
    for right in (0, 1):
        j_of = projector_of(p_from, (crossed != right))
        i_of = projector_of(p_to, lane * 0 + right == 1)
        chosen = [((i_of == i) & (lane < 80)).astype(F32) for i in range(9)]
        from_j = [(j_of == j).astype(F32) for j in range(9)]
        for n in range(2):
            rows = jnp.zeros((ATOMS, 128), F32)
            for i in range(9):
                of_i = d_ref[n, i]
                full = of_i[:, 0:1] * from_j[0]
                for j in range(1, 9):
                    full = full + of_i[:, j : j + 1] * from_j[j]
                rows = rows + full * chosen[i]
            info[4 * right : 4 * right + 4, 128 * n : 128 * n + 128] = rows
    infos[slot] = info[...]
    for a, b in NEAR:
        send(info, infos.at[slot], 0, device(a, b))
    place = (
        lax.broadcasted_iota(jnp.int32, (32, 128), 0) + 32 * ib == lax.broadcasted_iota(jnp.int32, (32, 128), 1)
    ).astype(BF16)
    high, low = split(pot_ref[...])
    rest = pot_ref[...] - high.astype(F32) - low.astype(F32)
    pots[ib] = dot(high, place) + dot(low, place) + dot(rest.astype(BF16), place)
    for i in range(1, nb):
        send(pots.at[ib], pots.at[ib], 2, device(0, 0, i))
    w = w_ref[...]
    loads[6].wait()
    kin = from_left("kin_own", w) + from_right(w, "kin_z")

    arrive(geos.at[pl.ds(0, 8)], 11)
    centres = jnp.swapaxes(geos[...].reshape(128, 128), 0, 1)
    slot_x, slot_y = lane // 32, (lane // 8) % 4
    right_lane = (lane // 4) % 2 == 1
    rel_x = lax.rem(slot_x - ix + 1 + 16, 4) - 1
    rel_y = lax.rem(slot_y - iy + 1 + 16, 4) - 1
    centre_x = centres[0:1, :] + (rel_x * CX).astype(F32)
    centre_y = centres[1:2, :] + (rel_y * CY).astype(F32)
    centre_z = centres[2:3, :]
    count = centres[3:4, :]
    active = (projector_of(row8, jnp.broadcast_to(right_lane, (8, 128))).astype(F32) < count).astype(F32)

    def bells(n, centre):
        r = lax.broadcasted_iota(jnp.int32, (n, 128), 0).astype(F32) - centre
        inside = ((r > -6.5) & (r < 5.5)).astype(F32)
        q = r * r
        return r, q, [inside * jnp.exp(q * (-1.0 / s)) for s in (8.0, 9.68, 11.52)]

    rz, qz, (zs, zp, zd) = bells(NZ, centre_z)
    zp, zd = zp * (1.0 / 2.2), zd * (1.0 / 5.76)
    zs = (
        jnp.where(right_lane, rz * zp, zs), jnp.where(right_lane, rz * zd, zp), jnp.where(right_lane, qz * zd, zd), zd,
    )
    for n, v in enumerate(split(jnp.concatenate(zs, axis=1))):
        zfun[n] = v
    rx, qx, (xs, xp, xd) = bells(CX, centre_x)
    ry, qy, (ys, yp, yd) = bells(CY, centre_y)
    pairs = (
        (jnp.where(right_lane, xp, xs), jnp.where(right_lane, yp, ys)),
        (jnp.where(right_lane, xd, rx * xp), jnp.where(right_lane, ry * yd, yp)),
        (jnp.where(right_lane, rx * xd, xp), jnp.where(right_lane, yd, ry * yp)),
        (jnp.where(right_lane, xd, rx * xd), jnp.where(right_lane, (2.0 * D_NORM) * yd, ry * yd)),
    )
    for p, (fx, fy) in enumerate(pairs):
        wfun[p] = ((AMPLITUDE * fx)[:, None, :] * fy[None, :, :]).reshape(128, 128)
    on_x = jnp.where(right_lane, -D_NORM, 0.5) * AMPLITUDE
    on_y = jnp.where(right_lane, -D_NORM, -0.5) * AMPLITUDE
    wfun[4] = (
        (on_x * qx * xd)[:, None, :] * yd[None, :, :] + xd[:, None, :] * (on_y * qy * yd)[None, :, :]
    ).reshape(128, 128)
    tile_of = (0, 1, 1, 2, 3)

    def overlaps(field, more):
        part = dot3(split(field), (zfun[0], zfun[1]))
        rows = [
            jnp.sum(part[:, 128 * tile_of[p] : 128 * tile_of[p] + 128] * wfun[p], axis=0, keepdims=True) for p in range(5)
        ]
        return jnp.concatenate(rows + more + [jnp.zeros((3 - len(more), 128), F32)], axis=0)

    keep_x = {-2: (rel_x == -1).astype(F32), 2: (rel_x == 1).astype(F32)}

    def gather_overlaps(own, ref):
        total = None
        for a in range(-2, 3):
            line = None
            for b in (-1, 0, 1):
                v = own if (a, b) == (0, 0) else ref[FAR.index((a, b))]
                line = v if line is None else line + v
            line = line * keep_x[a] if a in keep_x else line
            total = line if total is None else total + line
        return total * active

    def coefficients(q, n):
        swapped = jnp.where(right_lane, pltpu.roll(q, 4, 1), pltpu.roll(q, 124, 1))
        total = None
        for c, v in enumerate((q, swapped)):
            for p in range(5):
                at = (c * 5 + p) * 8
                term = infot[n, at : at + 8, :] * v[p : p + 1, :]
                total = term if total is None else total + term
        return total * active

    def weights(coefs):
        tiles = [None] * 4
        for p in range(5):
            term = wfun[p] * coefs[p : p + 1, :]
            t = tile_of[p]
            tiles[t] = term if tiles[t] is None else tiles[t] + term
        return jnp.concatenate(tiles, axis=1)

    def correction(weight):
        return dot3(split(weight), (zturn[0], zturn[1]))

    def ring_send(src, dst, k):
        for a, b in FAR:
            send(src, dst.at[FAR.index((-a, -b))], k, device(a, b))

    q_own = overlaps(w, [])
    qbuf[...] = q_own
    ring_send(qbuf, qrecv, 3)
    for n, v in enumerate(split(jnp.concatenate([jnp.swapaxes(z, 0, 1) for z in zs], axis=0))):
        zturn[n] = v
    arrive(infos.at[pl.ds(0, 8)], 0)
    for n in range(2):
        infot[n] = jnp.swapaxes(infos[:, :, 128 * n : 128 * n + 128].reshape(128, 128), 0, 1)

    arrive(halo, 1)
    kin = kin + from_left("kin_side", halo[...])
    if nb > 1:
        arrive(pots.at[pl.ds(0, nb - 1)], 2)
    potential = pots[0]
    for i in range(1, nb):
        potential = potential + pots[i]
    h_local = kin + potential * w
    local = jnp.concatenate(
        [
            jnp.sum(w * h_local, axis=0, keepdims=True), jnp.sum(w * w, axis=0, keepdims=True), jnp.zeros((6, 128), F32),
        ],
        axis=0,
    )
    nbuf[...] = local
    for a, b in SIDES:
        send(nbuf, nrecv.at[SIDES.index((-a, -b))], 12, device(a, b))

    arrive(qrecv, 3)
    q = gather_overlaps(q_own, qrecv)
    coef_h, coef_s = coefficients(q, 0), coefficients(q, 1)

    def total_of(v):
        return jnp.sum(v, axis=1, keepdims=True)

    both_terms = correction(jnp.concatenate([weights(coef_h), weights(coef_s)], axis=0))
    h_w = h_local + both_terms[:128]
    s_w = w + both_terms[128:]
    fields[0] = h_w
    fields[1] = s_w

    of_atoms = jnp.concatenate(
        [
            jnp.sum(q * coef_h, axis=0, keepdims=True), jnp.sum(q * coef_s, axis=0, keepdims=True), jnp.zeros((6, 128), F32),
        ],
        axis=0,
    )
    arrive(nrecv, 12)

    near = of_atoms * (rel_y == 0).astype(F32)
    esend[1] = near * (rel_x <= 0).astype(F32) + local + nrecv[0]
    esend[0] = near * (rel_x <= 1).astype(F32) + local + nrecv[0] + nrecv[1]

    def share(first, second, mine, table, k):
        mine[...] = jnp.where(lane < 64, first, second)
        table[me] = mine[...]

        for a in range(nx):
            for b in range(ny):
                if (a, b) != (0, 0):
                    send(mine, table.at[me], k, device(a, b))

    def shared(table, k):
        arrive(table.at[pl.ds(0, nx * ny - 1)], k)
        total = jnp.sum(table[...], axis=0)
        return total[:, 0:1], total[:, 64:65]

    flat = from_right(jnp.concatenate([h_w, s_w], axis=1), "down_z")
    one = from_left("down_one", jnp.concatenate([flat[:, :128], flat[:, 128:256]], axis=0))
    one_s[...] = one[:ROWS_ONE]
    one_r[ROWS_ONE:STACK_ONE, :] = one[ROWS_ONE:]
    for t in NEAR:
        at, block = BLOCKS_ONE[t]
        n = pad8(len(block))
        send(one_s.at[pl.ds(at, n)], one_r.at[pl.ds(at, n)], 6, device(*t))
    lower, upper = flat[:, 256:384], flat[:, 384:]
    two = from_left(
        "down_two",
        jnp.concatenate([lower, pltpu.roll(lower, 64, 1), upper, pltpu.roll(upper, 64, 1)], axis=0),
    )
    two_s[...] = two[:ROWS_TWO]
    two_r[ROWS_TWO:STACK_TWO, :] = two[ROWS_TWO:]
    for t in FAR:
        at, block = BLOCKS_TWO[t]
        n = pad8(len(block))
        send(two_s.at[pl.ds(at, n)], two_r.at[pl.ds(at, n)], 7, device(*t))

    for n, (a, b) in enumerate(WINDOWS):
        send(esend.at[a // 6], ebuf.at[n], 4, device(-a, -b))
    for f in range(2):
        bface[f, 0:8, :] = fields[f, pl.ds(0, 8, stride=16), :]
        bface[f, 8:16, :] = fields[f, pl.ds(15, 8, stride=16), :]
    send(fields.at[:, pl.ds(0, 16)], bhalo.at[:, pl.ds(16, 16)], 5, device(-1, 0))
    send(fields.at[:, pl.ds(112, 16)], bhalo.at[:, pl.ds(0, 16)], 5, device(1, 0))
    send(bface.at[:, pl.ds(0, 8)], bhalo.at[:, pl.ds(40, 8)], 5, device(0, -1))
    send(bface.at[:, pl.ds(8, 8)], bhalo.at[:, pl.ds(32, 8)], 5, device(0, 1))

    arrive(one_s, 6)
    level1 = one_r[...]
    level1_z = from_right(level1, "one_z")
    arrive(two_s, 7)
    flat = from_right(two_r[...], "sweep_two_z")
    x2 = from_left("sweep_two", jnp.concatenate([flat[:, :128], flat[:, 128:256], flat[:, 256:]], axis=0))
    flat = from_right(x2, "up_one_z")
    x1 = from_left("up_one", jnp.concatenate([level1, level1_z, flat[:, :128], flat[:, 128:]], axis=0))
    arrive(ebuf, 4)
    sums = jnp.sum(ebuf[...], axis=0) + esend[0]
    energy = total_of(sums[0:1]) / total_of(sums[1:2])
    residual = h_w - energy * s_w
    resid[...] = residual
    keep(1)
    x1 = x1 - energy * pltpu.roll(x1, 64, 1)
    flat = from_right(x1, "up_zero_z")
    arrive(bhalo, 5)
    faces = bhalo[0] - energy * bhalo[1]
    direction = from_left(
        "up_zero", jnp.concatenate([residual, flat[:, :128], flat[:, 128:], faces], axis=0)
    ) + (GAIN[0] * SIDE[0]) * from_right(residual, "zero_z")

    dirs[...] = direction
    for j in range(3):
        stage[48 + 8 * j : 56 + 8 * j, :] = dirs[pl.ds(j, 8, stride=16), :]
        stage[72 + 8 * j : 80 + 8 * j, :] = dirs[pl.ds(13 + j, 8, stride=16), :]
    send(dirs.at[pl.ds(0, 48)], halo2.at[pl.ds(48, 48)], 8, device(-1, 0))
    send(dirs.at[pl.ds(80, 48)], halo2.at[pl.ds(0, 48)], 8, device(1, 0))
    send(stage.at[pl.ds(48, 24)], halo2.at[pl.ds(120, 24)], 8, device(0, -1))
    send(stage.at[pl.ds(72, 24)], halo2.at[pl.ds(96, 24)], 8, device(0, 1))
    q_own = overlaps(direction, [])
    qbuf2[...] = q_own
    ring_send(qbuf2, qrecv2, 9)
    keep(0)
    change = from_left("kin_own", direction) + from_right(direction, "kin_z")
    change = change + (potential - energy) * direction
    arrive(halo2, 8)
    change = change + from_left("kin_side", halo2[...])
    arrive(qrecv2, 9)
    q = gather_overlaps(q_own, qrecv2)
    change = change + correction(weights(coefficients(q, 0) - energy * coefficients(q, 1)))
    along = total_of(jnp.sum(residual * change, axis=0, keepdims=True))
    square = total_of(jnp.sum(change * change, axis=0, keepdims=True))
    share(along, square, lsend, lbuf, 10)
    changes[...] = change
    keep(2)

    left(infos.at[pl.ds(0, 8)], 0)
    left(halo, 1)
    if nb > 1:
        left(pots.at[pl.ds(0, nb - 1)], 2)
    left(qrecv, 3)
    left(ebuf, 4)
    left(geos.at[pl.ds(0, 8)], 11)
    left(nrecv, 12)
    left(bhalo, 5)
    left(one_s, 6)
    left(two_s, 7)
    left(halo2, 8)
    left(qrecv2, 9)
    left(lbuf.at[pl.ds(0, nx * ny - 1)], 10)

    along, square = shared(lbuf, 10)
    sums_ref[...] = jnp.where(lane < 64, -along / square, energy)
    for n in range(3):
        kept(n).wait()


def finish(w_ref, dirs_ref, resid_ref, change_ref, sums_ref, bands_ref, new_ref, energy_ref):
    step = sums_ref[0:1, 0:1]
    bands_ref[...] = w_ref[...] + step * dirs_ref[...]
    new_ref[...] = resid_ref[...] + step * change_ref[...]
    energy_ref[0] = sums_ref[0, 127]


def solution(mesh):
    shape = tuple(mesh.shape[name] for name in ("band", "dx", "dy"))
    nb, nx, ny = shape
    table, packed_constants = packed()

    def on_device(wave_bands, potential, atom_offsets, proj_counts, dh_matrix, ds_matrix):
        vmem = pl.BlockSpec(memory_space=pltpu.VMEM)
        smem = pl.BlockSpec(memory_space=pltpu.SMEM)
        v = lambda *dims: pltpu.VMEM(dims, F32)
        hbm = pl.BlockSpec(memory_space=pltpu.HBM)
        grid = jax.ShapeDtypeStruct((128, 128), F32)
        dirs, resid, changes, sums = pl.pallas_call(
            functools.partial(kernel, shape, table),
            out_shape=(grid, grid, grid, jax.ShapeDtypeStruct((1, 128), F32)),
            in_specs=[hbm] * 7,
            out_specs=(hbm, hbm, hbm, vmem),
            scratch_shapes=[
                v(128, 128),
                v(128, 32),
                pltpu.SMEM((1, 3, 1, ATOMS), jnp.int32),
                pltpu.SMEM((1, 1, ATOMS), jnp.int32),
                v(2, 9, ATOMS, 9),
                pltpu.VMEM(packed_constants.shape, BF16),
                v(96, 128),
                v(144, 128),
                v(144, 128),
                v(128, 128),
                v(128, 128),
                v(128, 128),
                v(8, 128),
                v(16, 8, 128),
                v(8, 256),
                v(16, 8, 256),
                v(2, 128, 128),
                v(nb, 128, 128),
                v(8, 128),
                v(14, 8, 128),
                v(8, 128),
                v(14, 8, 128),
                v(2, 128, 128),
                v(2, 16, 128),
                v(2, 48, 128),
                v(ROWS_ONE, 128),
                v(STACK_ONE, 128),
                v(ROWS_TWO, 128),
                v(STACK_TWO, 128),
                v(2, 8, 128),
                v(23, 8, 128),
                v(8, 128),
                v(2, 8, 128),
                v(1, 128),
                v(nx * ny, 1, 128),
                pltpu.VMEM((2, 128, 512), BF16),
                pltpu.VMEM((2, 512, 128), BF16),
                v(5, 128, 128),
                pltpu.SemaphoreType.DMA((7,)),
                pltpu.SemaphoreType.DMA((13,)),
                pltpu.SemaphoreType.DMA((13,)),
                pltpu.SemaphoreType.DMA((3,)),
            ],
            compiler_params=pltpu.CompilerParams(
                collective_id=0, has_side_effects=True, vmem_limit_bytes=60 << 20
            ),
        )(
            wave_bands.reshape(128, 128),
            potential.reshape(128, 32),
            jnp.transpose(atom_offsets, (0, 3, 1, 2)),
            proj_counts,
            jnp.transpose(dh_matrix, (0, 1, 3, 2, 4)).reshape(9, ATOMS, 9),
            jnp.transpose(ds_matrix, (0, 1, 3, 2, 4)).reshape(9, ATOMS, 9),
            jnp.asarray(packed_constants),
        )
        bands, resid, energy = pl.pallas_call(
            finish,
            out_shape=(grid, grid, jax.ShapeDtypeStruct((1,), F32)),
            in_specs=[vmem] * 5,
            out_specs=(vmem, vmem, smem),
            compiler_params=pltpu.CompilerParams(vmem_limit_bytes=60 << 20),
        )(wave_bands.reshape(128, 128), dirs, resid, changes, sums)
        return bands.reshape(1, CX, CY, NZ), resid.reshape(1, CX, CY, NZ), energy

    return jax.shard_map(
        on_device,
        mesh=mesh,
        in_specs=(
            P("band", "dx", "dy", None),
            P("dx", "dy", "band"),
            P("dx", "dy", None, None),
            P("dx", "dy", None),
            P("dx", "dy", None, None, None),
            P("dx", "dy", None, None, None),
        ),
        out_specs=(P("band", "dx", "dy", None), P("band", "dx", "dy", None), P("band")),
        check_vma=False,
    )
```

```python
import functools

import jax
import jax.numpy as jnp
import numpy as np
from jax import lax
from jax.experimental import pallas as pl
from jax.experimental.pallas import tpu as pltpu
from jax.sharding import PartitionSpec as P

MESH = pl.DeviceIdType.MESH
F32 = jnp.float32
BF16 = jnp.bfloat16

STENCIL = (-49.0 / 18.0, 1.5, -0.15, 1.0 / 90.0)
RELAXATION = 2.0 / 3.0
MASS_SHIFT = 0.25
AMPLITUDE = 0.15
D_NORM = 0.28867513
CX, CY, NZ = 8, 16, 128
ATOMS = 4

DIAG = [3.0 / 4.0**level + MASS_SHIFT for level in range(3)]
GAIN = [RELAXATION / d for d in DIAG]
SIDE = [0.5 * GAIN[level] / 4.0**level for level in range(3)]


def pad8(n):
    return (n + 7) // 8 * 8


def cells(x0, x1, y0, y1):
    return [(i, j) for i in range(x0, x1) for j in range(y0, y1)]


def cross(out, inp):
    where = {c: n for n, c in enumerate(inp)}
    m = np.zeros((len(out), len(inp)))
    for row, (i, j) in enumerate(out):
        for c in ((i - 1, j), (i + 1, j), (i, j - 1), (i, j + 1)):
            if c in where:
                m[row, where[c]] = 1.0
    return m


def pick(out, inp):
    where = {c: n for n, c in enumerate(inp)}
    m = np.zeros((len(out), len(inp)))
    for row, c in enumerate(out):
        if c in where:
            m[row, where[c]] = 1.0
    return m


def average(out, inp):
    where = {c: n for n, c in enumerate(inp)}
    m = np.zeros((len(out), len(inp)))
    for row, (i, j) in enumerate(out):
        for c in cells(2 * i, 2 * i + 2, 2 * j, 2 * j + 2):
            if c in where:
                m[row, where[c]] = 0.25
    return m


def spread_to(out, inp):
    where = {c: n for n, c in enumerate(inp)}
    m = np.zeros((len(out), len(inp)))
    for row, (i, j) in enumerate(out):
        m[row, where[(i // 2, j // 2)]] = 1.0
    return m


def along_z(n):
    return np.eye(n, k=1) + np.eye(n, k=-1)


def halve_z(n):
    return np.repeat(np.eye(n // 2), 2, axis=0) * 0.5


def double_z(n):
    return np.repeat(np.eye(n), 2, axis=1)


def both(m):
    z = np.zeros_like(m)
    return np.block([[m, z], [z, m]])


def grown(m, rows, cols):
    out = np.zeros((rows, cols))
    out[: m.shape[0], : m.shape[1]] = m
    return out


FINE = cells(0, CX, 0, CY)
ONE = cells(-1, 5, -1, 9)
ONE_WIDE = cells(-2, 6, -2, 10)
TWO = cells(-1, 3, -1, 5)
TWO_WIDE = cells(-3, 5, -3, 7)

NEAR = [(a, b) for a in (-1, 0, 1) for b in (-1, 0, 1) if (a, b) != (0, 0)]
FAR = [(a, b) for a in (-2, -1, 0, 1, 2) for b in (-1, 0, 1) if (a, b) != (0, 0)]
GREET = NEAR + [(-1, -2), (1, -2)]
WINDOWS = [(a, b) for a in (0, 3, 6) for b in range(8) if (a, b) != (0, 0)]
SIDES = [(-1, 0), (1, 0)]


def within(among, of, reach):
    return [c for c in among if min(abs(c[0] - d[0]) + abs(c[1] - d[1]) for d in of) <= reach]


ONE_USED = [c for c in ONE if not (c[0] in (-1, 4) and c[1] in (-1, 8))]


def blocks(own, wide, step, targets, halves):
    wide = set(wide)
    table, at = {}, 0
    for t in targets:
        block = [c for c in own if (c[0] - step[0] * t[0], c[1] - step[1] * t[1]) in wide]
        rows = pad8((len(block) + halves - 1) // halves)
        table[t] = (at, rows, block)
        at += rows
    return table, at


BLOCKS_ONE, ROWS_ONE = blocks(ONE_USED, within(ONE_WIDE, ONE_USED, 1), (4, 8), NEAR, 1)
BLOCKS_TWO, ROWS_TWO = blocks(TWO, within(TWO_WIDE, TWO, 2), (2, 4), FAR, 2)
MIXED, ROWS_NEAR, ROWS_FAR = {}, 0, 0
for tile in FAR:
    rows_one = BLOCKS_ONE[tile][1] if tile in BLOCKS_ONE else 0
    rows_two = BLOCKS_TWO[tile][1]
    if rows_one:
        MIXED[tile] = (ROWS_NEAR, rows_one, rows_two)
        ROWS_NEAR += rows_one + rows_two
    else:
        MIXED[tile] = (ROWS_FAR, 0, rows_two)
        ROWS_FAR += rows_two
OWN_ONE = pad8(len(ONE))
OWN_TWO = 32
STACK_ONE = ROWS_ONE + OWN_ONE
STACK_TWO = ROWS_TWO + OWN_TWO


def senders(table, rows, own, own_rows, half=0):
    m = np.zeros((rows + own_rows, len(own)))
    for at, n, block in table.values():
        part = block[half * n : half * n + n]
        m[at : at + len(part)] = pick(part, own)
    if half == 0:
        m[rows : rows + len(own)] = np.eye(len(own))
    return m


def receivers(table, rows, own, own_rows, wide, step, half=0):
    m = np.zeros((len(wide), rows + own_rows))
    for t, (at, n, block) in table.items():
        here = [(i - step[0] * t[0], j - step[1] * t[1]) for i, j in block[half * n : half * n + n]]
        m[:, at : at + len(here)] = pick(wide, here)
    if half == 0:
        m[:, rows : rows + len(own)] = pick(wide, own)
    return m


def constants():
    c = {}
    stack = {}
    kin_own = np.zeros((128, 128))
    kin_side = np.zeros((128, 144))
    kin_z = np.zeros((NZ, NZ))
    halo = (
        cells(-3, 0, 0, CY)
        + cells(8, 11, 0, CY)
        + [(x, y) for y in range(-3, 0) for x in range(CX)]
        + [(x, y) for y in range(16, 19) for x in range(CX)]
    )
    where_own = {cell: n for n, cell in enumerate(FINE)}
    where_halo = {cell: n for n, cell in enumerate(halo)}
    for row, (x, y) in enumerate(FINE):
        kin_own[row, row] = -1.5 * STENCIL[0]
        for reach in (1, 2, 3):
            for cell in ((x - reach, y), (x + reach, y), (x, y - reach), (x, y + reach)):
                if cell in where_own:
                    kin_own[row, where_own[cell]] += -0.5 * STENCIL[reach]
                else:
                    kin_side[row, where_halo[cell]] += -0.5 * STENCIL[reach]
    for reach in (1, 2, 3):
        kin_z += -0.5 * STENCIL[reach] * (np.eye(NZ, k=reach) + np.eye(NZ, k=-reach))
    c["kin_own"], c["kin_side"], c["kin_z"] = kin_own, kin_side, kin_z

    ring0 = cells(-2, 10, -2, 18)
    avg = average(ONE, ring0)
    one_plane = avg @ (pick(ring0, FINE) / 3.0 + SIDE[0] * cross(ring0, FINE))
    one_along = avg @ pick(ring0, FINE) * SIDE[0]
    send = senders(BLOCKS_ONE, ROWS_ONE, ONE, OWN_ONE)
    c["down_one"] = np.concatenate([send @ one_plane, send @ one_along], axis=1)

    ring1 = cells(-2, 6, -2, 10)
    avg = average(TWO, ring1)
    two_plane = avg @ (pick(ring1, ONE) / 3.0 + SIDE[1] * cross(ring1, ONE))
    two_along = avg @ pick(ring1, ONE) * SIDE[1]
    sends = [senders(BLOCKS_TWO, ROWS_TWO, TWO, OWN_TWO, half) for half in (0, 1)]
    c["down_two"] = np.concatenate(
        [send @ two @ one for send in sends for two in (two_plane, two_along) for one in (one_plane, one_along)], axis=1
    )
    h0, n0, h1, n1 = halve_z(NZ), along_z(NZ), halve_z(64), along_z(64)
    c["down_z"] = np.concatenate(
        [both(m) for m in (h0, n0 @ h0, h0 @ h1, n0 @ h0 @ h1, h0 @ n1 @ h1, n0 @ h0 @ n1 @ h1)], axis=1
    )

    takes = [receivers(BLOCKS_TWO, ROWS_TWO, TWO, OWN_TWO, TWO_WIDE, (2, 4), half) for half in (0, 1)]
    mid = cells(-2, 4, -2, 6)
    n1 = cross(TWO, TWO_WIDE)
    n2 = cross(TWO, mid) @ cross(mid, TWO_WIDE)
    here = pick(TWO, TWO_WIDE)
    g, k = GAIN[2], SIDE[2]
    terms = [
        g * (13.0 / 9.0 * here + 5.0 / 3.0 * k * n1 + k * k * n2),
        g * (5.0 / 3.0 * k * here + 2.0 * k * k * n1),
        g * k * k * here,
    ]
    c["sweep_two"] = np.concatenate([t @ take for take in takes for t in terms], axis=1)
    nz = along_z(32)
    places = [grown(both(m), 64, 128) for m in (np.eye(32), nz, nz @ nz)]
    blank = np.zeros((64, 128))
    c["sweep_two_z"] = np.concatenate(
        [np.concatenate([m, blank]) for m in places] + [np.concatenate([blank, m]) for m in places], axis=1
    )

    take = receivers(BLOCKS_ONE, ROWS_ONE, ONE, OWN_ONE, ONE_WIDE, (4, 8))
    g, k = GAIN[1], SIDE[1]
    here, n1 = pick(ONE, ONE_WIDE), cross(ONE, ONE_WIDE)
    up = spread_to(ONE_WIDE, TWO)
    c["up_one"] = grown(
        np.concatenate(
            [
                g * (4.0 / 3.0 * here + k * n1) @ take,
                g * k * here @ take,
                grown((here / 3.0 + k * n1) @ up, len(ONE), OWN_TWO),
                grown(k * here @ up, len(ONE), OWN_TWO),
            ],
            axis=1,
        ),
        OWN_ONE,
        2 * STACK_ONE + 2 * OWN_TWO,
    )
    nz = along_z(64)
    c["one_z"] = both(nz)
    double = double_z(32)
    c["up_one_z"] = np.concatenate(
        [grown(both(double), 128, 128), grown(both(double @ nz), 128, 128)], axis=1
    )

    g, k = GAIN[0], SIDE[0]
    ring0 = cells(-1, 9, -1, 17)
    here, n1 = pick(FINE, ring0), cross(FINE, ring0)
    up = spread_to(ring0, ONE)
    faces = (
        cells(-1, 0, 0, CY) + cells(8, 9, 0, CY) + [(x, -1) for x in range(CX)] + [(x, 16) for x in range(CX)]
    )
    c["up_zero"] = np.concatenate(
        [
            g * (4.0 / 3.0 * np.eye(128) + k * cross(FINE, FINE)),
            grown((here / 3.0 + k * n1) @ up, 128, OWN_ONE),
            grown(k * here @ up, 128, OWN_ONE),
            g * k * cross(FINE, faces),
        ],
        axis=1,
    )
    nz = along_z(NZ)
    double = double_z(64)
    c["zero_z"] = nz
    c["up_zero_z"] = np.concatenate([grown(double, 128, 128), grown(double @ nz, 128, 128)], axis=1)
    return c


def packed():
    table, parts, at = {}, [], 0
    for name, m in constants().items():
        rows, cols = m.shape
        rows = (rows + 15) // 16 * 16
        m = grown(m, rows, (cols + 127) // 128 * 128).astype(np.float32)
        high = m.astype(jnp.bfloat16)
        low = (m - high.astype(np.float32)).astype(jnp.bfloat16)
        exact = not low.astype(np.float32).any()
        places = []
        for part in (high,) if exact else (high, low):
            tiles = [part[:, t : t + 128] for t in range(0, m.shape[1], 128)]
            places.append([at + n * rows for n in range(len(tiles))])
            at += rows * len(tiles)
            parts += tiles
        table[name] = (rows, cols, places)
    return table, np.concatenate(parts, axis=0)


def dot(a, b):
    return lax.dot_general(a, b, (((1,), (0,)), ((), ())), preferred_element_type=F32)


def split(x):
    high = x.astype(BF16)
    return high, (x - high.astype(F32)).astype(BF16)


def dot3(a, b):
    return dot(a[0], b[0]) + dot(a[1], b[0]) + dot(a[0], b[1])


def projector_of(p, right):
    left_of = jnp.where(p < 3, p, jnp.where(p == 3, 4, jnp.where(p == 4, 7, 99)))
    right_of = jnp.where(p == 0, 3, jnp.where(p < 3, p + 4, jnp.where(p < 5, 8, 99)))
    return jnp.where(right, right_of, left_of)


def kernel(shape, table, *refs):
    nb, nx, ny = shape
    (
        w_in, pot_in, offs_in, cnt_in, dh_in, ds_in, const_in,
        dirs_out, resid_out, change_out, sums_ref,
        w_ref, pot_ref, offs_ref, cnt_ref, d_ref, const,
        stage, halo, halo2, dirs, resid, changes, geo, geos, info, infos, infot, pots, qbuf, qrecv, qbuf2, qrecv2,
        fields, bface, bhalo, near_s, near_r, far_s, far_r, esend, ebuf, nbuf, nrecv, lsend, lbuf, zfun, zturn, wfun,
        lsem, ssem, rsem, osem,
    ) = refs
    loads = [
        pltpu.make_async_copy(src, dst, lsem.at[n])
        for n, (src, dst) in enumerate(
            (
                (offs_in, offs_ref), (cnt_in, cnt_ref), (dh_in, d_ref.at[0]), (ds_in, d_ref.at[1]),
                (w_in, w_ref), (pot_in, pot_ref), (const_in, const),
            )
        )
    ]
    for load in loads:
        load.start()

    def held(name):
        rows, cols, places = table[name]
        return [jnp.concatenate([const[at : at + rows, :] for at in tiles], axis=1)[:, :cols] for tiles in places]

    def from_left(name, x):
        c, (high, low) = held(name), split(x)
        total = dot(c[0], high) + dot(c[0], low)
        return total + dot(c[1], high) if len(c) > 1 else total

    def from_right(x, name):
        c, (high, low) = held(name), split(x)
        total = dot(high, c[0]) + dot(low, c[0])
        return total + dot(high, c[1]) if len(c) > 1 else total

    ib, ix, iy = lax.axis_index("band"), lax.axis_index("dx"), lax.axis_index("dy")

    def device(a, b, band=0):
        return (lax.rem(ib + band + nb, nb), lax.rem(ix + a + nx, nx), lax.rem(iy + b + ny, ny))

    def send(src, dst, k, where):
        pltpu.make_async_remote_copy(
            src_ref=src, dst_ref=dst, send_sem=ssem.at[k], recv_sem=rsem.at[k], device_id=where, device_id_type=MESH
        ).start()

    def arrive(ref, k):
        pltpu.make_async_copy(ref, ref, rsem.at[k]).wait()

    def left(ref, k):
        pltpu.make_async_copy(ref, ref, ssem.at[k]).wait()

    me = ix * ny + iy
    slot = lax.rem(ix, 4) * 4 + lax.rem(iy, 4)

    def kept(n):
        src, dst = ((dirs, dirs_out), (resid, resid_out), (changes, change_out))[n]
        return pltpu.make_async_copy(src, dst, osem.at[n])

    def keep(n):
        kept(n).start()

    infos[...] = jnp.zeros_like(infos)
    geos[...] = jnp.zeros_like(geos)
    barrier = pltpu.get_barrier_semaphore()

    for a, b in GREET:
        pl.semaphore_signal(barrier, inc=1, device_id=device(a, b), device_id_type=MESH)
    for i in range(1, nb):
        pl.semaphore_signal(barrier, inc=1, device_id=device(0, 0, i), device_id_type=MESH)

    lane = lax.broadcasted_iota(jnp.int32, (1, 128), 1)
    lane8 = lax.broadcasted_iota(jnp.int32, (8, 128), 1)
    row8 = lax.broadcasted_iota(jnp.int32, (8, 128), 0)
    loads[0].wait()
    loads[1].wait()
    centres = jnp.zeros((8, 128), F32)
    for k in range(ATOMS):
        for m, v in enumerate((offs_ref[0, 0, 0, k], offs_ref[0, 1, 0, k], offs_ref[0, 2, 0, k], cnt_ref[0, 0, k])):
            centres = jnp.where((lax.rem(row8, 4) == k) & (lane8 == m), v.astype(F32), centres)
    geo[...] = centres
    geos[slot] = centres
    loads[4].wait()
    for j in range(3):
        stage[8 * j : 8 * j + 8, :] = w_ref[pl.ds(j, 8, stride=16), :]
        stage[24 + 8 * j : 32 + 8 * j, :] = w_ref[pl.ds(13 + j, 8, stride=16), :]

    pl.semaphore_wait(barrier, len(GREET) + nb - 1)

    for a, b in NEAR:
        send(geo, geos.at[slot], 11, device(a, b))
    send(w_ref.at[pl.ds(0, 48)], halo.at[pl.ds(48, 48)], 1, device(-1, 0))
    send(w_ref.at[pl.ds(80, 48)], halo.at[pl.ds(0, 48)], 1, device(1, 0))
    send(stage.at[pl.ds(0, 24)], halo.at[pl.ds(120, 24)], 1, device(0, -1))
    send(stage.at[pl.ds(24, 24)], halo.at[pl.ds(96, 24)], 1, device(0, 1))
    for load in (loads[2], loads[3], loads[5]):
        load.wait()
    packed_pot = jnp.zeros((32, 128), F32)
    for g in range(4):
        place = (
            lax.broadcasted_iota(jnp.int32, (32, 128), 0) + 32 * g == lax.broadcasted_iota(jnp.int32, (32, 128), 1)
        ).astype(BF16)
        part = pot_ref[32 * g : 32 * g + 32, :]
        high, low = split(part)
        rest = part - high.astype(F32) - low.astype(F32)
        packed_pot = packed_pot + dot(high, place) + dot(low, place) + dot(rest.astype(BF16), place)
    pots[ib] = packed_pot
    for i in range(1, nb):
        send(pots.at[ib], pots.at[ib], 2, device(0, 0, i))
    crossed, p_from, p_to = lane // 40, (lane // 8) % 5, lane % 8
    for right in (0, 1):
        j_of = projector_of(p_from, (crossed != right))
        i_of = projector_of(p_to, lane * 0 + right == 1)
        chosen = [((i_of == i) & (lane < 80)).astype(F32) for i in range(9)]
        from_j = [(j_of == j).astype(F32) for j in range(9)]
        for n in range(2):
            rows = jnp.zeros((ATOMS, 128), F32)
            for i in range(9):
                of_i = d_ref[n, i]
                full = of_i[:, 0:1] * from_j[0]
                for j in range(1, 9):
                    full = full + of_i[:, j : j + 1] * from_j[j]
                rows = rows + full * chosen[i]
            info[4 * right : 4 * right + 4, 128 * n : 128 * n + 128] = rows
    infos[slot] = info[...]
    for a, b in NEAR:
        send(info, infos.at[slot], 0, device(a, b))
    w = w_ref[...]
    loads[6].wait()
    kin = from_left("kin_own", w) + from_right(w, "kin_z")

    arrive(geos.at[pl.ds(0, 8)], 11)
    centres = jnp.swapaxes(geos[...].reshape(128, 128), 0, 1)
    slot_x, slot_y = lane // 32, (lane // 8) % 4
    right_lane = (lane // 4) % 2 == 1
    rel_x = lax.rem(slot_x - ix + 1 + 16, 4) - 1
    rel_y = lax.rem(slot_y - iy + 1 + 16, 4) - 1
    centre_x = centres[0:1, :] + (rel_x * CX).astype(F32)
    centre_y = centres[1:2, :] + (rel_y * CY).astype(F32)
    centre_z = centres[2:3, :]
    count = centres[3:4, :]
    active = (projector_of(row8, jnp.broadcast_to(right_lane, (8, 128))).astype(F32) < count).astype(F32)

    def bells(n, centre):
        r = lax.broadcasted_iota(jnp.int32, (n, 128), 0).astype(F32) - centre
        inside = ((r > -6.5) & (r < 5.5)).astype(F32)
        q = r * r
        return r, q, [inside * jnp.exp(q * (-1.0 / s)) for s in (8.0, 9.68, 11.52)]

    rz, qz, (zs, zp, zd) = bells(NZ, centre_z)
    zp, zd = zp * (1.0 / 2.2), zd * (1.0 / 5.76)
    zs = (
        jnp.where(right_lane, rz * zp, zs), jnp.where(right_lane, rz * zd, zp), jnp.where(right_lane, qz * zd, zd), zd,
    )
    for n, v in enumerate(split(jnp.concatenate(zs, axis=1))):
        zfun[n] = v
    rx, qx, (xs, xp, xd) = bells(CX, centre_x)
    ry, qy, (ys, yp, yd) = bells(CY, centre_y)
    pairs = (
        (jnp.where(right_lane, xp, xs), jnp.where(right_lane, yp, ys)),
        (jnp.where(right_lane, xd, rx * xp), jnp.where(right_lane, ry * yd, yp)),
        (jnp.where(right_lane, rx * xd, xp), jnp.where(right_lane, yd, ry * yp)),
        (jnp.where(right_lane, xd, rx * xd), jnp.where(right_lane, (2.0 * D_NORM) * yd, ry * yd)),
    )
    for p, (fx, fy) in enumerate(pairs):
        wfun[p] = ((AMPLITUDE * fx)[:, None, :] * fy[None, :, :]).reshape(128, 128)
    on_x = jnp.where(right_lane, -D_NORM, 0.5) * AMPLITUDE
    on_y = jnp.where(right_lane, -D_NORM, -0.5) * AMPLITUDE
    wfun[4] = (
        (on_x * qx * xd)[:, None, :] * yd[None, :, :] + xd[:, None, :] * (on_y * qy * yd)[None, :, :]
    ).reshape(128, 128)
    tile_of = (0, 1, 1, 2, 3)

    def overlaps(field, more):
        part = dot3(split(field), (zfun[0], zfun[1]))
        rows = [
            jnp.sum(part[:, 128 * tile_of[p] : 128 * tile_of[p] + 128] * wfun[p], axis=0, keepdims=True) for p in range(5)
        ]
        return jnp.concatenate(rows + more + [jnp.zeros((3 - len(more), 128), F32)], axis=0)

    keep_x = {-2: (rel_x == -1).astype(F32), 2: (rel_x == 1).astype(F32)}

    def gather_overlaps(own, ref):
        total = None
        for a in range(-2, 3):
            line = None
            for b in (-1, 0, 1):
                v = own if (a, b) == (0, 0) else ref[FAR.index((a, b))]
                line = v if line is None else line + v
            line = line * keep_x[a] if a in keep_x else line
            total = line if total is None else total + line
        return total * active

    def coefficients(q, n):
        swapped = jnp.where(right_lane, pltpu.roll(q, 4, 1), pltpu.roll(q, 124, 1))
        total = None
        for c, v in enumerate((q, swapped)):
            for p in range(5):
                at = (c * 5 + p) * 8
                term = infot[n, at : at + 8, :] * v[p : p + 1, :]
                total = term if total is None else total + term
        return total * active

    def weights(coefs):
        tiles = [None] * 4
        for p in range(5):
            term = wfun[p] * coefs[p : p + 1, :]
            t = tile_of[p]
            tiles[t] = term if tiles[t] is None else tiles[t] + term
        return jnp.concatenate(tiles, axis=1)

    def correction(weight):
        return dot3(split(weight), (zturn[0], zturn[1]))

    def ring_send(src, dst, k):
        for a, b in FAR:
            send(src, dst.at[FAR.index((-a, -b))], k, device(a, b))

    q_own = overlaps(w, [])
    qbuf[...] = q_own
    ring_send(qbuf, qrecv, 3)
    for n, v in enumerate(split(jnp.concatenate([jnp.swapaxes(z, 0, 1) for z in zs], axis=0))):
        zturn[n] = v
    arrive(infos.at[pl.ds(0, 8)], 0)
    for n in range(2):
        infot[n] = jnp.swapaxes(infos[:, :, 128 * n : 128 * n + 128].reshape(128, 128), 0, 1)

    arrive(halo, 1)
    kin = kin + from_left("kin_side", halo[...])
    if nb > 1:
        arrive(pots.at[pl.ds(0, nb - 1)], 2)
    groups = []
    for g in range(4):
        group = jnp.zeros((32, 128), F32)
        for i in range(nb):
            turn = 32 * (i - g) % 128
            part = pltpu.roll(pots[i], turn, 1) if turn else pots[i]
            group = jnp.where(lane // 32 == i, part, group)
        groups.append(group)
    potential = jnp.concatenate(groups, axis=0)
    h_local = kin + potential * w
    local = jnp.concatenate(
        [
            jnp.sum(w * h_local, axis=0, keepdims=True), jnp.sum(w * w, axis=0, keepdims=True),
        ],
        axis=0,
    )
    nbuf[...] = local
    for a, b in SIDES:
        send(nbuf, nrecv.at[SIDES.index((-a, -b))], 12, device(a, b))

    arrive(qrecv, 3)
    q = gather_overlaps(q_own, qrecv)
    coef_h, coef_s = coefficients(q, 0), coefficients(q, 1)

    def total_of(v):
        return jnp.sum(v, axis=1, keepdims=True)

    of_atoms = jnp.concatenate(
        [
            jnp.sum(q * coef_h, axis=0, keepdims=True), jnp.sum(q * coef_s, axis=0, keepdims=True),
        ],
        axis=0,
    )
    arrive(nrecv, 12)

    near = of_atoms * (rel_y == 0).astype(F32)
    esend[1] = near * (rel_x <= 0).astype(F32) + local + nrecv[0]
    esend[0] = near * (rel_x <= 1).astype(F32) + local + nrecv[0] + nrecv[1]
    for n, (a, b) in enumerate(WINDOWS):
        send(esend.at[a // 6], ebuf.at[n], 4, device(-a, -b))

    both_terms = correction(jnp.concatenate([weights(coef_h), weights(coef_s)], axis=0))
    h_w = h_local + both_terms[:128]
    s_w = w + both_terms[128:]
    fields[0] = h_w
    fields[1] = s_w

    def share(first, second, mine, table, k):
        mine[...] = jnp.where(lane < 64, first, second)
        table[me] = mine[...]

        for a in range(nx):
            for b in range(ny):
                if (a, b) != (0, 0):
                    send(mine, table.at[me], k, device(a, b))

    def shared(table, k):
        arrive(table.at[pl.ds(0, nx * ny - 1)], k)
        total = jnp.sum(table[...], axis=0)
        return total[:, 0:1], total[:, 64:65]

    flat = from_right(jnp.concatenate([h_w, s_w], axis=1), "down_z")
    lower, upper = flat[:, 256:384], flat[:, 384:]
    turned = [lower, pltpu.roll(lower, 64, 1), upper, pltpu.roll(upper, 64, 1)]
    on_left = lane < 64
    two = from_left(
        "down_two",
        jnp.concatenate(
            [jnp.where(on_left, m, 0.0) for m in turned]
            + [jnp.where(on_left, 0.0, turned[n]) for n in (1, 0, 3, 2)],
            axis=0,
        ),
    )
    for t in FAR:
        at, n1, n2 = MIXED[t]
        if n1 == 0:
            far_s[at : at + n2, :] = two[BLOCKS_TWO[t][0] : BLOCKS_TWO[t][0] + n2]
            send(far_s.at[pl.ds(at, n2)], far_r.at[pl.ds(at, n2)], 7, device(*t))
    one = from_left("down_one", jnp.concatenate([flat[:, :128], flat[:, 128:256]], axis=0))
    for t in NEAR:
        at, n1, n2 = MIXED[t]
        near_s[at : at + n1, :] = one[BLOCKS_ONE[t][0] : BLOCKS_ONE[t][0] + n1]
        near_s[at + n1 : at + n1 + n2, :] = two[BLOCKS_TWO[t][0] : BLOCKS_TWO[t][0] + n2]
        send(near_s.at[pl.ds(at, n1 + n2)], near_r.at[pl.ds(at, n1 + n2)], 6, device(*t))
    for f in range(2):
        bface[f, 0:8, :] = fields[f, pl.ds(0, 8, stride=16), :]
        bface[f, 8:16, :] = fields[f, pl.ds(15, 8, stride=16), :]
    send(fields.at[:, pl.ds(0, 16)], bhalo.at[:, pl.ds(16, 16)], 5, device(-1, 0))
    send(fields.at[:, pl.ds(112, 16)], bhalo.at[:, pl.ds(0, 16)], 5, device(1, 0))
    send(bface.at[:, pl.ds(0, 8)], bhalo.at[:, pl.ds(40, 8)], 5, device(0, -1))
    send(bface.at[:, pl.ds(8, 8)], bhalo.at[:, pl.ds(32, 8)], 5, device(0, 1))

    arrive(near_s, 6)
    level1 = jnp.concatenate(
        [near_r[MIXED[t][0] : MIXED[t][0] + MIXED[t][1], :] for t in NEAR] + [one[ROWS_ONE:]], axis=0
    )
    level1_z = from_right(level1, "one_z")
    arrive(far_s, 7)
    level2 = [
        near_r[at + n1 : at + n1 + n2, :] if n1 else far_r[at : at + n2, :] for at, n1, n2 in (MIXED[t] for t in FAR)
    ]
    flat = from_right(jnp.concatenate(level2 + [two[ROWS_TWO:]], axis=0), "sweep_two_z")
    x2 = from_left("sweep_two", jnp.concatenate([flat[:, 128 * n : 128 * n + 128] for n in range(6)], axis=0))
    flat = from_right(x2, "up_one_z")
    x1 = from_left("up_one", jnp.concatenate([level1, level1_z, flat[:, :128], flat[:, 128:]], axis=0))
    arrive(ebuf, 4)
    sums = jnp.sum(ebuf[...], axis=0) + esend[0]
    energy = total_of(sums[0:1]) / total_of(sums[1:2])
    residual = h_w - energy * s_w
    resid[...] = residual
    keep(1)
    x1 = x1 - energy * pltpu.roll(x1, 64, 1)
    flat = from_right(x1, "up_zero_z")
    arrive(bhalo, 5)
    faces = bhalo[0] - energy * bhalo[1]
    direction = from_left(
        "up_zero", jnp.concatenate([residual, flat[:, :128], flat[:, 128:], faces], axis=0)
    ) + (GAIN[0] * SIDE[0]) * from_right(residual, "zero_z")

    dirs[...] = direction
    for j in range(3):
        stage[48 + 8 * j : 56 + 8 * j, :] = dirs[pl.ds(j, 8, stride=16), :]
        stage[72 + 8 * j : 80 + 8 * j, :] = dirs[pl.ds(13 + j, 8, stride=16), :]
    send(dirs.at[pl.ds(0, 48)], halo2.at[pl.ds(48, 48)], 8, device(-1, 0))
    send(dirs.at[pl.ds(80, 48)], halo2.at[pl.ds(0, 48)], 8, device(1, 0))
    send(stage.at[pl.ds(48, 24)], halo2.at[pl.ds(120, 24)], 8, device(0, -1))
    send(stage.at[pl.ds(72, 24)], halo2.at[pl.ds(96, 24)], 8, device(0, 1))
    q_own = overlaps(direction, [])
    qbuf2[...] = q_own
    ring_send(qbuf2, qrecv2, 9)
    keep(0)
    change = from_left("kin_own", direction) + from_right(direction, "kin_z")
    change = change + (potential - energy) * direction
    arrive(halo2, 8)
    change = change + from_left("kin_side", halo2[...])
    arrive(qrecv2, 9)
    q = gather_overlaps(q_own, qrecv2)
    change = change + correction(weights(coefficients(q, 0) - energy * coefficients(q, 1)))
    along = total_of(jnp.sum(residual * change, axis=0, keepdims=True))
    square = total_of(jnp.sum(change * change, axis=0, keepdims=True))
    share(along, square, lsend, lbuf, 10)
    changes[...] = change
    keep(2)

    left(infos.at[pl.ds(0, 8)], 0)
    left(halo, 1)
    if nb > 1:
        left(pots.at[pl.ds(0, nb - 1)], 2)
    left(qrecv, 3)
    left(ebuf, 4)
    left(geos.at[pl.ds(0, 8)], 11)
    left(nrecv, 12)
    left(bhalo, 5)
    left(near_s, 6)
    left(far_s, 7)
    left(halo2, 8)
    left(qrecv2, 9)
    left(lbuf.at[pl.ds(0, nx * ny - 1)], 10)

    along, square = shared(lbuf, 10)
    sums_ref[...] = jnp.where(lane < 64, -along / square, energy)
    for n in range(3):
        kept(n).wait()


def finish(w_ref, dirs_ref, resid_ref, change_ref, sums_ref, bands_ref, new_ref, energy_ref):
    step = sums_ref[0:1, 0:1]
    bands_ref[...] = w_ref[...] + step * dirs_ref[...]
    new_ref[...] = resid_ref[...] + step * change_ref[...]
    energy_ref[0] = sums_ref[0, 127]


def solution(mesh):
    shape = tuple(mesh.shape[name] for name in ("band", "dx", "dy"))
    nb, nx, ny = shape
    table, packed_constants = packed()

    def on_device(wave_bands, potential, atom_offsets, proj_counts, dh_matrix, ds_matrix):
        vmem = pl.BlockSpec(memory_space=pltpu.VMEM)
        smem = pl.BlockSpec(memory_space=pltpu.SMEM)
        v = lambda *dims: pltpu.VMEM(dims, F32)
        hbm = pl.BlockSpec(memory_space=pltpu.HBM)
        grid = jax.ShapeDtypeStruct((128, 128), F32)
        dirs, resid, changes, sums = pl.pallas_call(
            functools.partial(kernel, shape, table),
            out_shape=(grid, grid, grid, jax.ShapeDtypeStruct((1, 128), F32)),
            in_specs=[hbm] * 7,
            out_specs=(hbm, hbm, hbm, vmem),
            scratch_shapes=[
                v(128, 128),
                v(128, 32),
                pltpu.SMEM((1, 3, 1, ATOMS), jnp.int32),
                pltpu.SMEM((1, 1, ATOMS), jnp.int32),
                v(2, 9, ATOMS, 9),
                pltpu.VMEM(packed_constants.shape, BF16),
                v(96, 128),
                v(144, 128),
                v(144, 128),
                v(128, 128),
                v(128, 128),
                v(128, 128),
                v(8, 128),
                v(16, 8, 128),
                v(8, 256),
                v(16, 8, 256),
                v(2, 128, 128),
                v(nb, 32, 128),
                v(8, 128),
                v(14, 8, 128),
                v(8, 128),
                v(14, 8, 128),
                v(2, 128, 128),
                v(2, 16, 128),
                v(2, 48, 128),
                v(ROWS_NEAR, 128),
                v(ROWS_NEAR, 128),
                v(ROWS_FAR, 128),
                v(ROWS_FAR, 128),
                v(2, 2, 128),
                v(23, 2, 128),
                v(2, 128),
                v(2, 2, 128),
                v(1, 128),
                v(nx * ny, 1, 128),
                pltpu.VMEM((2, 128, 512), BF16),
                pltpu.VMEM((2, 512, 128), BF16),
                v(5, 128, 128),
                pltpu.SemaphoreType.DMA((7,)),
                pltpu.SemaphoreType.DMA((13,)),
                pltpu.SemaphoreType.DMA((13,)),
                pltpu.SemaphoreType.DMA((3,)),
            ],
            compiler_params=pltpu.CompilerParams(
                collective_id=0, has_side_effects=True, vmem_limit_bytes=60 << 20
            ),
        )(
            wave_bands.reshape(128, 128),
            potential.reshape(128, 32),
            jnp.transpose(atom_offsets, (0, 3, 1, 2)),
            proj_counts,
            jnp.transpose(dh_matrix, (0, 1, 3, 2, 4)).reshape(9, ATOMS, 9),
            jnp.transpose(ds_matrix, (0, 1, 3, 2, 4)).reshape(9, ATOMS, 9),
            jnp.asarray(packed_constants),
        )
        bands, resid, energy = pl.pallas_call(
            finish,
            out_shape=(grid, grid, jax.ShapeDtypeStruct((1,), F32)),
            in_specs=[vmem] * 5,
            out_specs=(vmem, vmem, smem),
            compiler_params=pltpu.CompilerParams(vmem_limit_bytes=60 << 20),
        )(wave_bands.reshape(128, 128), dirs, resid, changes, sums)
        return bands.reshape(1, CX, CY, NZ), resid.reshape(1, CX, CY, NZ), energy

    return jax.shard_map(
        on_device,
        mesh=mesh,
        in_specs=(
            P("band", "dx", "dy", None),
            P("dx", "dy", "band"),
            P("dx", "dy", None, None),
            P("dx", "dy", None),
            P("dx", "dy", None, None, None),
            P("dx", "dy", None, None, None),
        ),
        out_specs=(P("band", "dx", "dy", None), P("band", "dx", "dy", None), P("band")),
        check_vma=False,
    )
```

```python
import functools

import jax
import jax.numpy as jnp
import numpy as np
from jax import lax
from jax.experimental import pallas as pl
from jax.experimental.pallas import tpu as pltpu
from jax.sharding import PartitionSpec as P

MESH = pl.DeviceIdType.MESH
F32 = jnp.float32
BF16 = jnp.bfloat16

STENCIL = (-49.0 / 18.0, 1.5, -0.15, 1.0 / 90.0)
RELAXATION = 2.0 / 3.0
MASS_SHIFT = 0.25
AMPLITUDE = 0.15
D_NORM = 0.28867513
CX, CY, NZ = 8, 16, 128
ATOMS = 4

DIAG = [3.0 / 4.0**level + MASS_SHIFT for level in range(3)]
GAIN = [RELAXATION / d for d in DIAG]
SIDE = [0.5 * GAIN[level] / 4.0**level for level in range(3)]


def pad8(n):
    return (n + 7) // 8 * 8


def cells(x0, x1, y0, y1):
    return [(i, j) for i in range(x0, x1) for j in range(y0, y1)]


def cross(out, inp):
    where = {c: n for n, c in enumerate(inp)}
    m = np.zeros((len(out), len(inp)))
    for row, (i, j) in enumerate(out):
        for c in ((i - 1, j), (i + 1, j), (i, j - 1), (i, j + 1)):
            if c in where:
                m[row, where[c]] = 1.0
    return m


def pick(out, inp):
    where = {c: n for n, c in enumerate(inp)}
    m = np.zeros((len(out), len(inp)))
    for row, c in enumerate(out):
        if c in where:
            m[row, where[c]] = 1.0
    return m


def average(out, inp):
    where = {c: n for n, c in enumerate(inp)}
    m = np.zeros((len(out), len(inp)))
    for row, (i, j) in enumerate(out):
        for c in cells(2 * i, 2 * i + 2, 2 * j, 2 * j + 2):
            if c in where:
                m[row, where[c]] = 0.25
    return m


def spread_to(out, inp):
    where = {c: n for n, c in enumerate(inp)}
    m = np.zeros((len(out), len(inp)))
    for row, (i, j) in enumerate(out):
        m[row, where[(i // 2, j // 2)]] = 1.0
    return m


def along_z(n):
    return np.eye(n, k=1) + np.eye(n, k=-1)


def halve_z(n):
    return np.repeat(np.eye(n // 2), 2, axis=0) * 0.5


def double_z(n):
    return np.repeat(np.eye(n), 2, axis=1)


def both(m):
    z = np.zeros_like(m)
    return np.block([[m, z], [z, m]])


def grown(m, rows, cols):
    out = np.zeros((rows, cols))
    out[: m.shape[0], : m.shape[1]] = m
    return out


FINE = cells(0, CX, 0, CY)
ONE = cells(-1, 5, -1, 9)
ONE_WIDE = cells(-2, 6, -2, 10)
TWO = cells(-1, 3, -1, 5)
TWO_WIDE = cells(-3, 5, -3, 7)

NEAR = [(a, b) for a in (-1, 0, 1) for b in (-1, 0, 1) if (a, b) != (0, 0)]
FAR = [(a, b) for a in (-2, -1, 0, 1, 2) for b in (-1, 0, 1) if (a, b) != (0, 0)]
GREET = [(-1, -2), (1, -2), (-1, -1), (-1, 1), (1, -1), (1, 1), (-1, 0), (1, 0), (0, -1), (0, 1)]
WINDOWS = [(a, b) for a in (0, 3, 6) for b in range(8) if (a, b) != (0, 0)]
SIDES = [(-1, 0), (1, 0)]


def away(tile):
    return -(2 * min(tile[0] % 8, -tile[0] % 8) + min(tile[1] % 8, -tile[1] % 8))


def within(among, of, reach):
    return [c for c in among if min(abs(c[0] - d[0]) + abs(c[1] - d[1]) for d in of) <= reach]


ONE_USED = [c for c in ONE if not (c[0] in (-1, 4) and c[1] in (-1, 8))]


def blocks(own, wide, step, targets, halves):
    wide = set(wide)
    table, at = {}, 0
    for t in targets:
        block = [c for c in own if (c[0] - step[0] * t[0], c[1] - step[1] * t[1]) in wide]
        rows = pad8((len(block) + halves - 1) // halves)
        table[t] = (at, rows, block)
        at += rows
    return table, at


BLOCKS_ONE, ROWS_ONE = blocks(ONE_USED, within(ONE_WIDE, ONE_USED, 1), (4, 8), NEAR, 1)
BLOCKS_TWO, ROWS_TWO = blocks(TWO, within(TWO_WIDE, TWO, 2), (2, 4), FAR, 2)
MIXED, ROWS_NEAR, ROWS_FAR = {}, 0, 0
for tile in FAR:
    rows_one = BLOCKS_ONE[tile][1] if tile in BLOCKS_ONE else 0
    rows_two = BLOCKS_TWO[tile][1]
    if rows_one:
        MIXED[tile] = (ROWS_NEAR, rows_one, rows_two)
        ROWS_NEAR += rows_one + rows_two
    else:
        MIXED[tile] = (ROWS_FAR, 0, rows_two)
        ROWS_FAR += rows_two
OWN_ONE = pad8(len(ONE))
OWN_TWO = 32
STACK_ONE = ROWS_ONE + OWN_ONE
STACK_TWO = ROWS_TWO + OWN_TWO


def senders(table, rows, own, own_rows, half=0):
    m = np.zeros((rows + own_rows, len(own)))
    for at, n, block in table.values():
        part = block[half * n : half * n + n]
        m[at : at + len(part)] = pick(part, own)
    if half == 0:
        m[rows : rows + len(own)] = np.eye(len(own))
    return m


def receivers(table, rows, own, own_rows, wide, step, half=0):
    m = np.zeros((len(wide), rows + own_rows))
    for t, (at, n, block) in table.items():
        here = [(i - step[0] * t[0], j - step[1] * t[1]) for i, j in block[half * n : half * n + n]]
        m[:, at : at + len(here)] = pick(wide, here)
    if half == 0:
        m[:, rows : rows + len(own)] = pick(wide, own)
    return m


def constants():
    c = {}
    stack = {}
    kin_own = np.zeros((128, 128))
    kin_side = np.zeros((128, 144))
    kin_z = np.zeros((NZ, NZ))
    halo = (
        cells(-3, 0, 0, CY)
        + cells(8, 11, 0, CY)
        + [(x, y) for y in range(-3, 0) for x in range(CX)]
        + [(x, y) for y in range(16, 19) for x in range(CX)]
    )
    where_own = {cell: n for n, cell in enumerate(FINE)}
    where_halo = {cell: n for n, cell in enumerate(halo)}
    for row, (x, y) in enumerate(FINE):
        kin_own[row, row] = -1.5 * STENCIL[0]
        for reach in (1, 2, 3):
            for cell in ((x - reach, y), (x + reach, y), (x, y - reach), (x, y + reach)):
                if cell in where_own:
                    kin_own[row, where_own[cell]] += -0.5 * STENCIL[reach]
                else:
                    kin_side[row, where_halo[cell]] += -0.5 * STENCIL[reach]
    for reach in (1, 2, 3):
        kin_z += -0.5 * STENCIL[reach] * (np.eye(NZ, k=reach) + np.eye(NZ, k=-reach))
    c["kin_own"], c["kin_side"], c["kin_z"] = kin_own, kin_side, kin_z

    ring0 = cells(-2, 10, -2, 18)
    avg = average(ONE, ring0)
    one_plane = avg @ (pick(ring0, FINE) / 3.0 + SIDE[0] * cross(ring0, FINE))
    one_along = avg @ pick(ring0, FINE) * SIDE[0]
    send = senders(BLOCKS_ONE, ROWS_ONE, ONE, OWN_ONE)
    c["down_one"] = np.concatenate([send @ one_plane, send @ one_along], axis=1)

    ring1 = cells(-2, 6, -2, 10)
    avg = average(TWO, ring1)
    two_plane = avg @ (pick(ring1, ONE) / 3.0 + SIDE[1] * cross(ring1, ONE))
    two_along = avg @ pick(ring1, ONE) * SIDE[1]
    sends = [senders(BLOCKS_TWO, ROWS_TWO, TWO, OWN_TWO, half) for half in (0, 1)]
    c["down_two"] = np.concatenate(
        [send @ two @ one for send in sends for two in (two_plane, two_along) for one in (one_plane, one_along)], axis=1
    )
    h0, n0, h1, n1 = halve_z(NZ), along_z(NZ), halve_z(64), along_z(64)
    c["down_z"] = np.concatenate(
        [both(m) for m in (h0, n0 @ h0, h0 @ h1, n0 @ h0 @ h1, h0 @ n1 @ h1, n0 @ h0 @ n1 @ h1)], axis=1
    )

    takes = [receivers(BLOCKS_TWO, ROWS_TWO, TWO, OWN_TWO, TWO_WIDE, (2, 4), half) for half in (0, 1)]
    mid = cells(-2, 4, -2, 6)
    n1 = cross(TWO, TWO_WIDE)
    n2 = cross(TWO, mid) @ cross(mid, TWO_WIDE)
    here = pick(TWO, TWO_WIDE)
    g, k = GAIN[2], SIDE[2]
    terms = [
        g * (13.0 / 9.0 * here + 5.0 / 3.0 * k * n1 + k * k * n2),
        g * (5.0 / 3.0 * k * here + 2.0 * k * k * n1),
        g * k * k * here,
    ]
    c["sweep_two"] = np.concatenate([t @ take for take in takes for t in terms], axis=1)
    nz = along_z(32)
    places = [grown(both(m), 64, 128) for m in (np.eye(32), nz, nz @ nz)]
    blank = np.zeros((64, 128))
    c["sweep_two_z"] = np.concatenate(
        [np.concatenate([m, blank]) for m in places] + [np.concatenate([blank, m]) for m in places], axis=1
    )

    take = receivers(BLOCKS_ONE, ROWS_ONE, ONE, OWN_ONE, ONE_WIDE, (4, 8))
    g, k = GAIN[1], SIDE[1]
    here, n1 = pick(ONE, ONE_WIDE), cross(ONE, ONE_WIDE)
    up = spread_to(ONE_WIDE, TWO)
    c["up_one"] = grown(
        np.concatenate(
            [
                g * (4.0 / 3.0 * here + k * n1) @ take,
                g * k * here @ take,
                grown((here / 3.0 + k * n1) @ up, len(ONE), OWN_TWO),
                grown(k * here @ up, len(ONE), OWN_TWO),
            ],
            axis=1,
        ),
        OWN_ONE,
        2 * STACK_ONE + 2 * OWN_TWO,
    )
    nz = along_z(64)
    c["one_z"] = both(nz)
    double = double_z(32)
    c["up_one_z"] = np.concatenate(
        [grown(both(double), 128, 128), grown(both(double @ nz), 128, 128)], axis=1
    )

    g, k = GAIN[0], SIDE[0]
    ring0 = cells(-1, 9, -1, 17)
    here, n1 = pick(FINE, ring0), cross(FINE, ring0)
    up = spread_to(ring0, ONE)
    faces = (
        cells(-1, 0, 0, CY) + cells(8, 9, 0, CY) + [(x, -1) for x in range(CX)] + [(x, 16) for x in range(CX)]
    )
    c["up_zero"] = np.concatenate(
        [
            g * (4.0 / 3.0 * np.eye(128) + k * cross(FINE, FINE)),
            grown((here / 3.0 + k * n1) @ up, 128, OWN_ONE),
            grown(k * here @ up, 128, OWN_ONE),
            g * k * cross(FINE, faces),
        ],
        axis=1,
    )
    nz = along_z(NZ)
    double = double_z(64)
    c["zero_z"] = nz
    c["up_zero_z"] = np.concatenate([grown(double, 128, 128), grown(double @ nz, 128, 128)], axis=1)
    return c


def packed():
    table, parts, at = {}, [], 0
    for name, m in constants().items():
        rows, cols = m.shape
        rows = (rows + 15) // 16 * 16
        m = grown(m, rows, (cols + 127) // 128 * 128).astype(np.float32)
        high = m.astype(jnp.bfloat16)
        low = (m - high.astype(np.float32)).astype(jnp.bfloat16)
        exact = not low.astype(np.float32).any()
        places = []
        for part in (high,) if exact else (high, low):
            tiles = [part[:, t : t + 128] for t in range(0, m.shape[1], 128)]
            places.append([at + n * rows for n in range(len(tiles))])
            at += rows * len(tiles)
            parts += tiles
        table[name] = (rows, cols, places)
    return table, np.concatenate(parts, axis=0)


def dot(a, b):
    return lax.dot_general(a, b, (((1,), (0,)), ((), ())), preferred_element_type=F32)


def split(x):
    high = x.astype(BF16)
    return high, (x - high.astype(F32)).astype(BF16)


def dot3(a, b):
    return dot(a[0], b[0]) + dot(a[1], b[0]) + dot(a[0], b[1])


def projector_of(p, right):
    left_of = jnp.where(p < 3, p, jnp.where(p == 3, 4, jnp.where(p == 4, 7, 99)))
    right_of = jnp.where(p == 0, 3, jnp.where(p < 3, p + 4, jnp.where(p < 5, 8, 99)))
    return jnp.where(right, right_of, left_of)


def kernel(shape, table, *refs):
    nb, nx, ny = shape
    (
        w_in, pot_in, offs_in, cnt_in, dh_in, ds_in, const_in,
        dirs_out, resid_out, change_out, energy_out, lbuf,
        w_ref, pot_ref, offs_ref, cnt_ref, d_ref, const,
        stage, halo, halo2, dirs, resid, changes, geo, geos, info, infos, infot, pots, qbuf, qrecv, qbuf2, qrecv2,
        fields, bface, bhalo, near_s, near_r, far_s, far_r, esend, ebuf, nbuf, nrecv, lsend, level, zfun, zturn, wfun,
        lsem, ssem, rsem, osem,
    ) = refs
    loads = [
        pltpu.make_async_copy(src, dst, lsem.at[n])
        for n, (src, dst) in enumerate(
            (
                (offs_in, offs_ref), (cnt_in, cnt_ref), (dh_in, d_ref.at[0]), (ds_in, d_ref.at[1]),
                (w_in, w_ref), (pot_in, pot_ref), (const_in, const),
            )
        )
    ]
    for load in loads:
        load.start()

    def held(name):
        rows, cols, places = table[name]
        return [jnp.concatenate([const[at : at + rows, :] for at in tiles], axis=1)[:, :cols] for tiles in places]

    def from_left(name, x):
        c, (high, low) = held(name), split(x)
        total = dot(c[0], high) + dot(c[0], low)
        return total + dot(c[1], high) if len(c) > 1 else total

    def from_right(x, name):
        c, (high, low) = held(name), split(x)
        total = dot(high, c[0]) + dot(low, c[0])
        return total + dot(high, c[1]) if len(c) > 1 else total

    ib, ix, iy = lax.axis_index("band"), lax.axis_index("dx"), lax.axis_index("dy")

    def device(a, b, band=0):
        return (lax.rem(ib + band + nb, nb), lax.rem(ix + a + nx, nx), lax.rem(iy + b + ny, ny))

    def send(src, dst, k, where):
        pltpu.make_async_remote_copy(
            src_ref=src, dst_ref=dst, send_sem=ssem.at[k], recv_sem=rsem.at[k], device_id=where, device_id_type=MESH
        ).start()

    def arrive(ref, k):
        pltpu.make_async_copy(ref, ref, rsem.at[k]).wait()

    def left(ref, k):
        pltpu.make_async_copy(ref, ref, ssem.at[k]).wait()

    me = ix * ny + iy
    slot = lax.rem(ix, 4) * 4 + lax.rem(iy, 4)

    def kept(n):
        src, dst = ((dirs, dirs_out), (resid, resid_out), (changes, change_out), (level, energy_out), (lsend, lbuf.at[me]))[n]
        return pltpu.make_async_copy(src, dst, osem.at[n])

    def keep(n):
        kept(n).start()

    infos[...] = jnp.zeros_like(infos)
    geos[...] = jnp.zeros_like(geos)
    barrier = pltpu.get_barrier_semaphore()

    for i in range(1, nb):
        pl.semaphore_signal(barrier, inc=1, device_id=device(0, 0, i), device_id_type=MESH)
    for a, b in GREET:
        pl.semaphore_signal(barrier, inc=1, device_id=device(a, b), device_id_type=MESH)
    lane = lax.broadcasted_iota(jnp.int32, (1, 128), 1)
    lane8 = lax.broadcasted_iota(jnp.int32, (8, 128), 1)
    row8 = lax.broadcasted_iota(jnp.int32, (8, 128), 0)
    loads[0].wait()
    loads[1].wait()
    centres = jnp.zeros((8, 128), F32)
    for k in range(ATOMS):
        for m, v in enumerate((offs_ref[0, 0, 0, k], offs_ref[0, 1, 0, k], offs_ref[0, 2, 0, k], cnt_ref[0, 0, k])):
            centres = jnp.where((lax.rem(row8, 4) == k) & (lane8 == m), v.astype(F32), centres)
    geo[...] = centres
    geos[slot] = centres
    loads[4].wait()
    for j in range(3):
        stage[8 * j : 8 * j + 8, :] = w_ref[pl.ds(j, 8, stride=16), :]
        stage[24 + 8 * j : 32 + 8 * j, :] = w_ref[pl.ds(13 + j, 8, stride=16), :]

    pl.semaphore_wait(barrier, len(GREET) + nb - 1)

    for a, b in NEAR:
        send(geo, geos.at[slot], 11, device(a, b))
    send(w_ref.at[pl.ds(0, 48)], halo.at[pl.ds(48, 48)], 1, device(-1, 0))
    send(w_ref.at[pl.ds(80, 48)], halo.at[pl.ds(0, 48)], 1, device(1, 0))
    send(stage.at[pl.ds(0, 24)], halo.at[pl.ds(120, 24)], 1, device(0, -1))
    send(stage.at[pl.ds(24, 24)], halo.at[pl.ds(96, 24)], 1, device(0, 1))
    for load in (loads[2], loads[3], loads[5]):
        load.wait()
    packed_pot = jnp.zeros((32, 128), F32)
    for g in range(4):
        place = (
            lax.broadcasted_iota(jnp.int32, (32, 128), 0) + 32 * g == lax.broadcasted_iota(jnp.int32, (32, 128), 1)
        ).astype(BF16)
        part = pot_ref[32 * g : 32 * g + 32, :]
        high, low = split(part)
        rest = part - high.astype(F32) - low.astype(F32)
        packed_pot = packed_pot + dot(high, place) + dot(low, place) + dot(rest.astype(BF16), place)
    pots[ib] = packed_pot
    for i in range(1, nb):
        send(pots.at[ib], pots.at[ib], 2, device(0, 0, i))
    crossed, p_from, p_to = lane // 40, (lane // 8) % 5, lane % 8
    for right in (0, 1):
        j_of = projector_of(p_from, (crossed != right))
        i_of = projector_of(p_to, lane * 0 + right == 1)
        chosen = [((i_of == i) & (lane < 80)).astype(F32) for i in range(9)]
        from_j = [(j_of == j).astype(F32) for j in range(9)]
        for n in range(2):
            rows = jnp.zeros((ATOMS, 128), F32)
            for i in range(9):
                of_i = d_ref[n, i]
                full = of_i[:, 0:1] * from_j[0]
                for j in range(1, 9):
                    full = full + of_i[:, j : j + 1] * from_j[j]
                rows = rows + full * chosen[i]
            info[4 * right : 4 * right + 4, 128 * n : 128 * n + 128] = rows
    infos[slot] = info[...]
    for a, b in NEAR:
        send(info, infos.at[slot], 0, device(a, b))
    w = w_ref[...]
    loads[6].wait()
    kin = from_left("kin_own", w) + from_right(w, "kin_z")

    arrive(geos.at[pl.ds(0, 8)], 11)
    centres = jnp.swapaxes(geos[...].reshape(128, 128), 0, 1)
    slot_x, slot_y = lane // 32, (lane // 8) % 4
    right_lane = (lane // 4) % 2 == 1
    rel_x = lax.rem(slot_x - ix + 1 + 16, 4) - 1
    rel_y = lax.rem(slot_y - iy + 1 + 16, 4) - 1
    centre_x = centres[0:1, :] + (rel_x * CX).astype(F32)
    centre_y = centres[1:2, :] + (rel_y * CY).astype(F32)
    centre_z = centres[2:3, :]
    count = centres[3:4, :]
    active = (projector_of(row8, jnp.broadcast_to(right_lane, (8, 128))).astype(F32) < count).astype(F32)

    def bells(n, centre):
        r = lax.broadcasted_iota(jnp.int32, (n, 128), 0).astype(F32) - centre
        inside = ((r > -6.5) & (r < 5.5)).astype(F32)
        q = r * r
        return r, q, [inside * jnp.exp(q * (-1.0 / s)) for s in (8.0, 9.68, 11.52)]

    rz, qz, (zs, zp, zd) = bells(NZ, centre_z)
    zp, zd = zp * (1.0 / 2.2), zd * (1.0 / 5.76)
    zs = (
        jnp.where(right_lane, rz * zp, zs), jnp.where(right_lane, rz * zd, zp), jnp.where(right_lane, qz * zd, zd), zd,
    )
    for n, v in enumerate(split(jnp.concatenate(zs, axis=1))):
        zfun[n] = v
    rx, qx, (xs, xp, xd) = bells(CX, centre_x)
    ry, qy, (ys, yp, yd) = bells(CY, centre_y)
    pairs = (
        (jnp.where(right_lane, xp, xs), jnp.where(right_lane, yp, ys)),
        (jnp.where(right_lane, xd, rx * xp), jnp.where(right_lane, ry * yd, yp)),
        (jnp.where(right_lane, rx * xd, xp), jnp.where(right_lane, yd, ry * yp)),
        (jnp.where(right_lane, xd, rx * xd), jnp.where(right_lane, (2.0 * D_NORM) * yd, ry * yd)),
    )
    for p, (fx, fy) in enumerate(pairs):
        wfun[p] = ((AMPLITUDE * fx)[:, None, :] * fy[None, :, :]).reshape(128, 128)
    on_x = jnp.where(right_lane, -D_NORM, 0.5) * AMPLITUDE
    on_y = jnp.where(right_lane, -D_NORM, -0.5) * AMPLITUDE
    wfun[4] = (
        (on_x * qx * xd)[:, None, :] * yd[None, :, :] + xd[:, None, :] * (on_y * qy * yd)[None, :, :]
    ).reshape(128, 128)
    tile_of = (0, 1, 1, 2, 3)

    def overlaps(field):
        part = dot3(split(field), (zfun[0], zfun[1]))
        rows = [
            jnp.sum(part[:, 128 * tile_of[p] : 128 * tile_of[p] + 128] * wfun[p], axis=0, keepdims=True) for p in range(5)
        ]
        return jnp.concatenate(rows, axis=0)

    keep_x = {-2: (rel_x == -1).astype(F32), 2: (rel_x == 1).astype(F32)}

    def gather_overlaps(own, ref):
        total = None
        for a in range(-2, 3):
            line = None
            for b in (-1, 0, 1):
                v = own if (a, b) == (0, 0) else ref[FAR.index((a, b))]
                line = v if line is None else line + v
            line = line * keep_x[a] if a in keep_x else line
            total = line if total is None else total + line
        return total * active[:5]

    def coefficients(q, n):
        swapped = jnp.where(right_lane, pltpu.roll(q, 4, 1), pltpu.roll(q, 124, 1))
        total = None
        for c, v in enumerate((q, swapped)):
            for p in range(5):
                at = (c * 5 + p) * 8
                term = infot[n, at : at + 8, :] * v[p : p + 1, :]
                total = term if total is None else total + term
        return total * active

    def weights(coefs):
        tiles = [None] * 4
        for p in range(5):
            term = wfun[p] * coefs[p : p + 1, :]
            t = tile_of[p]
            tiles[t] = term if tiles[t] is None else tiles[t] + term
        return jnp.concatenate(tiles, axis=1)

    def correction(weight):
        return dot3(split(weight), (zturn[0], zturn[1]))

    def ring_send(src, dst, k):
        for a, b in sorted(FAR, key=away):
            send(src, dst.at[FAR.index((-a, -b))], k, device(a, b))

    q_own = overlaps(w)
    qbuf[...] = q_own
    ring_send(qbuf, qrecv, 3)
    for n, v in enumerate(split(jnp.concatenate([jnp.swapaxes(z, 0, 1) for z in zs], axis=0))):
        zturn[n] = v
    arrive(infos.at[pl.ds(0, 8)], 0)
    for n in range(2):
        infot[n] = jnp.swapaxes(infos[:, :, 128 * n : 128 * n + 128].reshape(128, 128), 0, 1)

    arrive(halo, 1)
    kin = kin + from_left("kin_side", halo[...])
    if nb > 1:
        arrive(pots.at[pl.ds(0, nb - 1)], 2)
    groups = []
    for g in range(4):
        group = jnp.zeros((32, 128), F32)
        for i in range(nb):
            turn = 32 * (i - g) % 128
            part = pltpu.roll(pots[i], turn, 1) if turn else pots[i]
            group = jnp.where(lane // 32 == i, part, group)
        groups.append(group)
    potential = jnp.concatenate(groups, axis=0)
    h_local = kin + potential * w
    local = jnp.concatenate(
        [
            jnp.sum(w * h_local, axis=0, keepdims=True), jnp.sum(w * w, axis=0, keepdims=True),
        ],
        axis=0,
    )
    nbuf[...] = local
    for a, b in SIDES:
        send(nbuf, nrecv.at[SIDES.index((-a, -b))], 12, device(a, b))

    arrive(qrecv, 3)
    q = gather_overlaps(q_own, qrecv)
    coef_h, coef_s = coefficients(q, 0), coefficients(q, 1)

    def total_of(v):
        return jnp.sum(v, axis=1, keepdims=True)

    of_atoms = jnp.concatenate(
        [
            jnp.sum(q * coef_h[:5], axis=0, keepdims=True), jnp.sum(q * coef_s[:5], axis=0, keepdims=True),
        ],
        axis=0,
    )
    arrive(nrecv, 12)

    near = of_atoms * (rel_y == 0).astype(F32)
    esend[1] = near * (rel_x <= 0).astype(F32) + local + nrecv[0]
    esend[0] = near * (rel_x <= 1).astype(F32) + local + nrecv[0] + nrecv[1]
    for n, (a, b) in sorted(enumerate(WINDOWS), key=lambda x: away(x[1])):
        send(esend.at[a // 6], ebuf.at[n], 4, device(-a, -b))

    both_terms = correction(jnp.concatenate([weights(coef_h), weights(coef_s)], axis=0))
    h_w = h_local + both_terms[:128]
    s_w = w + both_terms[128:]
    fields[0] = h_w
    fields[1] = s_w

    def share(first, second, mine, table, k):
        mine[...] = jnp.where(lane < 64, first, second)

        others = [(a, b) for a in range(nx) for b in range(ny) if (a, b) != (0, 0)]
        for a, b in sorted(others, key=away):
            send(mine, table.at[me], k, device(a, b))

    flat = from_right(jnp.concatenate([h_w, s_w], axis=1), "down_z")
    lower, upper = flat[:, 256:384], flat[:, 384:]
    turned = [lower, pltpu.roll(lower, 64, 1), upper, pltpu.roll(upper, 64, 1)]
    on_left = lane < 64
    two = from_left(
        "down_two",
        jnp.concatenate(
            [jnp.where(on_left, m, 0.0) for m in turned]
            + [jnp.where(on_left, 0.0, turned[n]) for n in (1, 0, 3, 2)],
            axis=0,
        ),
    )
    for t in FAR:
        at, n1, n2 = MIXED[t]
        if n1 == 0:
            far_s[at : at + n2, :] = two[BLOCKS_TWO[t][0] : BLOCKS_TWO[t][0] + n2]
            send(far_s.at[pl.ds(at, n2)], far_r.at[pl.ds(at, n2)], 7, device(*t))
    one = from_left("down_one", jnp.concatenate([flat[:, :128], flat[:, 128:256]], axis=0))
    for t in NEAR:
        at, n1, n2 = MIXED[t]
        near_s[at : at + n1, :] = one[BLOCKS_ONE[t][0] : BLOCKS_ONE[t][0] + n1]
        near_s[at + n1 : at + n1 + n2, :] = two[BLOCKS_TWO[t][0] : BLOCKS_TWO[t][0] + n2]
        send(near_s.at[pl.ds(at, n1 + n2)], near_r.at[pl.ds(at, n1 + n2)], 6, device(*t))
    for f in range(2):
        bface[f, 0:8, :] = fields[f, pl.ds(0, 8, stride=16), :]
        bface[f, 8:16, :] = fields[f, pl.ds(15, 8, stride=16), :]
    send(fields.at[:, pl.ds(0, 16)], bhalo.at[:, pl.ds(16, 16)], 5, device(-1, 0))
    send(fields.at[:, pl.ds(112, 16)], bhalo.at[:, pl.ds(0, 16)], 5, device(1, 0))
    send(bface.at[:, pl.ds(0, 8)], bhalo.at[:, pl.ds(40, 8)], 5, device(0, -1))
    send(bface.at[:, pl.ds(8, 8)], bhalo.at[:, pl.ds(32, 8)], 5, device(0, 1))

    arrive(near_s, 6)
    level1 = jnp.concatenate(
        [near_r[MIXED[t][0] : MIXED[t][0] + MIXED[t][1], :] for t in NEAR] + [one[ROWS_ONE:]], axis=0
    )
    level1_z = from_right(level1, "one_z")
    arrive(far_s, 7)
    level2 = [
        near_r[at + n1 : at + n1 + n2, :] if n1 else far_r[at : at + n2, :] for at, n1, n2 in (MIXED[t] for t in FAR)
    ]
    flat = from_right(jnp.concatenate(level2 + [two[ROWS_TWO:]], axis=0), "sweep_two_z")
    x2 = from_left("sweep_two", jnp.concatenate([flat[:, 128 * n : 128 * n + 128] for n in range(6)], axis=0))
    flat = from_right(x2, "up_one_z")
    x1 = from_left("up_one", jnp.concatenate([level1, level1_z, flat[:, :128], flat[:, 128:]], axis=0))
    arrive(ebuf, 4)
    sums = jnp.sum(ebuf[...], axis=0) + esend[0]
    energy = total_of(sums[0:1]) / total_of(sums[1:2])
    residual = h_w - energy * s_w
    resid[...] = residual
    keep(1)
    level[...] = lane * 0.0 + energy
    keep(3)
    x1 = x1 - energy * pltpu.roll(x1, 64, 1)
    flat = from_right(x1, "up_zero_z")
    arrive(bhalo, 5)
    faces = bhalo[0] - energy * bhalo[1]
    direction = from_left(
        "up_zero", jnp.concatenate([residual, flat[:, :128], flat[:, 128:], faces], axis=0)
    ) + (GAIN[0] * SIDE[0]) * from_right(residual, "zero_z")

    dirs[...] = direction
    for j in range(3):
        stage[48 + 8 * j : 56 + 8 * j, :] = dirs[pl.ds(j, 8, stride=16), :]
        stage[72 + 8 * j : 80 + 8 * j, :] = dirs[pl.ds(13 + j, 8, stride=16), :]
    send(dirs.at[pl.ds(0, 48)], halo2.at[pl.ds(48, 48)], 8, device(-1, 0))
    send(dirs.at[pl.ds(80, 48)], halo2.at[pl.ds(0, 48)], 8, device(1, 0))
    send(stage.at[pl.ds(48, 24)], halo2.at[pl.ds(120, 24)], 8, device(0, -1))
    send(stage.at[pl.ds(72, 24)], halo2.at[pl.ds(96, 24)], 8, device(0, 1))
    q_own = overlaps(direction)
    qbuf2[...] = q_own
    ring_send(qbuf2, qrecv2, 9)
    keep(0)
    change = from_left("kin_own", direction) + from_right(direction, "kin_z")
    change = change + (potential - energy) * direction
    arrive(halo2, 8)
    change = change + from_left("kin_side", halo2[...])
    arrive(qrecv2, 9)
    q = gather_overlaps(q_own, qrecv2)
    change = change + correction(weights(coefficients(q, 0) - energy * coefficients(q, 1)))
    along = total_of(jnp.sum(residual * change, axis=0, keepdims=True))
    square = total_of(jnp.sum(change * change, axis=0, keepdims=True))
    share(along, square, lsend, lbuf, 10)
    changes[...] = change
    keep(2)
    keep(4)

    left(infos.at[pl.ds(0, 8)], 0)
    left(halo, 1)
    if nb > 1:
        left(pots.at[pl.ds(0, nb - 1)], 2)
    left(qrecv, 3)
    left(ebuf, 4)
    left(geos.at[pl.ds(0, 8)], 11)
    left(nrecv, 12)
    left(bhalo, 5)
    left(near_s, 6)
    left(far_s, 7)
    left(halo2, 8)
    left(qrecv2, 9)
    left(lbuf.at[pl.ds(0, nx * ny - 1)], 10)

    arrive(lbuf.at[pl.ds(0, nx * ny - 1)], 10)
    for n in range(5):
        kept(n).wait()


def finish(w_ref, dirs_ref, resid_ref, change_ref, level_ref, sums_ref, bands_ref, new_ref, energy_ref):
    sums = jnp.sum(sums_ref[...], axis=0)
    step = -sums[:, 0:1] / sums[:, 64:65]
    bands_ref[...] = w_ref[...] + step * dirs_ref[...]
    new_ref[...] = resid_ref[...] + step * change_ref[...]
    energy_ref[0] = level_ref[0, 0]


def solution(mesh):
    shape = tuple(mesh.shape[name] for name in ("band", "dx", "dy"))
    nb, nx, ny = shape
    table, packed_constants = packed()

    def on_device(wave_bands, potential, atom_offsets, proj_counts, dh_matrix, ds_matrix):
        vmem = pl.BlockSpec(memory_space=pltpu.VMEM)
        smem = pl.BlockSpec(memory_space=pltpu.SMEM)
        v = lambda *dims: pltpu.VMEM(dims, F32)
        hbm = pl.BlockSpec(memory_space=pltpu.HBM)
        grid = jax.ShapeDtypeStruct((128, 128), F32)
        parts = pl.pallas_call(
            functools.partial(kernel, shape, table),
            out_shape=(
                grid, grid, grid, jax.ShapeDtypeStruct((1, 128), F32), jax.ShapeDtypeStruct((nx * ny, 1, 128), F32),
            ),
            in_specs=[hbm] * 7,
            out_specs=(hbm,) * 5,
            scratch_shapes=[
                v(128, 128),
                v(128, 32),
                pltpu.SMEM((1, 3, 1, ATOMS), jnp.int32),
                pltpu.SMEM((1, 1, ATOMS), jnp.int32),
                v(2, 9, ATOMS, 9),
                pltpu.VMEM(packed_constants.shape, BF16),
                v(96, 128),
                v(144, 128),
                v(144, 128),
                v(128, 128),
                v(128, 128),
                v(128, 128),
                v(8, 128),
                v(16, 8, 128),
                v(8, 256),
                v(16, 8, 256),
                v(2, 128, 128),
                v(nb, 32, 128),
                v(5, 128),
                v(14, 5, 128),
                v(5, 128),
                v(14, 5, 128),
                v(2, 128, 128),
                v(2, 16, 128),
                v(2, 48, 128),
                v(ROWS_NEAR, 128),
                v(ROWS_NEAR, 128),
                v(ROWS_FAR, 128),
                v(ROWS_FAR, 128),
                v(2, 2, 128),
                v(23, 2, 128),
                v(2, 128),
                v(2, 2, 128),
                v(1, 128),
                v(1, 128),
                pltpu.VMEM((2, 128, 512), BF16),
                pltpu.VMEM((2, 512, 128), BF16),
                v(5, 128, 128),
                pltpu.SemaphoreType.DMA((7,)),
                pltpu.SemaphoreType.DMA((13,)),
                pltpu.SemaphoreType.DMA((13,)),
                pltpu.SemaphoreType.DMA((5,)),
            ],
            compiler_params=pltpu.CompilerParams(
                collective_id=0, has_side_effects=True, vmem_limit_bytes=60 << 20
            ),
        )(
            wave_bands.reshape(128, 128),
            potential.reshape(128, 32),
            jnp.transpose(atom_offsets, (0, 3, 1, 2)),
            proj_counts,
            jnp.transpose(dh_matrix, (0, 1, 3, 2, 4)).reshape(9, ATOMS, 9),
            jnp.transpose(ds_matrix, (0, 1, 3, 2, 4)).reshape(9, ATOMS, 9),
            jnp.asarray(packed_constants),
        )
        bands, resid, energy = pl.pallas_call(
            finish,
            out_shape=(grid, grid, jax.ShapeDtypeStruct((1,), F32)),
            in_specs=[vmem] * 4 + [smem, vmem],
            out_specs=(vmem, vmem, smem),
            compiler_params=pltpu.CompilerParams(vmem_limit_bytes=60 << 20),
        )(wave_bands.reshape(128, 128), *parts)
        return bands.reshape(1, CX, CY, NZ), resid.reshape(1, CX, CY, NZ), energy

    return jax.shard_map(
        on_device,
        mesh=mesh,
        in_specs=(
            P("band", "dx", "dy", None),
            P("dx", "dy", "band"),
            P("dx", "dy", None, None),
            P("dx", "dy", None),
            P("dx", "dy", None, None, None),
            P("dx", "dy", None, None, None),
        ),
        out_specs=(P("band", "dx", "dy", None), P("band", "dx", "dy", None), P("band")),
        check_vma=False,
    )
```

```python
import functools

import jax
import jax.numpy as jnp
import numpy as np
from jax import lax
from jax.experimental import pallas as pl
from jax.experimental.pallas import tpu as pltpu
from jax.sharding import PartitionSpec as P

MESH = pl.DeviceIdType.MESH
F32 = jnp.float32
BF16 = jnp.bfloat16

STENCIL = (-49.0 / 18.0, 1.5, -0.15, 1.0 / 90.0)
RELAXATION = 2.0 / 3.0
MASS_SHIFT = 0.25
AMPLITUDE = 0.15
D_NORM = 0.28867513
CX, CY, NZ = 8, 16, 128
ATOMS = 4

DIAG = [3.0 / 4.0**level + MASS_SHIFT for level in range(3)]
GAIN = [RELAXATION / d for d in DIAG]
SIDE = [0.5 * GAIN[level] / 4.0**level for level in range(3)]


def pad8(n):
    return (n + 7) // 8 * 8


def cells(x0, x1, y0, y1):
    return [(i, j) for i in range(x0, x1) for j in range(y0, y1)]


def cross(out, inp):
    where = {c: n for n, c in enumerate(inp)}
    m = np.zeros((len(out), len(inp)))
    for row, (i, j) in enumerate(out):
        for c in ((i - 1, j), (i + 1, j), (i, j - 1), (i, j + 1)):
            if c in where:
                m[row, where[c]] = 1.0
    return m


def pick(out, inp):
    where = {c: n for n, c in enumerate(inp)}
    m = np.zeros((len(out), len(inp)))
    for row, c in enumerate(out):
        if c in where:
            m[row, where[c]] = 1.0
    return m


def average(out, inp):
    where = {c: n for n, c in enumerate(inp)}
    m = np.zeros((len(out), len(inp)))
    for row, (i, j) in enumerate(out):
        for c in cells(2 * i, 2 * i + 2, 2 * j, 2 * j + 2):
            if c in where:
                m[row, where[c]] = 0.25
    return m


def spread_to(out, inp):
    where = {c: n for n, c in enumerate(inp)}
    m = np.zeros((len(out), len(inp)))
    for row, (i, j) in enumerate(out):
        m[row, where[(i // 2, j // 2)]] = 1.0
    return m


def along_z(n):
    return np.eye(n, k=1) + np.eye(n, k=-1)


def halve_z(n):
    return np.repeat(np.eye(n // 2), 2, axis=0) * 0.5


def double_z(n):
    return np.repeat(np.eye(n), 2, axis=1)


def both(m):
    z = np.zeros_like(m)
    return np.block([[m, z], [z, m]])


def grown(m, rows, cols):
    out = np.zeros((rows, cols))
    out[: m.shape[0], : m.shape[1]] = m
    return out


FINE = cells(0, CX, 0, CY)
ONE = cells(-1, 5, -1, 9)
ONE_WIDE = cells(-2, 6, -2, 10)
TWO = cells(-1, 3, -1, 5)
TWO_WIDE = cells(-3, 5, -3, 7)

NEAR = [(a, b) for a in (-1, 0, 1) for b in (-1, 0, 1) if (a, b) != (0, 0)]
FAR = [(a, b) for a in (-2, -1, 0, 1, 2) for b in (-1, 0, 1) if (a, b) != (0, 0)]
GREET = [(-1, -2), (1, -2), (-1, -1), (-1, 1), (1, -1), (1, 1), (-1, 0), (1, 0), (0, -1), (0, 1)]
WINDOWS = [(a, b) for a in (0, 3, 6) for b in range(8) if (a, b) != (0, 0)]
SIDES = [(-1, 0), (1, 0)]


def away(tile):
    return -(2 * min(tile[0] % 8, -tile[0] % 8) + min(tile[1] % 8, -tile[1] % 8))


def within(among, of, reach):
    return [c for c in among if min(abs(c[0] - d[0]) + abs(c[1] - d[1]) for d in of) <= reach]


ONE_USED = [c for c in ONE if not (c[0] in (-1, 4) and c[1] in (-1, 8))]


def blocks(own, wide, step, targets, halves):
    wide = set(wide)
    table, at = {}, 0
    for t in targets:
        block = [c for c in own if (c[0] - step[0] * t[0], c[1] - step[1] * t[1]) in wide]
        rows = pad8((len(block) + halves - 1) // halves)
        table[t] = (at, rows, block)
        at += rows
    return table, at


BLOCKS_ONE, ROWS_ONE = blocks(ONE_USED, within(ONE_WIDE, ONE_USED, 1), (4, 8), NEAR, 1)
BLOCKS_TWO, ROWS_TWO = blocks(TWO, within(TWO_WIDE, TWO, 2), (2, 4), FAR, 2)
MIXED, ROWS_NEAR, ROWS_FAR = {}, 0, 0
for tile in FAR:
    rows_one = BLOCKS_ONE[tile][1] if tile in BLOCKS_ONE else 0
    rows_two = BLOCKS_TWO[tile][1]
    if rows_one:
        MIXED[tile] = (ROWS_NEAR, rows_one, rows_two)
        ROWS_NEAR += rows_one + rows_two
    else:
        MIXED[tile] = (ROWS_FAR, 0, rows_two)
        ROWS_FAR += rows_two
OWN_ONE = pad8(len(ONE))
OWN_TWO = 32
STACK_ONE = ROWS_ONE + OWN_ONE
STACK_TWO = ROWS_TWO + OWN_TWO


def senders(table, rows, own, own_rows, half=0):
    m = np.zeros((rows + own_rows, len(own)))
    for at, n, block in table.values():
        part = block[half * n : half * n + n]
        m[at : at + len(part)] = pick(part, own)
    if half == 0:
        m[rows : rows + len(own)] = np.eye(len(own))
    return m


def receivers(table, rows, own, own_rows, wide, step, half=0):
    m = np.zeros((len(wide), rows + own_rows))
    for t, (at, n, block) in table.items():
        here = [(i - step[0] * t[0], j - step[1] * t[1]) for i, j in block[half * n : half * n + n]]
        m[:, at : at + len(here)] = pick(wide, here)
    if half == 0:
        m[:, rows : rows + len(own)] = pick(wide, own)
    return m


def constants():
    c = {}
    stack = {}
    kin_own = np.zeros((128, 128))
    kin_side = np.zeros((128, 144))
    kin_z = np.zeros((NZ, NZ))
    halo = (
        cells(-3, 0, 0, CY)
        + cells(8, 11, 0, CY)
        + [(x, y) for y in range(-3, 0) for x in range(CX)]
        + [(x, y) for y in range(16, 19) for x in range(CX)]
    )
    where_own = {cell: n for n, cell in enumerate(FINE)}
    where_halo = {cell: n for n, cell in enumerate(halo)}
    for row, (x, y) in enumerate(FINE):
        kin_own[row, row] = -1.5 * STENCIL[0]
        for reach in (1, 2, 3):
            for cell in ((x - reach, y), (x + reach, y), (x, y - reach), (x, y + reach)):
                if cell in where_own:
                    kin_own[row, where_own[cell]] += -0.5 * STENCIL[reach]
                else:
                    kin_side[row, where_halo[cell]] += -0.5 * STENCIL[reach]
    for reach in (1, 2, 3):
        kin_z += -0.5 * STENCIL[reach] * (np.eye(NZ, k=reach) + np.eye(NZ, k=-reach))
    c["kin_own"], c["kin_side"], c["kin_z"] = kin_own, kin_side, kin_z

    ring0 = cells(-2, 10, -2, 18)
    avg = average(ONE, ring0)
    one_plane = avg @ (pick(ring0, FINE) / 3.0 + SIDE[0] * cross(ring0, FINE))
    one_along = avg @ pick(ring0, FINE) * SIDE[0]
    send = senders(BLOCKS_ONE, ROWS_ONE, ONE, OWN_ONE)
    c["down_one"] = np.concatenate([send @ one_plane, send @ one_along], axis=1)

    ring1 = cells(-2, 6, -2, 10)
    avg = average(TWO, ring1)
    two_plane = avg @ (pick(ring1, ONE) / 3.0 + SIDE[1] * cross(ring1, ONE))
    two_along = avg @ pick(ring1, ONE) * SIDE[1]
    sends = [senders(BLOCKS_TWO, ROWS_TWO, TWO, OWN_TWO, half) for half in (0, 1)]
    c["down_two"] = np.concatenate(
        [send @ two @ one for send in sends for two in (two_plane, two_along) for one in (one_plane, one_along)], axis=1
    )
    h0, n0, h1, n1 = halve_z(NZ), along_z(NZ), halve_z(64), along_z(64)
    c["down_z"] = np.concatenate(
        [both(m) for m in (h0, n0 @ h0, h0 @ h1, n0 @ h0 @ h1, h0 @ n1 @ h1, n0 @ h0 @ n1 @ h1)], axis=1
    )

    takes = [receivers(BLOCKS_TWO, ROWS_TWO, TWO, OWN_TWO, TWO_WIDE, (2, 4), half) for half in (0, 1)]
    mid = cells(-2, 4, -2, 6)
    n1 = cross(TWO, TWO_WIDE)
    n2 = cross(TWO, mid) @ cross(mid, TWO_WIDE)
    here = pick(TWO, TWO_WIDE)
    g, k = GAIN[2], SIDE[2]
    terms = [
        g * (13.0 / 9.0 * here + 5.0 / 3.0 * k * n1 + k * k * n2),
        g * (5.0 / 3.0 * k * here + 2.0 * k * k * n1),
        g * k * k * here,
    ]
    c["sweep_two"] = np.concatenate([t @ take for take in takes for t in terms], axis=1)
    nz = along_z(32)
    places = [grown(both(m), 64, 128) for m in (np.eye(32), nz, nz @ nz)]
    blank = np.zeros((64, 128))
    c["sweep_two_z"] = np.concatenate(
        [np.concatenate([m, blank]) for m in places] + [np.concatenate([blank, m]) for m in places], axis=1
    )

    take = receivers(BLOCKS_ONE, ROWS_ONE, ONE, OWN_ONE, ONE_WIDE, (4, 8))
    g, k = GAIN[1], SIDE[1]
    here, n1 = pick(ONE, ONE_WIDE), cross(ONE, ONE_WIDE)
    up = spread_to(ONE_WIDE, TWO)
    c["up_one"] = grown(
        np.concatenate(
            [
                g * (4.0 / 3.0 * here + k * n1) @ take,
                g * k * here @ take,
                grown((here / 3.0 + k * n1) @ up, len(ONE), OWN_TWO),
                grown(k * here @ up, len(ONE), OWN_TWO),
            ],
            axis=1,
        ),
        OWN_ONE,
        2 * STACK_ONE + 2 * OWN_TWO,
    )
    nz = along_z(64)
    c["one_z"] = both(nz)
    double = double_z(32)
    c["up_one_z"] = np.concatenate(
        [grown(both(double), 128, 128), grown(both(double @ nz), 128, 128)], axis=1
    )

    g, k = GAIN[0], SIDE[0]
    ring0 = cells(-1, 9, -1, 17)
    here, n1 = pick(FINE, ring0), cross(FINE, ring0)
    up = spread_to(ring0, ONE)
    faces = (
        cells(-1, 0, 0, CY) + cells(8, 9, 0, CY) + [(x, -1) for x in range(CX)] + [(x, 16) for x in range(CX)]
    )
    c["up_zero"] = np.concatenate(
        [
            g * (4.0 / 3.0 * np.eye(128) + k * cross(FINE, FINE)),
            grown((here / 3.0 + k * n1) @ up, 128, OWN_ONE),
            grown(k * here @ up, 128, OWN_ONE),
            g * k * cross(FINE, faces),
        ],
        axis=1,
    )
    nz = along_z(NZ)
    double = double_z(64)
    c["zero_z"] = nz
    c["up_zero_z"] = np.concatenate([grown(double, 128, 128), grown(double @ nz, 128, 128)], axis=1)
    return c


def packed():
    table, parts, at = {}, [], 0
    for name, m in constants().items():
        rows, cols = m.shape
        rows = (rows + 15) // 16 * 16
        m = grown(m, rows, (cols + 127) // 128 * 128).astype(np.float32)
        high = m.astype(jnp.bfloat16)
        low = (m - high.astype(np.float32)).astype(jnp.bfloat16)
        exact = not low.astype(np.float32).any()
        places = []
        for part in (high,) if exact else (high, low):
            tiles = [part[:, t : t + 128] for t in range(0, m.shape[1], 128)]
            places.append([at + n * rows for n in range(len(tiles))])
            at += rows * len(tiles)
            parts += tiles
        table[name] = (rows, cols, places)
    return table, np.concatenate(parts, axis=0)


def dot(a, b):
    return lax.dot_general(a, b, (((1,), (0,)), ((), ())), preferred_element_type=F32)


def split(x):
    high = x.astype(BF16)
    return high, (x - high.astype(F32)).astype(BF16)


def dot3(a, b):
    return dot(a[0], b[0]) + dot(a[1], b[0]) + dot(a[0], b[1])


def projector_of(p, right):
    left_of = jnp.where(p < 3, p, jnp.where(p == 3, 4, jnp.where(p == 4, 7, 99)))
    right_of = jnp.where(p == 0, 3, jnp.where(p < 3, p + 4, jnp.where(p < 5, 8, 99)))
    return jnp.where(right, right_of, left_of)


def kernel(shape, table, *refs):
    nb, nx, ny = shape
    (
        w_in, pot_in, offs_in, cnt_in, dh_in, ds_in, const_in,
        dirs_out, resid_out, change_out, energy_out, lbuf,
        w_ref, pot_ref, offs_ref, cnt_ref, d_ref, const,
        stage, halo, halo2, dirs, resid, changes, geo, geos, info, infos, infot, pots, qbuf, qrecv, qbuf2, qrecv2,
        fields, bface, bhalo, near_s, near_r, far_s, far_r, esend, ebuf, nbuf, nrecv, lsend, level, zfun, zturn, wfun,
        lsem, ssem, rsem, osem,
    ) = refs
    loads = [
        pltpu.make_async_copy(src, dst, lsem.at[n])
        for n, (src, dst) in enumerate(
            (
                (offs_in, offs_ref), (cnt_in, cnt_ref), (dh_in, d_ref.at[0]), (ds_in, d_ref.at[1]),
                (w_in, w_ref), (pot_in, pot_ref), (const_in, const),
            )
        )
    ]
    for load in loads:
        load.start()

    def held(name):
        rows, cols, places = table[name]
        return [jnp.concatenate([const[at : at + rows, :] for at in tiles], axis=1)[:, :cols] for tiles in places]

    def from_left(name, x):
        c, (high, low) = held(name), split(x)
        total = dot(c[0], high) + dot(c[0], low)
        return total + dot(c[1], high) if len(c) > 1 else total

    def from_right(x, name):
        c, (high, low) = held(name), split(x)
        total = dot(high, c[0]) + dot(low, c[0])
        return total + dot(high, c[1]) if len(c) > 1 else total

    ib, ix, iy = lax.axis_index("band"), lax.axis_index("dx"), lax.axis_index("dy")

    def device(a, b, band=0):
        return (lax.rem(ib + band + nb, nb), lax.rem(ix + a + nx, nx), lax.rem(iy + b + ny, ny))

    def send(src, dst, k, where):
        pltpu.make_async_remote_copy(
            src_ref=src, dst_ref=dst, send_sem=ssem.at[k], recv_sem=rsem.at[k], device_id=where, device_id_type=MESH
        ).start()

    def arrive(ref, k):
        pltpu.make_async_copy(ref, ref, rsem.at[k]).wait()

    def left(ref, k):
        pltpu.make_async_copy(ref, ref, ssem.at[k]).wait()

    me = ix * ny + iy
    slot = lax.rem(ix, 4) * 4 + lax.rem(iy, 4)

    def kept(n):
        src, dst = ((dirs, dirs_out), (resid, resid_out), (changes, change_out), (level, energy_out), (lsend, lbuf.at[me]))[n]
        return pltpu.make_async_copy(src, dst, osem.at[n])

    def keep(n):
        kept(n).start()

    infos[...] = jnp.zeros_like(infos)
    geos[...] = jnp.zeros_like(geos)
    barrier = pltpu.get_barrier_semaphore()

    for i in range(1, nb):
        pl.semaphore_signal(barrier, inc=1, device_id=device(0, 0, i), device_id_type=MESH)
    for a, b in GREET:
        pl.semaphore_signal(barrier, inc=1, device_id=device(a, b), device_id_type=MESH)
    lane = lax.broadcasted_iota(jnp.int32, (1, 128), 1)
    lane8 = lax.broadcasted_iota(jnp.int32, (8, 128), 1)
    row8 = lax.broadcasted_iota(jnp.int32, (8, 128), 0)
    loads[0].wait()
    loads[1].wait()
    centres = jnp.zeros((1, 128), F32)
    for k in range(ATOMS):
        for m, v in enumerate((offs_ref[0, 0, 0, k], offs_ref[0, 1, 0, k], offs_ref[0, 2, 0, k], cnt_ref[0, 0, k])):
            centres = jnp.where(lane == 4 * m + k, v.astype(F32), centres)
    geo[...] = centres
    geos[slot] = centres
    loads[4].wait()
    for j in range(3):
        stage[8 * j : 8 * j + 8, :] = w_ref[pl.ds(j, 8, stride=16), :]
        stage[24 + 8 * j : 32 + 8 * j, :] = w_ref[pl.ds(13 + j, 8, stride=16), :]

    pl.semaphore_wait(barrier, len(GREET) + nb - 1)

    for a, b in NEAR:
        send(geo, geos.at[slot], 11, device(a, b))
    send(w_ref.at[pl.ds(0, 48)], halo.at[pl.ds(48, 48)], 1, device(-1, 0))
    send(w_ref.at[pl.ds(80, 48)], halo.at[pl.ds(0, 48)], 1, device(1, 0))
    send(stage.at[pl.ds(0, 24)], halo.at[pl.ds(120, 24)], 1, device(0, -1))
    send(stage.at[pl.ds(24, 24)], halo.at[pl.ds(96, 24)], 1, device(0, 1))
    for load in (loads[2], loads[3], loads[5]):
        load.wait()
    packed_pot = jnp.zeros((32, 128), F32)
    for g in range(4):
        place = (
            lax.broadcasted_iota(jnp.int32, (32, 128), 0) + 32 * g == lax.broadcasted_iota(jnp.int32, (32, 128), 1)
        ).astype(BF16)
        part = pot_ref[32 * g : 32 * g + 32, :]
        high, low = split(part)
        rest = part - high.astype(F32) - low.astype(F32)
        packed_pot = packed_pot + dot(high, place) + dot(low, place) + dot(rest.astype(BF16), place)
    pots[ib] = packed_pot
    for i in range(1, nb):
        send(pots.at[ib], pots.at[ib], 2, device(0, 0, i))
    crossed, p_from, p_to = lane // 40, (lane // 8) % 5, lane % 8
    for right in (0, 1):
        j_of = projector_of(p_from, (crossed != right))
        i_of = projector_of(p_to, lane * 0 + right == 1)
        chosen = [((i_of == i) & (lane < 80)).astype(F32) for i in range(9)]
        from_j = [(j_of == j).astype(F32) for j in range(9)]
        for n in range(2):
            rows = jnp.zeros((ATOMS, 128), F32)
            for i in range(9):
                of_i = d_ref[n, i]
                full = of_i[:, 0:1] * from_j[0]
                for j in range(1, 9):
                    full = full + of_i[:, j : j + 1] * from_j[j]
                rows = rows + full * chosen[i]
            info[4 * right : 4 * right + 4, 128 * n : 128 * n + 128] = rows
    infos[slot] = info[...]
    for a, b in NEAR:
        send(info, infos.at[slot], 0, device(a, b))
    w = w_ref[...]
    loads[6].wait()
    kin = from_left("kin_own", w) + from_right(w, "kin_z")

    arrive(geos.at[pl.ds(0, 8)], 11)
    chosen = ((lax.rem(lane8, 4) == lax.rem(row8, 4)) & (lane8 < 16)).astype(F32)
    turned = jnp.swapaxes((geos[...] * chosen[None]).reshape(128, 128), 0, 1)
    centres = [jnp.sum(turned[4 * m : 4 * m + 4], axis=0, keepdims=True) for m in range(4)]
    slot_x, slot_y = lane // 32, (lane // 8) % 4
    right_lane = (lane // 4) % 2 == 1
    rel_x = lax.rem(slot_x - ix + 1 + 16, 4) - 1
    rel_y = lax.rem(slot_y - iy + 1 + 16, 4) - 1
    centre_x = centres[0] + (rel_x * CX).astype(F32)
    centre_y = centres[1] + (rel_y * CY).astype(F32)
    centre_z = centres[2]
    count = centres[3]
    active = (projector_of(row8, jnp.broadcast_to(right_lane, (8, 128))).astype(F32) < count).astype(F32)

    def bells(n, centre):
        r = lax.broadcasted_iota(jnp.int32, (n, 128), 0).astype(F32) - centre
        inside = ((r > -6.5) & (r < 5.5)).astype(F32)
        q = r * r
        return r, q, [inside * jnp.exp(q * (-1.0 / s)) for s in (8.0, 9.68, 11.52)]

    rz, qz, (zs, zp, zd) = bells(NZ, centre_z)
    zp, zd = zp * (1.0 / 2.2), zd * (1.0 / 5.76)
    zs = (
        jnp.where(right_lane, rz * zp, zs), jnp.where(right_lane, rz * zd, zp), jnp.where(right_lane, qz * zd, zd), zd,
    )
    for n, v in enumerate(split(jnp.concatenate(zs, axis=1))):
        zfun[n] = v
    rx, qx, (xs, xp, xd) = bells(CX, centre_x)
    ry, qy, (ys, yp, yd) = bells(CY, centre_y)
    pairs = (
        (jnp.where(right_lane, xp, xs), jnp.where(right_lane, yp, ys)),
        (jnp.where(right_lane, xd, rx * xp), jnp.where(right_lane, ry * yd, yp)),
        (jnp.where(right_lane, rx * xd, xp), jnp.where(right_lane, yd, ry * yp)),
        (jnp.where(right_lane, xd, rx * xd), jnp.where(right_lane, (2.0 * D_NORM) * yd, ry * yd)),
    )
    for p, (fx, fy) in enumerate(pairs):
        wfun[p] = ((AMPLITUDE * fx)[:, None, :] * fy[None, :, :]).reshape(128, 128)
    on_x = jnp.where(right_lane, -D_NORM, 0.5) * AMPLITUDE
    on_y = jnp.where(right_lane, -D_NORM, -0.5) * AMPLITUDE
    wfun[4] = (
        (on_x * qx * xd)[:, None, :] * yd[None, :, :] + xd[:, None, :] * (on_y * qy * yd)[None, :, :]
    ).reshape(128, 128)
    tile_of = (0, 1, 1, 2, 3)

    def overlaps(field):
        part = dot3(split(field), (zfun[0], zfun[1]))
        rows = [
            jnp.sum(part[:, 128 * tile_of[p] : 128 * tile_of[p] + 128] * wfun[p], axis=0, keepdims=True) for p in range(5)
        ]
        return jnp.concatenate(rows, axis=0)

    keep_x = {-2: (rel_x == -1).astype(F32), 2: (rel_x == 1).astype(F32)}

    def gather_overlaps(own, ref):
        total = None
        for a in range(-2, 3):
            line = None
            for b in (-1, 0, 1):
                v = own if (a, b) == (0, 0) else ref[FAR.index((a, b))]
                line = v if line is None else line + v
            line = line * keep_x[a] if a in keep_x else line
            total = line if total is None else total + line
        return total * active[:5]

    def coefficients(q, n):
        swapped = jnp.where(right_lane, pltpu.roll(q, 4, 1), pltpu.roll(q, 124, 1))
        total = None
        for c, v in enumerate((q, swapped)):
            for p in range(5):
                at = (c * 5 + p) * 8
                term = infot[n, at : at + 8, :] * v[p : p + 1, :]
                total = term if total is None else total + term
        return total * active

    def weights(coefs):
        tiles = [None] * 4
        for p in range(5):
            term = wfun[p] * coefs[p : p + 1, :]
            t = tile_of[p]
            tiles[t] = term if tiles[t] is None else tiles[t] + term
        return jnp.concatenate(tiles, axis=1)

    def correction(weight):
        return dot3(split(weight), (zturn[0], zturn[1]))

    def ring_send(src, dst, k):
        for a, b in sorted(FAR, key=away):
            send(src, dst.at[FAR.index((-a, -b))], k, device(a, b))

    q_own = overlaps(w)
    qbuf[...] = q_own
    ring_send(qbuf, qrecv, 3)
    for n, v in enumerate(split(jnp.concatenate([jnp.swapaxes(z, 0, 1) for z in zs], axis=0))):
        zturn[n] = v
    arrive(infos.at[pl.ds(0, 8)], 0)
    for n in range(2):
        infot[n] = jnp.swapaxes(infos[:, :, 128 * n : 128 * n + 128].reshape(128, 128), 0, 1)

    arrive(halo, 1)
    kin = kin + from_left("kin_side", halo[...])
    if nb > 1:
        arrive(pots.at[pl.ds(0, nb - 1)], 2)
    groups = []
    for g in range(4):
        group = jnp.zeros((32, 128), F32)
        for i in range(nb):
            turn = 32 * (i - g) % 128
            part = pltpu.roll(pots[i], turn, 1) if turn else pots[i]
            group = jnp.where(lane // 32 == i, part, group)
        groups.append(group)
    potential = jnp.concatenate(groups, axis=0)
    h_local = kin + potential * w
    local = jnp.concatenate(
        [
            jnp.sum(w * h_local, axis=0, keepdims=True), jnp.sum(w * w, axis=0, keepdims=True),
        ],
        axis=0,
    )
    nbuf[...] = local
    for a, b in SIDES:
        send(nbuf, nrecv.at[SIDES.index((-a, -b))], 12, device(a, b))

    arrive(qrecv, 3)
    q = gather_overlaps(q_own, qrecv)
    coef_h, coef_s = coefficients(q, 0), coefficients(q, 1)

    def total_of(v):
        return jnp.sum(v, axis=1, keepdims=True)

    of_atoms = jnp.concatenate(
        [
            jnp.sum(q * coef_h[:5], axis=0, keepdims=True), jnp.sum(q * coef_s[:5], axis=0, keepdims=True),
        ],
        axis=0,
    )
    arrive(nrecv, 12)

    near = of_atoms * (rel_y == 0).astype(F32)
    esend[1] = near * (rel_x <= 0).astype(F32) + local + nrecv[0]
    esend[0] = near * (rel_x <= 1).astype(F32) + local + nrecv[0] + nrecv[1]
    for n, (a, b) in sorted(enumerate(WINDOWS), key=lambda x: away(x[1])):
        send(esend.at[a // 6], ebuf.at[n], 4, device(-a, -b))

    both_terms = correction(jnp.concatenate([weights(coef_h), weights(coef_s)], axis=0))
    h_w = h_local + both_terms[:128]
    s_w = w + both_terms[128:]
    fields[0] = h_w
    fields[1] = s_w

    def share(first, second, mine, table, k):
        mine[...] = jnp.where(lane < 64, first, second)

        others = [(a, b) for a in range(nx) for b in range(ny) if (a, b) != (0, 0)]
        for a, b in sorted(others, key=away):
            send(mine, table.at[me], k, device(a, b))

    flat = from_right(jnp.concatenate([h_w, s_w], axis=1), "down_z")
    lower, upper = flat[:, 256:384], flat[:, 384:]
    turned = [lower, pltpu.roll(lower, 64, 1), upper, pltpu.roll(upper, 64, 1)]
    on_left = lane < 64
    two = from_left(
        "down_two",
        jnp.concatenate(
            [jnp.where(on_left, m, 0.0) for m in turned]
            + [jnp.where(on_left, 0.0, turned[n]) for n in (1, 0, 3, 2)],
            axis=0,
        ),
    )
    for t in FAR:
        at, n1, n2 = MIXED[t]
        if n1 == 0:
            far_s[at : at + n2, :] = two[BLOCKS_TWO[t][0] : BLOCKS_TWO[t][0] + n2]
            send(far_s.at[pl.ds(at, n2)], far_r.at[pl.ds(at, n2)], 7, device(*t))
    one = from_left("down_one", jnp.concatenate([flat[:, :128], flat[:, 128:256]], axis=0))
    for t in NEAR:
        at, n1, n2 = MIXED[t]
        near_s[at : at + n1, :] = one[BLOCKS_ONE[t][0] : BLOCKS_ONE[t][0] + n1]
        near_s[at + n1 : at + n1 + n2, :] = two[BLOCKS_TWO[t][0] : BLOCKS_TWO[t][0] + n2]
        send(near_s.at[pl.ds(at, n1 + n2)], near_r.at[pl.ds(at, n1 + n2)], 6, device(*t))
    for f in range(2):
        bface[f, 0:8, :] = fields[f, pl.ds(0, 8, stride=16), :]
        bface[f, 8:16, :] = fields[f, pl.ds(15, 8, stride=16), :]
    send(fields.at[:, pl.ds(0, 16)], bhalo.at[:, pl.ds(16, 16)], 5, device(-1, 0))
    send(fields.at[:, pl.ds(112, 16)], bhalo.at[:, pl.ds(0, 16)], 5, device(1, 0))
    send(bface.at[:, pl.ds(0, 8)], bhalo.at[:, pl.ds(40, 8)], 5, device(0, -1))
    send(bface.at[:, pl.ds(8, 8)], bhalo.at[:, pl.ds(32, 8)], 5, device(0, 1))

    arrive(near_s, 6)
    level1 = jnp.concatenate(
        [near_r[MIXED[t][0] : MIXED[t][0] + MIXED[t][1], :] for t in NEAR] + [one[ROWS_ONE:]], axis=0
    )
    level1_z = from_right(level1, "one_z")
    arrive(far_s, 7)
    level2 = [
        near_r[at + n1 : at + n1 + n2, :] if n1 else far_r[at : at + n2, :] for at, n1, n2 in (MIXED[t] for t in FAR)
    ]
    flat = from_right(jnp.concatenate(level2 + [two[ROWS_TWO:]], axis=0), "sweep_two_z")
    x2 = from_left("sweep_two", jnp.concatenate([flat[:, 128 * n : 128 * n + 128] for n in range(6)], axis=0))
    flat = from_right(x2, "up_one_z")
    x1 = from_left("up_one", jnp.concatenate([level1, level1_z, flat[:, :128], flat[:, 128:]], axis=0))
    arrive(ebuf, 4)
    sums = jnp.sum(ebuf[...], axis=0) + esend[0]
    energy = total_of(sums[0:1]) / total_of(sums[1:2])
    residual = h_w - energy * s_w
    resid[...] = residual
    keep(1)
    level[...] = lane * 0.0 + energy
    keep(3)
    x1 = x1 - energy * pltpu.roll(x1, 64, 1)
    flat = from_right(x1, "up_zero_z")
    arrive(bhalo, 5)
    faces = bhalo[0] - energy * bhalo[1]
    direction = from_left(
        "up_zero", jnp.concatenate([residual, flat[:, :128], flat[:, 128:], faces], axis=0)
    ) + (GAIN[0] * SIDE[0]) * from_right(residual, "zero_z")

    dirs[...] = direction
    q_own = overlaps(direction)
    qbuf2[...] = q_own
    ring_send(qbuf2, qrecv2, 9)
    for j in range(3):
        stage[48 + 8 * j : 56 + 8 * j, :] = dirs[pl.ds(j, 8, stride=16), :]
        stage[72 + 8 * j : 80 + 8 * j, :] = dirs[pl.ds(13 + j, 8, stride=16), :]
    send(dirs.at[pl.ds(0, 48)], halo2.at[pl.ds(48, 48)], 8, device(-1, 0))
    send(dirs.at[pl.ds(80, 48)], halo2.at[pl.ds(0, 48)], 8, device(1, 0))
    send(stage.at[pl.ds(48, 24)], halo2.at[pl.ds(120, 24)], 8, device(0, -1))
    send(stage.at[pl.ds(72, 24)], halo2.at[pl.ds(96, 24)], 8, device(0, 1))
    keep(0)
    change = from_left("kin_own", direction) + from_right(direction, "kin_z")
    change = change + (potential - energy) * direction
    arrive(halo2, 8)
    change = change + from_left("kin_side", halo2[...])
    arrive(qrecv2, 9)
    q = gather_overlaps(q_own, qrecv2)
    change = change + correction(weights(coefficients(q, 0) - energy * coefficients(q, 1)))
    along = jnp.sum(residual * change, axis=0, keepdims=True)
    square = jnp.sum(change * change, axis=0, keepdims=True)
    along = along + pltpu.roll(along, 64, 1)
    square = square + pltpu.roll(square, 64, 1)
    share(along, square, lsend, lbuf, 10)
    changes[...] = change
    keep(2)
    keep(4)

    left(infos.at[pl.ds(0, 8)], 0)
    left(halo, 1)
    if nb > 1:
        left(pots.at[pl.ds(0, nb - 1)], 2)
    left(qrecv, 3)
    left(ebuf, 4)
    left(geos.at[pl.ds(0, 8)], 11)
    left(nrecv, 12)
    left(bhalo, 5)
    left(near_s, 6)
    left(far_s, 7)
    left(halo2, 8)
    left(qrecv2, 9)
    left(lbuf.at[pl.ds(0, nx * ny - 1)], 10)

    arrive(lbuf.at[pl.ds(0, nx * ny - 1)], 10)
    for n in range(5):
        kept(n).wait()


def finish(w_ref, dirs_ref, resid_ref, change_ref, level_ref, sums_ref, bands_ref, new_ref, energy_ref):
    sums = jnp.sum(sums_ref[...], axis=0)
    first = lax.broadcasted_iota(jnp.int32, (1, 128), 1) < 64
    along = jnp.sum(jnp.where(first, sums, 0.0), axis=1, keepdims=True)
    square = jnp.sum(jnp.where(first, 0.0, sums), axis=1, keepdims=True)
    step = -along / square
    bands_ref[...] = w_ref[...] + step * dirs_ref[...]
    new_ref[...] = resid_ref[...] + step * change_ref[...]
    energy_ref[0] = level_ref[0, 0]


def solution(mesh):
    shape = tuple(mesh.shape[name] for name in ("band", "dx", "dy"))
    nb, nx, ny = shape
    table, packed_constants = packed()

    def on_device(wave_bands, potential, atom_offsets, proj_counts, dh_matrix, ds_matrix):
        vmem = pl.BlockSpec(memory_space=pltpu.VMEM)
        smem = pl.BlockSpec(memory_space=pltpu.SMEM)
        v = lambda *dims: pltpu.VMEM(dims, F32)
        hbm = pl.BlockSpec(memory_space=pltpu.HBM)
        grid = jax.ShapeDtypeStruct((128, 128), F32)
        parts = pl.pallas_call(
            functools.partial(kernel, shape, table),
            out_shape=(
                grid, grid, grid, jax.ShapeDtypeStruct((1, 128), F32), jax.ShapeDtypeStruct((nx * ny, 1, 128), F32),
            ),
            in_specs=[hbm] * 7,
            out_specs=(hbm,) * 5,
            scratch_shapes=[
                v(128, 128),
                v(128, 32),
                pltpu.SMEM((1, 3, 1, ATOMS), jnp.int32),
                pltpu.SMEM((1, 1, ATOMS), jnp.int32),
                v(2, 9, ATOMS, 9),
                pltpu.VMEM(packed_constants.shape, BF16),
                v(96, 128),
                v(144, 128),
                v(144, 128),
                v(128, 128),
                v(128, 128),
                v(128, 128),
                v(1, 128),
                v(16, 1, 128),
                v(8, 256),
                v(16, 8, 256),
                v(2, 128, 128),
                v(nb, 32, 128),
                v(5, 128),
                v(14, 5, 128),
                v(5, 128),
                v(14, 5, 128),
                v(2, 128, 128),
                v(2, 16, 128),
                v(2, 48, 128),
                v(ROWS_NEAR, 128),
                v(ROWS_NEAR, 128),
                v(ROWS_FAR, 128),
                v(ROWS_FAR, 128),
                v(2, 2, 128),
                v(23, 2, 128),
                v(2, 128),
                v(2, 2, 128),
                v(1, 128),
                v(1, 128),
                pltpu.VMEM((2, 128, 512), BF16),
                pltpu.VMEM((2, 512, 128), BF16),
                v(5, 128, 128),
                pltpu.SemaphoreType.DMA((7,)),
                pltpu.SemaphoreType.DMA((13,)),
                pltpu.SemaphoreType.DMA((13,)),
                pltpu.SemaphoreType.DMA((5,)),
            ],
            compiler_params=pltpu.CompilerParams(
                collective_id=0, has_side_effects=True, vmem_limit_bytes=60 << 20
            ),
        )(
            wave_bands.reshape(128, 128),
            potential.reshape(128, 32),
            jnp.transpose(atom_offsets, (0, 3, 1, 2)),
            proj_counts,
            jnp.transpose(dh_matrix, (0, 1, 3, 2, 4)).reshape(9, ATOMS, 9),
            jnp.transpose(ds_matrix, (0, 1, 3, 2, 4)).reshape(9, ATOMS, 9),
            jnp.asarray(packed_constants),
        )
        bands, resid, energy = pl.pallas_call(
            finish,
            out_shape=(grid, grid, jax.ShapeDtypeStruct((1,), F32)),
            in_specs=[vmem] * 4 + [smem, vmem],
            out_specs=(vmem, vmem, smem),
            compiler_params=pltpu.CompilerParams(vmem_limit_bytes=60 << 20),
        )(wave_bands.reshape(128, 128), *parts)
        return bands.reshape(1, CX, CY, NZ), resid.reshape(1, CX, CY, NZ), energy

    return jax.shard_map(
        on_device,
        mesh=mesh,
        in_specs=(
            P("band", "dx", "dy", None),
            P("dx", "dy", "band"),
            P("dx", "dy", None, None),
            P("dx", "dy", None),
            P("dx", "dy", None, None, None),
            P("dx", "dy", None, None, None),
        ),
        out_specs=(P("band", "dx", "dy", None), P("band", "dx", "dy", None), P("band")),
        check_vma=False,
    )
```

```python
import functools

import jax
import jax.numpy as jnp
import numpy as np
from jax import lax
from jax.experimental import pallas as pl
from jax.experimental.pallas import tpu as pltpu
from jax.sharding import PartitionSpec as P

MESH = pl.DeviceIdType.MESH
F32 = jnp.float32
BF16 = jnp.bfloat16

STENCIL = (-49.0 / 18.0, 1.5, -0.15, 1.0 / 90.0)
RELAXATION = 2.0 / 3.0
MASS_SHIFT = 0.25
AMPLITUDE = 0.15
D_NORM = 0.28867513
CX, CY, NZ = 8, 16, 128
ATOMS = 4

DIAG = [3.0 / 4.0**level + MASS_SHIFT for level in range(3)]
GAIN = [RELAXATION / d for d in DIAG]
SIDE = [0.5 * GAIN[level] / 4.0**level for level in range(3)]


def pad8(n):
    return (n + 7) // 8 * 8


def cells(x0, x1, y0, y1):
    return [(i, j) for i in range(x0, x1) for j in range(y0, y1)]


def cross(out, inp):
    where = {c: n for n, c in enumerate(inp)}
    m = np.zeros((len(out), len(inp)))
    for row, (i, j) in enumerate(out):
        for c in ((i - 1, j), (i + 1, j), (i, j - 1), (i, j + 1)):
            if c in where:
                m[row, where[c]] = 1.0
    return m


def pick(out, inp):
    where = {c: n for n, c in enumerate(inp)}
    m = np.zeros((len(out), len(inp)))
    for row, c in enumerate(out):
        if c in where:
            m[row, where[c]] = 1.0
    return m


def average(out, inp):
    where = {c: n for n, c in enumerate(inp)}
    m = np.zeros((len(out), len(inp)))
    for row, (i, j) in enumerate(out):
        for c in cells(2 * i, 2 * i + 2, 2 * j, 2 * j + 2):
            if c in where:
                m[row, where[c]] = 0.25
    return m


def spread_to(out, inp):
    where = {c: n for n, c in enumerate(inp)}
    m = np.zeros((len(out), len(inp)))
    for row, (i, j) in enumerate(out):
        m[row, where[(i // 2, j // 2)]] = 1.0
    return m


def along_z(n):
    return np.eye(n, k=1) + np.eye(n, k=-1)


def halve_z(n):
    return np.repeat(np.eye(n // 2), 2, axis=0) * 0.5


def double_z(n):
    return np.repeat(np.eye(n), 2, axis=1)


def both(m):
    z = np.zeros_like(m)
    return np.block([[m, z], [z, m]])


def grown(m, rows, cols):
    out = np.zeros((rows, cols))
    out[: m.shape[0], : m.shape[1]] = m
    return out


FINE = cells(0, CX, 0, CY)
ONE = cells(-1, 5, -1, 9)
ONE_WIDE = cells(-2, 6, -2, 10)
TWO = cells(-1, 3, -1, 5)
TWO_WIDE = cells(-3, 5, -3, 7)

NEAR = [(a, b) for a in (-1, 0, 1) for b in (-1, 0, 1) if (a, b) != (0, 0)]
FAR = [(a, b) for a in (-2, -1, 0, 1, 2) for b in (-1, 0, 1) if (a, b) != (0, 0)]
GREET = [(-1, -2), (1, -2), (-1, -1), (-1, 1), (1, -1), (1, 1), (-1, 0), (1, 0), (0, -1), (0, 1)]
WINDOWS = [(a, b) for a in (0, 3, 6) for b in range(8) if (a, b) != (0, 0)]
SIDES = [(-1, 0), (1, 0)]


def away(tile):
    return -(2 * min(tile[0] % 8, -tile[0] % 8) + min(tile[1] % 8, -tile[1] % 8))


def within(among, of, reach):
    return [c for c in among if min(abs(c[0] - d[0]) + abs(c[1] - d[1]) for d in of) <= reach]


ONE_USED = [c for c in ONE if not (c[0] in (-1, 4) and c[1] in (-1, 8))]


def blocks(own, wide, step, targets, halves):
    wide = set(wide)
    table, at = {}, 0
    for t in targets:
        block = [c for c in own if (c[0] - step[0] * t[0], c[1] - step[1] * t[1]) in wide]
        rows = pad8((len(block) + halves - 1) // halves)
        table[t] = (at, rows, block)
        at += rows
    return table, at


BLOCKS_ONE, ROWS_ONE = blocks(ONE_USED, within(ONE_WIDE, ONE_USED, 1), (4, 8), NEAR, 1)
BLOCKS_TWO, ROWS_TWO = blocks(TWO, within(TWO_WIDE, TWO, 2), (2, 4), FAR, 2)
MIXED, ROWS_NEAR, ROWS_FAR = {}, 0, 0
for tile in FAR:
    rows_one = BLOCKS_ONE[tile][1] if tile in BLOCKS_ONE else 0
    rows_two = BLOCKS_TWO[tile][1]
    if rows_one:
        MIXED[tile] = (ROWS_NEAR, rows_one, rows_two)
        ROWS_NEAR += rows_one + rows_two
    else:
        MIXED[tile] = (ROWS_FAR, 0, rows_two)
        ROWS_FAR += rows_two
OWN_ONE = pad8(len(ONE))
OWN_TWO = 32
STACK_ONE = ROWS_ONE + OWN_ONE
STACK_TWO = ROWS_TWO + OWN_TWO


def senders(table, rows, own, own_rows, half=0):
    m = np.zeros((rows + own_rows, len(own)))
    for at, n, block in table.values():
        part = block[half * n : half * n + n]
        m[at : at + len(part)] = pick(part, own)
    if half == 0:
        m[rows : rows + len(own)] = np.eye(len(own))
    return m


def receivers(table, rows, own, own_rows, wide, step, half=0):
    m = np.zeros((len(wide), rows + own_rows))
    for t, (at, n, block) in table.items():
        here = [(i - step[0] * t[0], j - step[1] * t[1]) for i, j in block[half * n : half * n + n]]
        m[:, at : at + len(here)] = pick(wide, here)
    if half == 0:
        m[:, rows : rows + len(own)] = pick(wide, own)
    return m


def constants():
    c = {}
    stack = {}
    kin_own = np.zeros((128, 128))
    kin_side = np.zeros((128, 144))
    kin_z = np.zeros((NZ, NZ))
    halo = (
        cells(-3, 0, 0, CY)
        + cells(8, 11, 0, CY)
        + [(x, y) for y in range(-3, 0) for x in range(CX)]
        + [(x, y) for y in range(16, 19) for x in range(CX)]
    )
    where_own = {cell: n for n, cell in enumerate(FINE)}
    where_halo = {cell: n for n, cell in enumerate(halo)}
    for row, (x, y) in enumerate(FINE):
        kin_own[row, row] = -1.5 * STENCIL[0]
        for reach in (1, 2, 3):
            for cell in ((x - reach, y), (x + reach, y), (x, y - reach), (x, y + reach)):
                if cell in where_own:
                    kin_own[row, where_own[cell]] += -0.5 * STENCIL[reach]
                else:
                    kin_side[row, where_halo[cell]] += -0.5 * STENCIL[reach]
    for reach in (1, 2, 3):
        kin_z += -0.5 * STENCIL[reach] * (np.eye(NZ, k=reach) + np.eye(NZ, k=-reach))
    c["kin_own"], c["kin_side"], c["kin_z"] = kin_own, kin_side, kin_z

    ring0 = cells(-2, 10, -2, 18)
    avg = average(ONE, ring0)
    one_plane = avg @ (pick(ring0, FINE) / 3.0 + SIDE[0] * cross(ring0, FINE))
    one_along = avg @ pick(ring0, FINE) * SIDE[0]
    send = senders(BLOCKS_ONE, ROWS_ONE, ONE, OWN_ONE)
    c["down_one"] = np.concatenate([send @ one_plane, send @ one_along], axis=1)

    ring1 = cells(-2, 6, -2, 10)
    avg = average(TWO, ring1)
    two_plane = avg @ (pick(ring1, ONE) / 3.0 + SIDE[1] * cross(ring1, ONE))
    two_along = avg @ pick(ring1, ONE) * SIDE[1]
    sends = [senders(BLOCKS_TWO, ROWS_TWO, TWO, OWN_TWO, half) for half in (0, 1)]
    c["down_two"] = np.concatenate(
        [send @ two @ one for send in sends for two in (two_plane, two_along) for one in (one_plane, one_along)], axis=1
    )
    h0, n0, h1, n1 = halve_z(NZ), along_z(NZ), halve_z(64), along_z(64)
    c["down_z"] = np.concatenate(
        [both(m) for m in (h0, n0 @ h0, h0 @ h1, n0 @ h0 @ h1, h0 @ n1 @ h1, n0 @ h0 @ n1 @ h1)], axis=1
    )

    takes = [receivers(BLOCKS_TWO, ROWS_TWO, TWO, OWN_TWO, TWO_WIDE, (2, 4), half) for half in (0, 1)]
    mid = cells(-2, 4, -2, 6)
    n1 = cross(TWO, TWO_WIDE)
    n2 = cross(TWO, mid) @ cross(mid, TWO_WIDE)
    here = pick(TWO, TWO_WIDE)
    g, k = GAIN[2], SIDE[2]
    terms = [
        g * (13.0 / 9.0 * here + 5.0 / 3.0 * k * n1 + k * k * n2),
        g * (5.0 / 3.0 * k * here + 2.0 * k * k * n1),
        g * k * k * here,
    ]
    c["sweep_two"] = np.concatenate([t @ take for take in takes for t in terms], axis=1)
    nz = along_z(32)
    places = [grown(both(m), 64, 128) for m in (np.eye(32), nz, nz @ nz)]
    blank = np.zeros((64, 128))
    c["sweep_two_z"] = np.concatenate(
        [np.concatenate([m, blank]) for m in places] + [np.concatenate([blank, m]) for m in places], axis=1
    )

    take = receivers(BLOCKS_ONE, ROWS_ONE, ONE, OWN_ONE, ONE_WIDE, (4, 8))
    g, k = GAIN[1], SIDE[1]
    here, n1 = pick(ONE, ONE_WIDE), cross(ONE, ONE_WIDE)
    up = spread_to(ONE_WIDE, TWO)
    c["up_one"] = grown(
        np.concatenate(
            [
                g * (4.0 / 3.0 * here + k * n1) @ take,
                g * k * here @ take,
                grown((here / 3.0 + k * n1) @ up, len(ONE), OWN_TWO),
                grown(k * here @ up, len(ONE), OWN_TWO),
            ],
            axis=1,
        ),
        OWN_ONE,
        2 * STACK_ONE + 2 * OWN_TWO,
    )
    nz = along_z(64)
    c["one_z"] = both(nz)
    double = double_z(32)
    c["up_one_z"] = np.concatenate(
        [grown(both(double), 128, 128), grown(both(double @ nz), 128, 128)], axis=1
    )

    g, k = GAIN[0], SIDE[0]
    ring0 = cells(-1, 9, -1, 17)
    here, n1 = pick(FINE, ring0), cross(FINE, ring0)
    up = spread_to(ring0, ONE)
    faces = (
        cells(-1, 0, 0, CY) + cells(8, 9, 0, CY) + [(x, -1) for x in range(CX)] + [(x, 16) for x in range(CX)]
    )
    c["up_zero"] = np.concatenate(
        [
            g * (4.0 / 3.0 * np.eye(128) + k * cross(FINE, FINE)),
            grown((here / 3.0 + k * n1) @ up, 128, OWN_ONE),
            grown(k * here @ up, 128, OWN_ONE),
            g * k * cross(FINE, faces),
        ],
        axis=1,
    )
    nz = along_z(NZ)
    double = double_z(64)
    c["zero_z"] = nz
    c["up_zero_z"] = np.concatenate([grown(double, 128, 128), grown(double @ nz, 128, 128)], axis=1)
    return c


def packed():
    table, parts, at = {}, [], 0
    for name, m in constants().items():
        rows, cols = m.shape
        rows = (rows + 15) // 16 * 16
        m = grown(m, rows, (cols + 127) // 128 * 128).astype(np.float32)
        high = m.astype(jnp.bfloat16)
        low = (m - high.astype(np.float32)).astype(jnp.bfloat16)
        exact = not low.astype(np.float32).any()
        places = []
        for part in (high,) if exact else (high, low):
            tiles = [part[:, t : t + 128] for t in range(0, m.shape[1], 128)]
            places.append([at + n * rows for n in range(len(tiles))])
            at += rows * len(tiles)
            parts += tiles
        table[name] = (rows, cols, places)
    return table, np.concatenate(parts, axis=0)


def dot(a, b):
    return lax.dot_general(a, b, (((1,), (0,)), ((), ())), preferred_element_type=F32)


def split(x):
    high = x.astype(BF16)
    return high, (x - high.astype(F32)).astype(BF16)


def dot3(a, b):
    return dot(a[0], b[0]) + dot(a[1], b[0]) + dot(a[0], b[1])


def projector_of(p, right):
    left_of = jnp.where(p < 3, p, jnp.where(p == 3, 4, jnp.where(p == 4, 7, 99)))
    right_of = jnp.where(p == 0, 3, jnp.where(p < 3, p + 4, jnp.where(p < 5, 8, 99)))
    return jnp.where(right, right_of, left_of)


def kernel(shape, table, *refs):
    nb, nx, ny = shape
    (
        w_in, pot_in, offs_in, cnt_in, dh_in, ds_in, const_in,
        dirs_out, resid_out, change_out, energy_out, lbuf,
        w_ref, pot_ref, offs_ref, cnt_ref, d_ref, const,
        stage, halo, halo2, dirs, resid, changes, geo, geos, info, infos, infot, pots, qbuf, qrecv, qbuf2, qrecv2,
        fields, bface, bhalo, near_s, near_r, far_s, far_r, esend, ebuf, nbuf, nrecv, lsend, level, zfun, zturn, wfun,
        lsem, ssem, rsem, osem,
    ) = refs
    loads = [
        pltpu.make_async_copy(src, dst, lsem.at[n])
        for n, (src, dst) in enumerate(
            (
                (offs_in, offs_ref), (cnt_in, cnt_ref), (dh_in, d_ref.at[0]), (ds_in, d_ref.at[1]),
                (w_in, w_ref), (pot_in, pot_ref), (const_in, const),
            )
        )
    ]
    for n in (0, 1, 4):
        loads[n].start()

    def held(name):
        rows, cols, places = table[name]
        return [jnp.concatenate([const[at : at + rows, :] for at in tiles], axis=1)[:, :cols] for tiles in places]

    def from_left(name, x):
        c, (high, low) = held(name), split(x)
        total = dot(c[0], high) + dot(c[0], low)
        return total + dot(c[1], high) if len(c) > 1 else total

    def from_right(x, name):
        c, (high, low) = held(name), split(x)
        total = dot(high, c[0]) + dot(low, c[0])
        return total + dot(high, c[1]) if len(c) > 1 else total

    ib, ix, iy = lax.axis_index("band"), lax.axis_index("dx"), lax.axis_index("dy")

    def device(a, b, band=0):
        return (lax.rem(ib + band + nb, nb), lax.rem(ix + a + nx, nx), lax.rem(iy + b + ny, ny))

    def send(src, dst, k, where):
        pltpu.make_async_remote_copy(
            src_ref=src, dst_ref=dst, send_sem=ssem.at[k], recv_sem=rsem.at[k], device_id=where, device_id_type=MESH
        ).start()

    def arrive(ref, k):
        pltpu.make_async_copy(ref, ref, rsem.at[k]).wait()

    def left(ref, k):
        pltpu.make_async_copy(ref, ref, ssem.at[k]).wait()

    me = ix * ny + iy
    slot = lax.rem(ix, 4) * 4 + lax.rem(iy, 4)

    def kept(n):
        src, dst = ((dirs, dirs_out), (resid, resid_out), (changes, change_out), (level, energy_out), (lsend, lbuf.at[me]))[n]
        return pltpu.make_async_copy(src, dst, osem.at[n])

    def keep(n):
        kept(n).start()

    infos[...] = jnp.zeros_like(infos)
    geos[...] = jnp.zeros_like(geos)
    barrier = pltpu.get_barrier_semaphore()

    for i in range(1, nb):
        pl.semaphore_signal(barrier, inc=1, device_id=device(0, 0, i), device_id_type=MESH)
    for a, b in GREET:
        pl.semaphore_signal(barrier, inc=1, device_id=device(a, b), device_id_type=MESH)
    for n in (5, 2, 3, 6):
        loads[n].start()

    lane = lax.broadcasted_iota(jnp.int32, (1, 128), 1)
    lane8 = lax.broadcasted_iota(jnp.int32, (8, 128), 1)
    row8 = lax.broadcasted_iota(jnp.int32, (8, 128), 0)
    loads[0].wait()
    loads[1].wait()
    centres = jnp.zeros((1, 128), F32)
    for k in range(ATOMS):
        for m, v in enumerate((offs_ref[0, 0, 0, k], offs_ref[0, 1, 0, k], offs_ref[0, 2, 0, k], cnt_ref[0, 0, k])):
            centres = jnp.where(lane == 4 * m + k, v.astype(F32), centres)
    geo[...] = centres
    geos[slot] = centres
    loads[4].wait()
    for j in range(3):
        stage[8 * j : 8 * j + 8, :] = w_ref[pl.ds(j, 8, stride=16), :]
        stage[24 + 8 * j : 32 + 8 * j, :] = w_ref[pl.ds(13 + j, 8, stride=16), :]

    pl.semaphore_wait(barrier, len(GREET) + nb - 1)

    for a, b in NEAR:
        send(geo, geos.at[slot], 11, device(a, b))
    send(w_ref.at[pl.ds(0, 48)], halo.at[pl.ds(48, 48)], 1, device(-1, 0))
    send(w_ref.at[pl.ds(80, 48)], halo.at[pl.ds(0, 48)], 1, device(1, 0))
    send(stage.at[pl.ds(0, 24)], halo.at[pl.ds(120, 24)], 1, device(0, -1))
    send(stage.at[pl.ds(24, 24)], halo.at[pl.ds(96, 24)], 1, device(0, 1))
    for load in (loads[2], loads[3], loads[5]):
        load.wait()
    packed_pot = jnp.zeros((32, 128), F32)
    for g in range(4):
        place = (
            lax.broadcasted_iota(jnp.int32, (32, 128), 0) + 32 * g == lax.broadcasted_iota(jnp.int32, (32, 128), 1)
        ).astype(BF16)
        part = pot_ref[32 * g : 32 * g + 32, :]
        high, low = split(part)
        rest = part - high.astype(F32) - low.astype(F32)
        packed_pot = packed_pot + dot(high, place) + dot(low, place) + dot(rest.astype(BF16), place)
    pots[ib] = packed_pot
    for i in range(1, nb):
        send(pots.at[ib], pots.at[ib], 2, device(0, 0, i))
    crossed, p_from, p_to = lane // 40, (lane // 8) % 5, lane % 8
    for right in (0, 1):
        j_of = projector_of(p_from, (crossed != right))
        i_of = projector_of(p_to, lane * 0 + right == 1)
        chosen = [((i_of == i) & (lane < 80)).astype(F32) for i in range(9)]
        from_j = [(j_of == j).astype(F32) for j in range(9)]
        for n in range(2):
            rows = jnp.zeros((ATOMS, 128), F32)
            for i in range(9):
                of_i = d_ref[n, i]
                full = of_i[:, 0:1] * from_j[0]
                for j in range(1, 9):
                    full = full + of_i[:, j : j + 1] * from_j[j]
                rows = rows + full * chosen[i]
            info[4 * right : 4 * right + 4, 128 * n : 128 * n + 128] = rows
    infos[slot] = info[...]
    for a, b in NEAR:
        send(info, infos.at[slot], 0, device(a, b))
    w = w_ref[...]
    loads[6].wait()
    kin = from_left("kin_own", w) + from_right(w, "kin_z")

    arrive(geos.at[pl.ds(0, 8)], 11)
    chosen = ((lax.rem(lane8, 4) == lax.rem(row8, 4)) & (lane8 < 16)).astype(F32)
    turned = jnp.swapaxes((geos[...] * chosen[None]).reshape(128, 128), 0, 1)
    centres = [jnp.sum(turned[4 * m : 4 * m + 4], axis=0, keepdims=True) for m in range(4)]
    slot_x, slot_y = lane // 32, (lane // 8) % 4
    right_lane = (lane // 4) % 2 == 1
    rel_x = lax.rem(slot_x - ix + 1 + 16, 4) - 1
    rel_y = lax.rem(slot_y - iy + 1 + 16, 4) - 1
    centre_x = centres[0] + (rel_x * CX).astype(F32)
    centre_y = centres[1] + (rel_y * CY).astype(F32)
    centre_z = centres[2]
    count = centres[3]
    active = (projector_of(row8, jnp.broadcast_to(right_lane, (8, 128))).astype(F32) < count).astype(F32)

    def bells(n, centre):
        r = lax.broadcasted_iota(jnp.int32, (n, 128), 0).astype(F32) - centre
        inside = ((r > -6.5) & (r < 5.5)).astype(F32)
        q = r * r
        return r, q, [inside * jnp.exp(q * (-1.0 / s)) for s in (8.0, 9.68, 11.52)]

    rz, qz, (zs, zp, zd) = bells(NZ, centre_z)
    zp, zd = zp * (1.0 / 2.2), zd * (1.0 / 5.76)
    zs = (
        jnp.where(right_lane, rz * zp, zs), jnp.where(right_lane, rz * zd, zp), jnp.where(right_lane, qz * zd, zd), zd,
    )
    for n, v in enumerate(split(jnp.concatenate(zs, axis=1))):
        zfun[n] = v
    rx, qx, (xs, xp, xd) = bells(CX, centre_x)
    ry, qy, (ys, yp, yd) = bells(CY, centre_y)
    pairs = (
        (jnp.where(right_lane, xp, xs), jnp.where(right_lane, yp, ys)),
        (jnp.where(right_lane, xd, rx * xp), jnp.where(right_lane, ry * yd, yp)),
        (jnp.where(right_lane, rx * xd, xp), jnp.where(right_lane, yd, ry * yp)),
        (jnp.where(right_lane, xd, rx * xd), jnp.where(right_lane, (2.0 * D_NORM) * yd, ry * yd)),
    )
    for p, (fx, fy) in enumerate(pairs):
        wfun[p] = ((AMPLITUDE * fx)[:, None, :] * fy[None, :, :]).reshape(128, 128)
    on_x = jnp.where(right_lane, -D_NORM, 0.5) * AMPLITUDE
    on_y = jnp.where(right_lane, -D_NORM, -0.5) * AMPLITUDE
    wfun[4] = (
        (on_x * qx * xd)[:, None, :] * yd[None, :, :] + xd[:, None, :] * (on_y * qy * yd)[None, :, :]
    ).reshape(128, 128)
    tile_of = (0, 1, 1, 2, 3)

    def overlaps(field):
        part = dot3(split(field), (zfun[0], zfun[1]))
        rows = [
            jnp.sum(part[:, 128 * tile_of[p] : 128 * tile_of[p] + 128] * wfun[p], axis=0, keepdims=True) for p in range(5)
        ]
        return jnp.concatenate(rows, axis=0)

    keep_x = {-2: (rel_x == -1).astype(F32), 2: (rel_x == 1).astype(F32)}

    def gather_overlaps(own, ref):
        total = None
        for a in range(-2, 3):
            line = None
            for b in (-1, 0, 1):
                v = own if (a, b) == (0, 0) else ref[FAR.index((a, b))]
                line = v if line is None else line + v
            line = line * keep_x[a] if a in keep_x else line
            total = line if total is None else total + line
        return total * active[:5]

    def coefficients(q, n):
        swapped = jnp.where(right_lane, pltpu.roll(q, 4, 1), pltpu.roll(q, 124, 1))
        total = None
        for c, v in enumerate((q, swapped)):
            for p in range(5):
                at = (c * 5 + p) * 8
                term = infot[n, at : at + 8, :] * v[p : p + 1, :]
                total = term if total is None else total + term
        return total * active

    def weights(coefs):
        tiles = [None] * 4
        for p in range(5):
            term = wfun[p] * coefs[p : p + 1, :]
            t = tile_of[p]
            tiles[t] = term if tiles[t] is None else tiles[t] + term
        return jnp.concatenate(tiles, axis=1)

    def correction(weight):
        return dot3(split(weight), (zturn[0], zturn[1]))

    def ring_send(src, dst, k):
        for a, b in sorted(FAR, key=away):
            send(src, dst.at[FAR.index((-a, -b))], k, device(a, b))

    q_own = overlaps(w)
    qbuf[...] = q_own
    ring_send(qbuf, qrecv, 3)
    for n, v in enumerate(split(jnp.concatenate([jnp.swapaxes(z, 0, 1) for z in zs], axis=0))):
        zturn[n] = v
    arrive(infos.at[pl.ds(0, 8)], 0)
    for n in range(2):
        infot[n] = jnp.swapaxes(infos[:, :, 128 * n : 128 * n + 128].reshape(128, 128), 0, 1)

    arrive(halo, 1)
    kin = kin + from_left("kin_side", halo[...])
    if nb > 1:
        arrive(pots.at[pl.ds(0, nb - 1)], 2)
    groups = []
    for g in range(4):
        group = jnp.zeros((32, 128), F32)
        for i in range(nb):
            turn = 32 * (i - g) % 128
            part = pltpu.roll(pots[i], turn, 1) if turn else pots[i]
            group = jnp.where(lane // 32 == i, part, group)
        groups.append(group)
    potential = jnp.concatenate(groups, axis=0)
    h_local = kin + potential * w
    local = jnp.concatenate(
        [
            jnp.sum(w * h_local, axis=0, keepdims=True), jnp.sum(w * w, axis=0, keepdims=True),
        ],
        axis=0,
    )
    nbuf[...] = local
    for a, b in SIDES:
        send(nbuf, nrecv.at[SIDES.index((-a, -b))], 12, device(a, b))

    arrive(qrecv, 3)
    q = gather_overlaps(q_own, qrecv)
    coef_h, coef_s = coefficients(q, 0), coefficients(q, 1)

    def total_of(v):
        return jnp.sum(v, axis=1, keepdims=True)

    of_atoms = jnp.concatenate(
        [
            jnp.sum(q * coef_h[:5], axis=0, keepdims=True), jnp.sum(q * coef_s[:5], axis=0, keepdims=True),
        ],
        axis=0,
    )
    arrive(nrecv, 12)

    near = of_atoms * (rel_y == 0).astype(F32)
    esend[1] = near * (rel_x <= 0).astype(F32) + local + nrecv[0]
    esend[0] = near * (rel_x <= 1).astype(F32) + local + nrecv[0] + nrecv[1]
    for n, (a, b) in sorted(enumerate(WINDOWS), key=lambda x: away(x[1])):
        send(esend.at[a // 6], ebuf.at[n], 4, device(-a, -b))

    both_terms = correction(jnp.concatenate([weights(coef_h), weights(coef_s)], axis=0))
    h_w = h_local + both_terms[:128]
    s_w = w + both_terms[128:]
    fields[0] = h_w
    fields[1] = s_w

    def share(first, second, mine, table, k):
        mine[...] = jnp.where(lane < 64, first, second)

        others = [(a, b) for a in range(nx) for b in range(ny) if (a, b) != (0, 0)]
        for a, b in sorted(others, key=away):
            send(mine, table.at[me], k, device(a, b))

    flat = from_right(jnp.concatenate([h_w, s_w], axis=1), "down_z")
    lower, upper = flat[:, 256:384], flat[:, 384:]
    turned = [lower, pltpu.roll(lower, 64, 1), upper, pltpu.roll(upper, 64, 1)]
    on_left = lane < 64
    two = from_left(
        "down_two",
        jnp.concatenate(
            [jnp.where(on_left, m, 0.0) for m in turned]
            + [jnp.where(on_left, 0.0, turned[n]) for n in (1, 0, 3, 2)],
            axis=0,
        ),
    )
    for t in FAR:
        at, n1, n2 = MIXED[t]
        if n1 == 0:
            far_s[at : at + n2, :] = two[BLOCKS_TWO[t][0] : BLOCKS_TWO[t][0] + n2]
            send(far_s.at[pl.ds(at, n2)], far_r.at[pl.ds(at, n2)], 7, device(*t))
    one = from_left("down_one", jnp.concatenate([flat[:, :128], flat[:, 128:256]], axis=0))
    for t in NEAR:
        at, n1, n2 = MIXED[t]
        near_s[at : at + n1, :] = one[BLOCKS_ONE[t][0] : BLOCKS_ONE[t][0] + n1]
        near_s[at + n1 : at + n1 + n2, :] = two[BLOCKS_TWO[t][0] : BLOCKS_TWO[t][0] + n2]
        send(near_s.at[pl.ds(at, n1 + n2)], near_r.at[pl.ds(at, n1 + n2)], 6, device(*t))
    for f in range(2):
        bface[f, 0:8, :] = fields[f, pl.ds(0, 8, stride=16), :]
        bface[f, 8:16, :] = fields[f, pl.ds(15, 8, stride=16), :]
    send(fields.at[:, pl.ds(0, 16)], bhalo.at[:, pl.ds(16, 16)], 5, device(-1, 0))
    send(fields.at[:, pl.ds(112, 16)], bhalo.at[:, pl.ds(0, 16)], 5, device(1, 0))
    send(bface.at[:, pl.ds(0, 8)], bhalo.at[:, pl.ds(40, 8)], 5, device(0, -1))
    send(bface.at[:, pl.ds(8, 8)], bhalo.at[:, pl.ds(32, 8)], 5, device(0, 1))

    arrive(near_s, 6)
    level1 = jnp.concatenate(
        [near_r[MIXED[t][0] : MIXED[t][0] + MIXED[t][1], :] for t in NEAR] + [one[ROWS_ONE:]], axis=0
    )
    level1_z = from_right(level1, "one_z")
    arrive(far_s, 7)
    level2 = [
        near_r[at + n1 : at + n1 + n2, :] if n1 else far_r[at : at + n2, :] for at, n1, n2 in (MIXED[t] for t in FAR)
    ]
    flat = from_right(jnp.concatenate(level2 + [two[ROWS_TWO:]], axis=0), "sweep_two_z")
    x2 = from_left("sweep_two", jnp.concatenate([flat[:, 128 * n : 128 * n + 128] for n in range(6)], axis=0))
    flat = from_right(x2, "up_one_z")
    x1 = from_left("up_one", jnp.concatenate([level1, level1_z, flat[:, :128], flat[:, 128:]], axis=0))
    arrive(ebuf, 4)
    sums = jnp.sum(ebuf[...], axis=0) + esend[0]
    energy = total_of(sums[0:1]) / total_of(sums[1:2])
    residual = h_w - energy * s_w
    resid[...] = residual
    keep(1)
    level[...] = lane * 0.0 + energy
    keep(3)
    x1 = x1 - energy * pltpu.roll(x1, 64, 1)
    flat = from_right(x1, "up_zero_z")
    arrive(bhalo, 5)
    faces = bhalo[0] - energy * bhalo[1]
    direction = from_left(
        "up_zero", jnp.concatenate([residual, flat[:, :128], flat[:, 128:], faces], axis=0)
    ) + (GAIN[0] * SIDE[0]) * from_right(residual, "zero_z")

    dirs[...] = direction
    q_own = overlaps(direction)
    qbuf2[...] = q_own
    ring_send(qbuf2, qrecv2, 9)
    for j in range(3):
        stage[48 + 8 * j : 56 + 8 * j, :] = dirs[pl.ds(j, 8, stride=16), :]
        stage[72 + 8 * j : 80 + 8 * j, :] = dirs[pl.ds(13 + j, 8, stride=16), :]
    send(dirs.at[pl.ds(0, 48)], halo2.at[pl.ds(48, 48)], 8, device(-1, 0))
    send(dirs.at[pl.ds(80, 48)], halo2.at[pl.ds(0, 48)], 8, device(1, 0))
    send(stage.at[pl.ds(48, 24)], halo2.at[pl.ds(120, 24)], 8, device(0, -1))
    send(stage.at[pl.ds(72, 24)], halo2.at[pl.ds(96, 24)], 8, device(0, 1))
    keep(0)
    change = from_left("kin_own", direction) + from_right(direction, "kin_z")
    change = change + (potential - energy) * direction
    arrive(halo2, 8)
    change = change + from_left("kin_side", halo2[...])
    arrive(qrecv2, 9)
    q = gather_overlaps(q_own, qrecv2)
    change = change + correction(weights(coefficients(q, 0) - energy * coefficients(q, 1)))
    along = jnp.sum(residual * change, axis=0, keepdims=True)
    square = jnp.sum(change * change, axis=0, keepdims=True)
    along = along + pltpu.roll(along, 64, 1)
    square = square + pltpu.roll(square, 64, 1)
    share(along, square, lsend, lbuf, 10)
    changes[...] = change
    keep(2)
    keep(4)

    left(infos.at[pl.ds(0, 8)], 0)
    left(halo, 1)
    if nb > 1:
        left(pots.at[pl.ds(0, nb - 1)], 2)
    left(qrecv, 3)
    left(ebuf, 4)
    left(geos.at[pl.ds(0, 8)], 11)
    left(nrecv, 12)
    left(bhalo, 5)
    left(near_s, 6)
    left(far_s, 7)
    left(halo2, 8)
    left(qrecv2, 9)
    left(lbuf.at[pl.ds(0, nx * ny - 1)], 10)

    arrive(lbuf.at[pl.ds(0, nx * ny - 1)], 10)
    for n in range(5):
        kept(n).wait()


def finish(w_ref, dirs_ref, resid_ref, change_ref, level_ref, sums_ref, bands_ref, new_ref, energy_ref):
    sums = jnp.sum(sums_ref[...], axis=0)
    first = lax.broadcasted_iota(jnp.int32, (1, 128), 1) < 64
    along = jnp.sum(jnp.where(first, sums, 0.0), axis=1, keepdims=True)
    square = jnp.sum(jnp.where(first, 0.0, sums), axis=1, keepdims=True)
    step = -along / square
    bands_ref[...] = w_ref[...] + step * dirs_ref[...]
    new_ref[...] = resid_ref[...] + step * change_ref[...]
    energy_ref[0] = level_ref[0, 0]


def solution(mesh):
    shape = tuple(mesh.shape[name] for name in ("band", "dx", "dy"))
    nb, nx, ny = shape
    table, packed_constants = packed()

    def on_device(wave_bands, potential, atom_offsets, proj_counts, dh_matrix, ds_matrix):
        vmem = pl.BlockSpec(memory_space=pltpu.VMEM)
        smem = pl.BlockSpec(memory_space=pltpu.SMEM)
        v = lambda *dims: pltpu.VMEM(dims, F32)
        hbm = pl.BlockSpec(memory_space=pltpu.HBM)
        grid = jax.ShapeDtypeStruct((128, 128), F32)
        parts = pl.pallas_call(
            functools.partial(kernel, shape, table),
            out_shape=(
                grid, grid, grid, jax.ShapeDtypeStruct((1, 128), F32), jax.ShapeDtypeStruct((nx * ny, 1, 128), F32),
            ),
            in_specs=[hbm] * 7,
            out_specs=(hbm,) * 5,
            scratch_shapes=[
                v(128, 128),
                v(128, 32),
                pltpu.SMEM((1, 3, 1, ATOMS), jnp.int32),
                pltpu.SMEM((1, 1, ATOMS), jnp.int32),
                v(2, 9, ATOMS, 9),
                pltpu.VMEM(packed_constants.shape, BF16),
                v(96, 128),
                v(144, 128),
                v(144, 128),
                v(128, 128),
                v(128, 128),
                v(128, 128),
                v(1, 128),
                v(16, 1, 128),
                v(8, 256),
                v(16, 8, 256),
                v(2, 128, 128),
                v(nb, 32, 128),
                v(5, 128),
                v(14, 5, 128),
                v(5, 128),
                v(14, 5, 128),
                v(2, 128, 128),
                v(2, 16, 128),
                v(2, 48, 128),
                v(ROWS_NEAR, 128),
                v(ROWS_NEAR, 128),
                v(ROWS_FAR, 128),
                v(ROWS_FAR, 128),
                v(2, 2, 128),
                v(23, 2, 128),
                v(2, 128),
                v(2, 2, 128),
                v(1, 128),
                v(1, 128),
                pltpu.VMEM((2, 128, 512), BF16),
                pltpu.VMEM((2, 512, 128), BF16),
                v(5, 128, 128),
                pltpu.SemaphoreType.DMA((7,)),
                pltpu.SemaphoreType.DMA((13,)),
                pltpu.SemaphoreType.DMA((13,)),
                pltpu.SemaphoreType.DMA((5,)),
            ],
            compiler_params=pltpu.CompilerParams(
                collective_id=0, has_side_effects=True, vmem_limit_bytes=60 << 20
            ),
        )(
            wave_bands.reshape(128, 128),
            potential.reshape(128, 32),
            jnp.transpose(atom_offsets, (0, 3, 1, 2)),
            proj_counts,
            jnp.transpose(dh_matrix, (0, 1, 3, 2, 4)).reshape(9, ATOMS, 9),
            jnp.transpose(ds_matrix, (0, 1, 3, 2, 4)).reshape(9, ATOMS, 9),
            jnp.asarray(packed_constants),
        )
        bands, resid, energy = pl.pallas_call(
            finish,
            out_shape=(grid, grid, jax.ShapeDtypeStruct((1,), F32)),
            in_specs=[vmem] * 4 + [smem, vmem],
            out_specs=(vmem, vmem, smem),
            compiler_params=pltpu.CompilerParams(vmem_limit_bytes=60 << 20),
        )(wave_bands.reshape(128, 128), *parts)
        return bands.reshape(1, CX, CY, NZ), resid.reshape(1, CX, CY, NZ), energy

    return jax.shard_map(
        on_device,
        mesh=mesh,
        in_specs=(
            P("band", "dx", "dy", None),
            P("dx", "dy", "band"),
            P("dx", "dy", None, None),
            P("dx", "dy", None),
            P("dx", "dy", None, None, None),
            P("dx", "dy", None, None, None),
        ),
        out_specs=(P("band", "dx", "dy", None), P("band", "dx", "dy", None), P("band")),
        check_vma=False,
    )
```
